128 devices in a mesh: cuts: 32 (over z, y, core), event: 4 (over x).
Axes of the slice: x: 4, y: 4, z: 4, core: 2. Of those that a mesh axis runs over, the one named last changes fastest.
Arguments:
- kernels: float32 [8, 7, 2097152], P('event', None, 'cuts')
- shots: int32 [8], replicated, may hold values from 1 to 8
- coords: float32 [3, 2097152], P(None, 'cuts'), may hold values from 0 to 3
- send_list: int32 [32, 4, 6, 32], P('cuts', 'event'), may hold values from 0 to 511, as said below
- block_list: int32 [32, 512, 8], P('cuts', 'event'), may hold values from 0 to 703, as said below
- block_count: int32 [32, 512], P('cuts', 'event'), may hold values from 1 to 8
Outputs:
- smoothed: float32 [7, 2097152], P(None, ('cuts', 'event'))
The draws below stay inside these ranges and needn't reach their ends.
Inputs may be any that keep to these rules, and one draw needn't show every extreme that they name: `send_list`: group g of slice s and range r lists 32 blocks of slice s needed by range r of slice (s + offset[g]) mod 32; its first live entries, 16 or more, are distinct, the rest are 0 and never named by block_list. `block_list`: entry 0 of each list is the target block itself; entries at k >= block_count are 0 and unused; remote entries name only live entries of their group.
All inputs are finite; a program needn't handle non-finite values.
Results may differ from the reference program's by a relative error of at most 0.0003.
Values sent between devices are 32-bit elements; how exact they have to be, the bound alone decides.
No kernel may reach another device: no remote copies, remote signals or barrier semaphores. Data moves between devices by JAX's collectives and lax.ppermute only.
A program may use at most 64 MiB of HBM per device.

```python
import math
import jax
import jax.numpy as jnp
from jax import lax

PARAMS = 7
BLOCK = 128
P_DEV = 65536
E_DEV = 2
KMAX = 8
CAP = 32
NPEER = 6
SLICES = 32
NPTS = 2097152
EVENTS = 8
TGT_DEV = 128


OFFSETS = (1, -1, 2, -2, 3, -3)


def neighbour_plan(key):
    blocks = P_DEV // BLOCK
    ranges = EVENTS // E_DEV
    key_order, key_live, key_first, key_second = jax.random.split(key, 4)
    scores = jax.random.randint(key_order, (SLICES, ranges, NPEER, blocks), 0, 2 ** 20)
    scores = scores * blocks + jnp.arange(blocks, dtype=jnp.int32)
    scores = scores.at[0, 0, 0, blocks - 1].set(-1)
    wanted = jnp.argsort(scores, axis=3)[..., :CAP].astype(jnp.int32)
    live = jax.random.randint(key_live, (SLICES, ranges, NPEER), (CAP + 1) // 2, CAP + 1)
    live = live.at[0, 0, 0].set((CAP + 1) // 2)
    live = live.at[0, 0, NPEER - 1].set(CAP)
    first = jax.random.randint(key_first, (SLICES, blocks), 0, KMAX)
    second = jax.random.randint(key_second, (SLICES, blocks), 0, KMAX)
    counts = KMAX - jnp.minimum(first, second) // 2
    counts = counts.at[0, 0].set(KMAX)
    counts = counts.at[0, 1].set(1)
    return (wanted, live.astype(jnp.int32), counts.astype(jnp.int32))


def draw_send_list(key, part):
    wanted, live, counts = neighbour_plan(key)
    key = jax.random.fold_in(key, 2)
    ranges = EVENTS // E_DEV
    offsets = jnp.array(OFFSETS, dtype=jnp.int32)
    receivers = (jnp.arange(SLICES, dtype=jnp.int32)[:, None] + offsets[None, :]) % SLICES
    range_ids = jnp.arange(ranges, dtype=jnp.int32)[None, :, None]
    group_ids = jnp.arange(NPEER, dtype=jnp.int32)[None, None, :]
    picked = wanted[receivers[:, None, :], range_ids, group_ids]
    live_picked = live[receivers[:, None, :], range_ids, group_ids]
    keep = jnp.arange(CAP, dtype=jnp.int32)[None, None, None, :] < live_picked[..., None]
    return jnp.where(keep, picked, 0).astype(jnp.int32)


def draw_block_count(key, part):
    wanted, live, counts = neighbour_plan(key)
    key = jax.random.fold_in(key, 3)
    return counts


def draw_block_list(key, part):
    wanted, live, counts = neighbour_plan(key)
    key = jax.random.fold_in(key, 4)
    blocks = P_DEV // BLOCK
    key_side, key_local, key_group, key_entry = jax.random.split(key, 4)
    shape = (SLICES, blocks, KMAX)
    use_local = jax.random.randint(key_side, shape, 0, 2) == 0
    local_pick = jax.random.randint(key_local, shape, 0, blocks)
    group = jax.random.randint(key_group, shape, 0, NPEER)
    ranges = jnp.arange(blocks, dtype=jnp.int32) // TGT_DEV
    group_live = live[jnp.arange(SLICES, dtype=jnp.int32)[:, None, None], ranges[None, :, None], group]
    entry = jax.random.randint(key_entry, shape, 0, 2 ** 20) % group_live
    remote = blocks + group * CAP + entry
    lists = jnp.where(use_local, local_pick, remote)
    lists = lists.at[:, :, 0].set(jnp.arange(blocks, dtype=jnp.int32)[None, :])
    lists = lists.at[0, 0, 1].set(blocks + (NPEER - 1) * CAP + CAP - 1)
    keep = jnp.arange(KMAX, dtype=jnp.int32)[None, None, :] < counts[:, :, None]
    return jnp.where(keep, lists, 0).astype(jnp.int32)


def draw_kernels(key, part):
    key = jax.random.fold_in(key, 7)
    key_rows, key_cols, key_noise, key_common = jax.random.split(key, 4)
    rows = jnp.exp(jax.random.uniform(key_rows, (EVENTS, PARAMS, 1), jnp.float32, 0.0, math.log(10.0)))
    spot = jnp.arange(NPTS, dtype=jnp.float32) / NPTS
    cols = jnp.exp(math.log(3.0) * spot + jax.random.uniform(key_cols, (NPTS,), jnp.float32, 0.0, math.log(10.0))) / 3.0
    noise = jax.random.normal(key_noise, (EVENTS, PARAMS, NPTS), jnp.float32)
    return (noise * rows * cols).astype(jnp.float32)


def set_ends(drawn, stream_key, smallest, top_value):
    longest = drawn.shape.index(max(drawn.shape))
    spots = []
    for shift in (0, 1):
        where = [jax.random.randint(jax.random.fold_in(stream_key, axis), (), 0, length) for axis, length in enumerate(drawn.shape)]
        where[longest] = (where[longest] + shift) % drawn.shape[longest]
        spots.append(tuple(where))
    return drawn.at[spots[0]].set(smallest).at[spots[1]].set(top_value)


def block_scale(rng, extent, shards, least, largest):
    loudness = 1.0
    for axis_at, parts in shards:
        steps = jax.random.uniform(jax.random.fold_in(jax.random.fold_in(rng, 6), axis_at), (parts,), jnp.float32, least / len(shards), largest / len(shards))
        loudness = loudness * jnp.repeat(jnp.exp(steps), extent[axis_at] // parts).reshape((-1,) + (1,) * (len(extent) - 1 - axis_at))
    return loudness


def setup_inputs(seed: int = 0) -> dict:
    keys = jax.random.split(jax.random.key(seed), 7)
    return {
        "kernels": draw_kernels(jax.random.fold_in(keys[6], 71), 0),
        "shots": set_ends(jax.random.randint(keys[1], (EVENTS,), 1, 9), jax.random.fold_in(keys[1], 1), 1, 8).astype(jnp.int32),
        "coords": jnp.clip(3.0 * jax.random.uniform(keys[2], (3, NPTS), jnp.float32) ** block_scale(keys[2], (3, NPTS), ((1, 32),), -0.2, 0.2), 0.0, 3.0),
        "send_list": draw_send_list(jax.random.fold_in(keys[6], 71), 0),
        "block_list": draw_block_list(jax.random.fold_in(keys[6], 71), 0),
        "block_count": draw_block_count(jax.random.fold_in(keys[6], 71), 0),
    }


OFFSETS = (1, -1, 2, -2, 3, -3)

def reference(kernels, shots, coords, send_list, block_list, block_count):
    power = lax.optimization_barrier(jnp.sum(kernels * kernels, axis=2))
    rms = jnp.sqrt(power / NPTS + 1e-06)
    weights = shots.astype(jnp.float32)
    field = lax.optimization_barrier(jnp.sum(weights[:, None, None] * (kernels / rms[:, :, None]), axis=0)) / jnp.sum(weights)
    blocks = P_DEV // BLOCK
    field_blocks = field.reshape(PARAMS, SLICES, blocks, BLOCK)
    coord_blocks = coords.reshape(3, SLICES, blocks, BLOCK)
    offsets = jnp.array(OFFSETS, dtype=jnp.int32)
    ranges = (jnp.arange(blocks, dtype=jnp.int32) // TGT_DEV).astype(jnp.int32)

    def one_slice(slice_id):
        lists = block_list[slice_id]
        counts = block_count[slice_id]
        local = lists < blocks
        remote = jnp.maximum(lists - blocks, 0)
        group = remote // CAP
        entry = remote % CAP
        sender = ((slice_id - offsets[group]) % SLICES).astype(jnp.int32)
        remote_block = send_list[sender, ranges[:, None], group, entry]
        src_slice = jnp.where(local, slice_id, sender)
        src_block = jnp.where(local, lists, remote_block)
        target = coord_blocks[:, slice_id]
        numer = jnp.zeros((PARAMS, blocks, BLOCK), jnp.float32)
        denom = jnp.zeros((blocks, BLOCK), jnp.float32)
        for slot in range(KMAX):
            src_coord = coord_blocks[:, src_slice[:, slot], src_block[:, slot]]
            src_field = field_blocks[:, src_slice[:, slot], src_block[:, slot]]
            diff0 = target[0][:, :, None] - src_coord[0][:, None, :]
            diff1 = target[1][:, :, None] - src_coord[1][:, None, :]
            diff2 = target[2][:, :, None] - src_coord[2][:, None, :]
            dist = diff0 * diff0 + diff1 * diff1 + diff2 * diff2
            live = (slot < counts).astype(jnp.float32)
            weight = jnp.exp(-0.5 * dist) * live[:, None, None]
            numer = numer + jnp.einsum('bij,pbj->pbi', weight, src_field, precision=lax.Precision.HIGHEST)
            denom = denom + lax.optimization_barrier(jnp.sum(weight, axis=2))
        return (numer / denom[None]).reshape(PARAMS, P_DEV)
    result = lax.map(one_slice, jnp.arange(SLICES, dtype=jnp.int32))
    return jnp.transpose(result, (1, 0, 2)).reshape(PARAMS, NPTS)
```

```python
import functools

import jax
import jax.numpy as jnp
from jax import lax
from jax.experimental import pallas as pl
from jax.experimental.pallas import tpu as pltpu
from jax.sharding import PartitionSpec as P

BLOCK = 128
OFFSETS = (1, -1, 2, -2, 3, -3)
BF = jnp.bfloat16
F32 = jnp.float32
LOG2E = 1.4426950408889634
NT = (((1,), (1,)), ((), ()))
TN = (((0,), (0,)), ((), ()))
VMEM = pl.BlockSpec(memory_space=pltpu.VMEM)
SMEM = pl.BlockSpec(memory_space=pltpu.SMEM)
HBM = pl.BlockSpec(memory_space=pl.ANY)


def params(mib):
    return pltpu.CompilerParams(vmem_limit_bytes=mib << 20)


def shifted(value, axis, steps):
    count = lax.axis_size(axis)
    pairs = [(source, (source + steps) % count) for source in range(count)]
    return lax.ppermute(value, axis, pairs)


def rows(shape):
    return lax.broadcasted_iota(jnp.int32, shape, 0)


def block(index):
    return pl.ds(pl.multiple_of(index * BLOCK, BLOCK), BLOCK)


def power_kernel(kernels, out, acc):
    step = pl.program_id(0)

    @pl.when(step == 0)
    def _():
        acc[...] = jnp.zeros_like(acc)

    for event in range(2):
        def add(i, total):
            x = kernels[event, :, block(i)]
            return total + x * x
        acc[event] += lax.fori_loop(
            0, kernels.shape[2] // BLOCK, add, jnp.zeros((7, BLOCK), F32), unroll=16
        )

    @pl.when(step == pl.num_programs(0) - 1)
    def _():
        first = jnp.sum(acc[0], axis=1, keepdims=True)
        second = jnp.sum(acc[1], axis=1, keepdims=True)
        lane = lax.broadcasted_iota(jnp.int32, (7, BLOCK), 1)
        tile = jnp.where(lane < 64, first, second)
        tile = jnp.concatenate([tile, jnp.zeros((1, BLOCK), F32)], axis=0)
        for peer in range(out.shape[0]):
            out[peer] = tile


def local_power(kernels, peers):
    width = kernels.shape[2] // 4
    return pl.pallas_call(
        power_kernel,
        grid=(4,),
        out_shape=jax.ShapeDtypeStruct((peers, 8, BLOCK), F32),
        in_specs=[pl.BlockSpec((2, 7, width), lambda i: (0, 0, i))],
        out_specs=pl.BlockSpec((peers, 8, BLOCK), lambda i: (0, 0, 0)),
        scratch_shapes=[pltpu.VMEM((2, 7, BLOCK), F32)],
        compiler_params=params(32),
    )(kernels)


def scale_kernel(npts, rank, shots, power, kernels, *outs):
    total = jnp.sum(power[...], axis=0)
    weight = jnp.int32(0)
    for event in range(shots.shape[0]):
        weight += shots[event]
    weight = jnp.full((8, 1), weight, jnp.int32).astype(F32)
    me = rank[0]
    scales = []
    for event in range(2):
        rms = jnp.sqrt(total[:, 64 * event:64 * event + 1] / npts + 1e-06)
        shot = jnp.full((8, 1), shots[2 * me + event], jnp.int32).astype(F32)
        scales.append(jnp.broadcast_to((shot / (rms * weight))[0:7], (7, BLOCK)))
    quarter = outs[0].shape[0]
    for turn, out in enumerate(outs):
        base = lax.rem(me + turn, len(outs)) * quarter

        def one(i, _):
            at = block(base + i)
            x = kernels[0, :, at] * scales[0] + kernels[1, :, at] * scales[1]
            out[i] = jnp.concatenate([x, jnp.zeros((1, BLOCK), F32)], axis=0)
            return 0
        lax.fori_loop(0, quarter, one, 0, unroll=8)


def weighted(rank, shots, power, kernels, npts, ranges):
    quarter = kernels.shape[2] // BLOCK // ranges
    return pl.pallas_call(
        functools.partial(scale_kernel, npts),
        out_shape=[jax.ShapeDtypeStruct((quarter, 8, BLOCK), F32)] * ranges,
        in_specs=[SMEM, SMEM, VMEM, VMEM],
        out_specs=[VMEM] * ranges,
        compiler_params=params(40),
    )(rank, shots, power, kernels)


def source_rows(x):
    row = rows(x.shape)
    high = x.astype(BF).astype(F32)
    rest = x - high
    low = rest.astype(BF).astype(F32)
    first = jnp.where(row == 7, low, high)
    second = jnp.where(row == 3, rest - low, jnp.where(row == 7, 0.0, low))
    return jnp.concatenate([first, second], axis=0).astype(BF)


def target_rows(x):
    row = rows(x.shape)
    high = x.astype(BF).astype(F32)
    low = x - high
    first = jnp.where(row % 4 == 3, 1.0, jnp.where(row < 4, high, low))
    second = jnp.where(row == 7, 0.0, first)
    return jnp.concatenate([first, second], axis=0).astype(BF)


def field_rows(x):
    row = rows(x.shape)
    high = x.astype(BF).astype(F32)
    low = jnp.where(row == 7, 0.0, x - high)
    high = jnp.where(row == 7, 1.0, high)
    return jnp.concatenate([high, low], axis=0).astype(BF)


def coord_kernel(rank, send, coords, source, target, *outs):
    targets = target.shape[0]
    start = rank[0] * targets

    def point(index):
        x = (coords[:, block(index)] - 1.5) * (LOG2E ** 0.5)
        half = -0.5 * jnp.sum(x * x, axis=0, keepdims=True)
        return jnp.concatenate([x, half], axis=0)

    def sources(i, _):
        x = point(i)
        source[i] = source_rows(jnp.concatenate([x, x], axis=0))
        return 0
    lax.fori_loop(0, source.shape[0], sources, 0, unroll=4)

    def aims(i, _):
        x = point(start + i)
        target[i] = target_rows(jnp.concatenate([x, x], axis=0))
        return 0
    lax.fori_loop(0, targets, aims, 0, unroll=4)
    for group, out in enumerate(outs):
        def pick(i, _):
            base = (group * out.shape[0] + i) * 2
            out[i] = jnp.concatenate([point(send[base]), point(send[base + 1])], axis=0)
            return 0
        lax.fori_loop(0, out.shape[0], pick, 0, unroll=4)


def coord_tables(rank, send, coords, targets, npeer, cap):
    blocks = coords.shape[1] // BLOCK
    return pl.pallas_call(
        coord_kernel,
        out_shape=[
            jax.ShapeDtypeStruct((blocks, 16, BLOCK), BF),
            jax.ShapeDtypeStruct((targets, 16, BLOCK), BF),
        ] + [jax.ShapeDtypeStruct((cap // 2, 8, BLOCK), F32)] * npeer,
        in_specs=[SMEM, SMEM, VMEM],
        out_specs=[VMEM] * (2 + npeer),
        compiler_params=params(40),
    )(rank, send, coords)


def gather_kernel(rank, send, own, left, right, far_left, far_right, table, *rest):
    outs, full = rest[:-1], rest[-1]
    quarter, half = own.shape[0], far_left.shape[0]
    me = rank[0]
    places = (
        (own, lax.rem(me, 4) * quarter),
        (left, lax.rem(me + 3, 4) * quarter),
        (right, lax.rem(me + 1, 4) * quarter),
        (far_left, lax.rem(me + 2, 4) * quarter),
        (far_right, lax.rem(me + 2, 4) * quarter + half),
    )
    for part, base in places:
        def store(i, _):
            x = part[i]
            full[base + i] = x
            table[base + i] = field_rows(x)
            return 0
        lax.fori_loop(0, part.shape[0], store, 0, unroll=8)
    for group, out in enumerate(outs):
        def pick(i, _):
            out[i] = full[send[group * out.shape[0] + i]]
            return 0
        lax.fori_loop(0, out.shape[0], pick, 0, unroll=8)


def gathered(rank, send, parts, npeer, cap):
    blocks = 4 * parts[0].shape[0]
    return pl.pallas_call(
        gather_kernel,
        out_shape=[jax.ShapeDtypeStruct((blocks, 16, BLOCK), BF)]
        + [jax.ShapeDtypeStruct((cap, 8, BLOCK), F32)] * npeer,
        in_specs=[SMEM, SMEM] + [VMEM] * 5,
        out_specs=[VMEM] * (1 + npeer),
        scratch_shapes=[pltpu.VMEM((blocks, 8, BLOCK), F32)],
        compiler_params=params(40),
    )(rank, send, *parts)


def smooth_kernel(npeer, lists, target, local_source, local_table, *rest):
    far_coord, far_field = rest[:npeer], rest[npeer:2 * npeer]
    out, source, table, sems = rest[2 * npeer:]
    blocks = local_source.shape[0]
    copies = [
        pltpu.make_async_copy(local_source, source.at[pl.ds(0, blocks)], sems.at[0]),
        pltpu.make_async_copy(local_table, table.at[pl.ds(0, blocks)], sems.at[1]),
    ]
    for copy in copies:
        copy.start()
    cap = far_field[0].shape[0]
    for group in range(npeer):
        base = blocks + group * cap

        def coords(i, _):
            x = far_coord[group][i]
            turned = pltpu.roll(x, 4, 0)
            row = rows(x.shape)
            source[base + 2 * i] = source_rows(jnp.where(row < 4, x, turned))
            source[base + 2 * i + 1] = source_rows(jnp.where(row < 4, turned, x))
            return 0
        lax.fori_loop(0, cap // 2, coords, 0, unroll=4)

        def fields(i, _):
            table[base + i] = field_rows(far_field[group][i])
            return 0
        lax.fori_loop(0, cap, fields, 0, unroll=8)
    none = blocks + npeer * cap
    source[none] = jnp.zeros((16, BLOCK), BF)
    table[none] = jnp.zeros((16, BLOCK), BF)
    for copy in copies:
        copy.wait()
    kmax = 8

    def one(b):
        slots = [lists[b * kmax + k] for k in range(kmax)]
        coords = jnp.concatenate([source[s] for s in slots], axis=1)
        power = lax.dot_general(target[b], coords, TN, preferred_element_type=F32)
        weight = jnp.exp2(power)
        high = weight.astype(BF)
        low = (weight - high.astype(F32)).astype(BF)
        field = jnp.concatenate([table[s] for s in slots], axis=1)
        sums = lax.dot_general(high, field, NT, preferred_element_type=F32)
        sums += lax.dot_general(low, field, NT, preferred_element_type=F32)
        sums = sums.T
        out[:, block(b)] = (sums[0:7] + sums[8:15]) / sums[7:8]

    def body(i, _):
        one(2 * i)
        one(2 * i + 1)
        return 0
    lax.fori_loop(0, target.shape[0] // 2, body, 0)


def smooth(lists, target, source, table, far_coord, far_field):
    targets, blocks = target.shape[0], source.shape[0]
    npeer, cap = len(far_field), far_field[0].shape[0]
    size = blocks + npeer * cap + 1
    return pl.pallas_call(
        functools.partial(smooth_kernel, npeer),
        out_shape=jax.ShapeDtypeStruct((7, targets * BLOCK), F32),
        in_specs=[SMEM, VMEM, HBM, HBM] + [VMEM] * (2 * npeer),
        out_specs=VMEM,
        scratch_shapes=[
            pltpu.VMEM((size, 16, BLOCK), BF),
            pltpu.VMEM((size, 16, BLOCK), BF),
            pltpu.SemaphoreType.DMA((2,)),
        ],
        compiler_params=params(48),
    )(lists, target, source, table, *far_coord, *far_field)


def body(kernels, shots, coords, send_list, block_list, block_count):
    slices = lax.axis_size("cuts")
    ranges = lax.axis_size("event")
    points = kernels.shape[2]
    npeer, cap = send_list.shape[2:]
    targets, kmax = block_list.shape[1:]
    rank = jnp.reshape(lax.axis_index("event"), (1,)).astype(jnp.int32)
    send = send_list.reshape(npeer * cap)
    none = points // BLOCK + npeer * cap
    slot = jnp.arange(kmax, dtype=jnp.int32)
    lists = jnp.where(slot < block_count[0][:, None], block_list[0], none)
    lists = lists.reshape(targets * kmax)

    power = local_power(kernels, slices)
    power = lax.all_to_all(power, "cuts", 0, 0)
    source, target, *near_coord = coord_tables(rank, send, coords, targets, npeer, cap)
    far_coord = [shifted(x, "cuts", OFFSETS[g]) for g, x in enumerate(near_coord)]

    mine, ahead, across, behind = weighted(
        rank, shots, power, kernels, float(points * slices), ranges
    )
    half = mine.shape[0] // 2
    from_left = shifted(across[:half], "event", 1)
    from_right = shifted(across[half:], "event", -1)
    ahead = jnp.concatenate([ahead[:half] + from_left, ahead[half:]], axis=0)
    behind = jnp.concatenate([behind[:half], behind[half:] + from_right], axis=0)
    own = mine + shifted(ahead, "event", 1) + shifted(behind, "event", -1)

    left = shifted(own, "event", 1)
    right = shifted(own, "event", -1)
    far_left = shifted(left[:half], "event", 1)
    far_right = shifted(right[half:], "event", -1)

    table, *near_field = gathered(
        rank, send, (own, left, right, far_left, far_right), npeer, cap
    )
    far_field = [shifted(x, "cuts", OFFSETS[g]) for g, x in enumerate(near_field)]
    return smooth(lists, target, source, table, far_coord, far_field)


def solution(mesh):
    placed = (
        P("event", None, "cuts"),
        P(),
        P(None, "cuts"),
        P("cuts", "event", None, None),
        P("cuts", "event", None),
        P("cuts", "event"),
    )
    return jax.shard_map(
        body, mesh=mesh, in_specs=placed, out_specs=P(None, ("cuts", "event")), check_vma=False
    )
```

```python
import functools

import jax
import jax.numpy as jnp
from jax import lax
from jax.experimental import pallas as pl
from jax.experimental.pallas import tpu as pltpu
from jax.sharding import PartitionSpec as P

BLOCK = 128
OFFSETS = (1, -1, 2, -2, 3, -3)
BF = jnp.bfloat16
F32 = jnp.float32
LOG2E = 1.4426950408889634
NT = (((1,), (1,)), ((), ()))
TN = (((0,), (0,)), ((), ()))
VMEM = pl.BlockSpec(memory_space=pltpu.VMEM)
SMEM = pl.BlockSpec(memory_space=pltpu.SMEM)
HBM = pl.BlockSpec(memory_space=pl.ANY)


def params(mib):
    return pltpu.CompilerParams(vmem_limit_bytes=mib << 20)


def cost(flops, moved):
    return pl.CostEstimate(flops=flops, bytes_accessed=moved, transcendentals=0)


def shifted(value, axis, steps):
    count = lax.axis_size(axis)
    pairs = [(source, (source + steps) % count) for source in range(count)]
    return lax.ppermute(value, axis, pairs)


def rows(shape):
    return lax.broadcasted_iota(jnp.int32, shape, 0)


def block(index):
    return pl.ds(pl.multiple_of(index * BLOCK, BLOCK), BLOCK)


def power_kernel(kernels, out):
    params_here, count = kernels.shape[0], kernels.shape[1] // 8
    lane = lax.broadcasted_iota(jnp.int32, (8, BLOCK), 1)
    tile = jnp.zeros((8, BLOCK), F32)
    for p in range(params_here):
        def add(i, total):
            x = kernels[p, pl.ds(pl.multiple_of(i * 8, 8), 8), :]
            return total + x * x
        total = lax.fori_loop(0, count, add, jnp.zeros((8, BLOCK), F32), unroll=16)
        tile = jnp.where(lane == p, jnp.sum(total, axis=1, keepdims=True), tile)
    for peer in range(out.shape[0]):
        out[peer] = tile


def local_power(kernels, peers):
    return pl.pallas_call(
        power_kernel,
        out_shape=jax.ShapeDtypeStruct((peers, 8, BLOCK), F32),
        in_specs=[VMEM],
        out_specs=VMEM,
        compiler_params=params(16),
        cost_estimate=cost(2 * kernels.size, 4 * kernels.size),
    )(kernels)


def scale_kernel(npts, rank, shots, power, kernels, *outs):
    total = jnp.sum(power[...], axis=0)
    total = total + pltpu.roll(total, 2, 0)
    total = total + pltpu.roll(total, 4, 0)
    weight = jnp.int32(0)
    for event in range(shots.shape[0]):
        weight += shots[event]
    weight = jnp.full((8, BLOCK), weight, jnp.int32).astype(F32)
    me = rank[0]
    row = rows((8, BLOCK))
    shot = jnp.where(
        row % 2 == 0,
        jnp.full((8, BLOCK), shots[2 * me], jnp.int32),
        jnp.full((8, BLOCK), shots[2 * me + 1], jnp.int32),
    ).astype(F32)
    scale = shot / (jnp.sqrt(total / npts + 1e-06) * weight)
    half = outs[0].shape[1]
    ranges = len(outs) // 2
    for p in range(kernels.shape[0]):
        factor = jnp.broadcast_to(scale[:, p:p + 1], (8, BLOCK))
        for turn, out in enumerate(outs):
            base = (lax.rem(me + turn // 2, ranges) * 2 + turn % 2) * half * 2

            def one(i, _):
                at = pl.multiple_of(base + i * 16, 16)
                x = kernels[p, pl.ds(at, 8), :] * factor
                y = kernels[p, pl.ds(at + 8, 8), :] * factor
                x = x + pltpu.roll(x, 7, 0)
                y = y + pltpu.roll(y, 1, 0)
                out[p, pl.ds(pl.multiple_of(i * 8, 8), 8), :] = jnp.where(row % 2 == 0, x, y)
                return 0
            lax.fori_loop(0, half // 8, one, 0, unroll=4)


def weighted(rank, shots, power, kernels, npts, ranges):
    half = kernels.shape[1] // 2 // ranges // 2
    return pl.pallas_call(
        functools.partial(scale_kernel, npts),
        out_shape=[jax.ShapeDtypeStruct((7, half, BLOCK), F32)] * (2 * ranges),
        in_specs=[SMEM, SMEM, VMEM, VMEM],
        out_specs=[VMEM] * (2 * ranges),
        compiler_params=params(16),
        cost_estimate=cost(3 * kernels.size, 6 * kernels.size),
    )(rank, shots, power, kernels)


def source_rows(x):
    row = rows(x.shape)
    high = x.astype(BF).astype(F32)
    rest = x - high
    low = rest.astype(BF).astype(F32)
    first = jnp.where(row == 7, low, high)
    second = jnp.where(row == 3, rest - low, jnp.where(row == 7, 0.0, low))
    return jnp.concatenate([first, second], axis=0).astype(BF)


def target_rows(x):
    row = rows(x.shape)
    high = x.astype(BF).astype(F32)
    low = x - high
    first = jnp.where(row % 4 == 3, 1.0, jnp.where(row < 4, high, low))
    second = jnp.where(row == 7, 0.0, first)
    return jnp.concatenate([first, second], axis=0).astype(BF)


def field_rows(x):
    high = x.astype(BF).astype(F32)
    return jnp.concatenate([high, x - high], axis=0).astype(BF)


def coord_kernel(rank, send, coords, source, target, out):
    targets = target.shape[0]
    start = rank[0] * targets
    npeer, cap = send.shape
    blocks = coords.shape[1] // BLOCK

    def point(index):
        x = (coords[:, block(index)] - 1.5) * (LOG2E ** 0.5)
        half = -0.5 * jnp.sum(x * x, axis=0, keepdims=True)
        return jnp.concatenate([x, half], axis=0)

    def sources(i, _):
        x = point(i)
        source[i] = source_rows(jnp.concatenate([x, x], axis=0))
        return 0
    lax.fori_loop(0, blocks, sources, 0, unroll=4)
    source[blocks] = jnp.zeros((16, BLOCK), BF)

    def aims(i, _):
        x = point(start + i)
        target[i] = target_rows(jnp.concatenate([x, x], axis=0))
        return 0
    lax.fori_loop(0, targets, aims, 0, unroll=4)
    for group in range(npeer):
        def pick(i, _):
            pair = [point(send[group, 2 * i]), point(send[group, 2 * i + 1])]
            out[group * (cap // 2) + i] = jnp.concatenate(pair, axis=0)
            return 0
        lax.fori_loop(0, cap // 2, pick, 0, unroll=4)


def coord_tables(rank, send, coords, targets):
    blocks = coords.shape[1] // BLOCK
    return pl.pallas_call(
        coord_kernel,
        out_shape=[
            jax.ShapeDtypeStruct((blocks + 1, 16, BLOCK), BF),
            jax.ShapeDtypeStruct((targets, 16, BLOCK), BF),
            jax.ShapeDtypeStruct((send.size // 2, 8, BLOCK), F32),
        ],
        in_specs=[SMEM, SMEM, VMEM],
        out_specs=[VMEM] * 3,
        compiler_params=params(16),
        cost_estimate=cost(coords.size * 30, coords.size * 12),
    )(rank, send, coords)


STEP = 8
SHIFT = 1 << 10


def list_kernel(blocks, remote, lists, counts, near, far, sizes):
    kmax, targets = lists.shape

    def one(b, at):
        a, c = at
        count = counts[0, b]
        for k in range(kmax):
            v = lists[k, b]
            live = (k < count).astype(jnp.int32)
            local = (v < blocks).astype(jnp.int32)
            near[a] = b * SHIFT + v
            far[c] = b * SHIFT + v - blocks
            a += live * local
            c += live * (1 - local)
        return a, c
    a, c = lax.fori_loop(0, targets, one, (jnp.int32(0), jnp.int32(0)))
    for i in range(STEP):
        near[a + i] = jnp.int32(blocks)
        far[c + i] = jnp.int32(remote)
    sizes[0] = a
    sizes[1] = c


def work_lists(lists, counts, blocks, remote):
    size = lists.size + STEP
    return pl.pallas_call(
        functools.partial(list_kernel, blocks, remote),
        out_shape=[
            jax.ShapeDtypeStruct((size,), jnp.int32),
            jax.ShapeDtypeStruct((size,), jnp.int32),
            jax.ShapeDtypeStruct((2,), jnp.int32),
        ],
        in_specs=[SMEM, SMEM],
        out_specs=[SMEM] * 3,
        cost_estimate=cost(lists.size * 2000, lists.size * 8),
    )(lists, counts)


def place(index):
    inner = index & 7
    return index - inner + 2 * (inner & 3) + (inner >> 2)


def gather_kernel(rank, send, coords, *rest):
    parts, outs, full = rest[:8], rest[8:-1], rest[-1]
    half = parts[0].shape[1]
    blocks = 8 * half
    me = rank[0]
    for turn, part in enumerate(parts):
        base = (lax.rem(me + turn // 2, 4) * 2 + turn % 2) * half
        for p in range(7):
            def store(i, _):
                at = pl.multiple_of(i * 8, 8)
                full[pl.ds(pl.multiple_of(p * blocks + base + at, 8), 8), :] = part[p, pl.ds(at, 8), :]
                return 0
            lax.fori_loop(0, half // 8, store, 0, unroll=True)

    def ones(i, _):
        full[pl.ds(pl.multiple_of(7 * blocks + i * 8, 8), 8), :] = jnp.ones((8, BLOCK), F32)
        return 0
    lax.fori_loop(0, blocks // 8, ones, 0, unroll=8)
    npeer, cap = send.shape
    for group, out in enumerate(outs):
        def pick(i, _):
            out[i] = full[pl.ds(place(send[group, i]), 8, stride=blocks), :]
            return 0
        lax.fori_loop(0, cap, pick, 0, unroll=8)

        def copy(i, _):
            out[cap + i] = coords[group * (cap // 2) + i]
            return 0
        lax.fori_loop(0, cap // 2, copy, 0, unroll=8)


def gathered(rank, send, coords, parts):
    blocks = 8 * parts[0].shape[1]
    npeer, cap = send.shape
    *sends, full = pl.pallas_call(
        gather_kernel,
        out_shape=[jax.ShapeDtypeStruct((cap + cap // 2, 8, BLOCK), F32)] * npeer
        + [jax.ShapeDtypeStruct((8 * blocks, BLOCK), F32)],
        in_specs=[SMEM, SMEM, VMEM] + [VMEM] * 8,
        out_specs=[VMEM] * (npeer + 1),
        compiler_params=params(16),
    )(rank, send, coords, *parts)
    return sends, full


def weigh(items, count, target, source, table, sums):
    def clear(i, _):
        sums[i] = jnp.zeros(sums.shape[1:], F32)
        return 0
    lax.fori_loop(0, sums.shape[0], clear, 0)
    empty = jnp.zeros((16, BLOCK), BF)

    def step(i, _):
        done = []
        for pair in range(STEP // 2):
            both = [items[i * STEP + 2 * pair], items[i * STEP + 2 * pair + 1]]
            aims = [v >> 10 for v in both]
            froms = [v & 1023 for v in both]
            left = jnp.concatenate([target[t] for t in aims], axis=0)
            right = jnp.concatenate([
                jnp.concatenate([source[froms[0]], empty], axis=1),
                jnp.concatenate([empty, source[froms[1]]], axis=1),
            ], axis=0)
            weight = jnp.exp2(lax.dot_general(left, right, TN, preferred_element_type=F32))
            high = weight.astype(BF)
            low = (weight - high.astype(F32)).astype(BF)
            for item in range(2):
                at = slice(item * BLOCK, (item + 1) * BLOCK)
                field = table[froms[item]]
                part = lax.dot_general(
                    jnp.concatenate([high[:, at], low[:, at]], axis=1),
                    jnp.concatenate([field, field], axis=1),
                    NT,
                    preferred_element_type=F32,
                )
                done.append((aims[item], part))
        for aim, part in done:
            sums[aim] += part
        return 0
    lax.fori_loop(0, (count + STEP - 1) // STEP, step, 0)


def near_kernel(items, sizes, target, source, full, ready, out, table, sums):
    blocks = source.shape[0] - 1

    def build(i, _):
        x = full[pl.ds(place(i), 8, stride=blocks), :]
        table[i] = field_rows(x)
        return 0
    lax.fori_loop(0, blocks, build, 0, unroll=8)
    table[blocks] = jnp.zeros((16, BLOCK), BF)
    weigh(items, sizes[0], target, source, table, sums)

    def turn(b, _):
        out[b] = sums[b].T
        return 0
    lax.fori_loop(0, target.shape[0], turn, 0, unroll=4)


def near_sums(items, sizes, target, source, full, ready):
    targets, size = target.shape[0], source.shape[0]
    return pl.pallas_call(
        near_kernel,
        out_shape=jax.ShapeDtypeStruct((targets, 16, BLOCK), F32),
        in_specs=[SMEM, SMEM, VMEM, VMEM, VMEM, HBM],
        out_specs=VMEM,
        scratch_shapes=[
            pltpu.VMEM((size, 16, BLOCK), BF),
            pltpu.VMEM((targets, BLOCK, 16), F32),
        ],
        compiler_params=params(24),
        cost_estimate=cost(2 * 10 ** 10, 10 ** 7),
    )(items, sizes, target, source, full, ready)


def far_kernel(items, sizes, target, start, *rest):
    parts = rest[:-4]
    out, source, table, sums = rest[-4:]
    cap = parts[0].shape[0] * 2 // 3
    for group, part in enumerate(parts):
        base = group * cap

        def coords(i, _):
            x = part[cap + i]
            turned = pltpu.roll(x, 4, 0)
            row = rows(x.shape)
            source[base + 2 * i] = source_rows(jnp.where(row < 4, x, turned))
            source[base + 2 * i + 1] = source_rows(jnp.where(row < 4, turned, x))
            return 0
        lax.fori_loop(0, cap // 2, coords, 0, unroll=4)

        def fields(i, _):
            table[base + i] = field_rows(part[i])
            return 0
        lax.fori_loop(0, cap, fields, 0, unroll=8)
    none = len(parts) * cap
    source[none] = jnp.zeros((16, BLOCK), BF)
    table[none] = jnp.zeros((16, BLOCK), BF)
    weigh(items, sizes[1], target, source, table, sums)

    def finish(b, _):
        total = sums[b].T + start[b]
        out[:, block(b)] = (total[0:7] + total[8:15]) / total[7:8]
        return 0
    lax.fori_loop(0, target.shape[0], finish, 0, unroll=4)


def far_sums(items, sizes, target, start, parts):
    targets = target.shape[0]
    size = len(parts) * parts[0].shape[0] * 2 // 3 + 1
    return pl.pallas_call(
        far_kernel,
        out_shape=jax.ShapeDtypeStruct((7, targets * BLOCK), F32),
        in_specs=[SMEM, SMEM, VMEM, VMEM] + [VMEM] * len(parts),
        out_specs=VMEM,
        scratch_shapes=[
            pltpu.VMEM((size, 16, BLOCK), BF),
            pltpu.VMEM((size, 16, BLOCK), BF),
            pltpu.VMEM((targets, BLOCK, 16), F32),
        ],
        compiler_params=params(24),
    )(items, sizes, target, start, *parts)


def body(kernels, shots, coords, send_list, block_list, block_count):
    slices = lax.axis_size("cuts")
    ranges = lax.axis_size("event")
    events, nparams, points = kernels.shape
    blocks = points // BLOCK
    npeer, cap = send_list.shape[2:]
    targets = block_list.shape[1]
    rank = jnp.reshape(lax.axis_index("event"), (1,)).astype(jnp.int32)
    send = send_list.reshape(npeer, cap)
    kernels = kernels.transpose(1, 0, 2).reshape(nparams, events, blocks, BLOCK)
    kernels = kernels.transpose(0, 2, 1, 3).reshape(nparams, blocks * events, BLOCK)

    power = local_power(kernels, slices)
    coords, lists, power = lax.optimization_barrier((coords, block_list, power))
    power = lax.all_to_all(power, "cuts", 0, 0)
    source, target, near_coord = coord_tables(rank, send, coords, targets)
    near_items, far_items, sizes = work_lists(
        lists[0].T, block_count, blocks, npeer * cap
    )
    power, source, target, near_coord, near_items, far_items, sizes = lax.optimization_barrier(
        (power, source, target, near_coord, near_items, far_items, sizes)
    )
    mine_a, mine_b, ahead_a, ahead_b, across_a, across_b, behind_a, behind_b = weighted(
        rank, shots, power, kernels, float(points * slices), ranges
    )
    from_left = shifted(across_a, "event", 1)
    from_right = shifted(across_b, "event", -1)
    left_b = shifted(ahead_b, "event", 1)
    right_a = shifted(behind_a, "event", -1)
    left_a = shifted(ahead_a + from_left, "event", 1)
    right_b = shifted(behind_b + from_right, "event", -1)
    own_a = mine_a + left_a + right_a
    own_b = mine_b + left_b + right_b

    left_a = shifted(own_a, "event", 1)
    right_b = shifted(own_b, "event", -1)
    left_b = shifted(own_b, "event", 1)
    right_a = shifted(own_a, "event", -1)
    far_a = shifted(left_a, "event", 1)
    far_b = shifted(right_b, "event", -1)

    sends, full = gathered(
        rank, send, near_coord,
        (own_a, own_b, right_a, right_b, far_a, far_b, left_a, left_b),
    )
    parts = [shifted(x, "cuts", OFFSETS[g]) for g, x in enumerate(sends)]
    start = near_sums(near_items, sizes, target, source, full, parts[0])
    return far_sums(far_items, sizes, target, start, parts)


def solution(mesh):
    placed = (
        P("event", None, "cuts"),
        P(),
        P(None, "cuts"),
        P("cuts", "event", None, None),
        P("cuts", "event", None),
        P("cuts", "event"),
    )
    return jax.shard_map(
        body, mesh=mesh, in_specs=placed, out_specs=P(None, ("cuts", "event")), check_vma=False
    )
```

```python
import functools

import jax
import jax.numpy as jnp
from jax import lax
from jax.experimental import pallas as pl
from jax.experimental.pallas import tpu as pltpu
from jax.sharding import PartitionSpec as P

BLOCK = 128
OFFSETS = (1, -1, 2, -2, 3, -3)
BF = jnp.bfloat16
F32 = jnp.float32
LOG2E = 1.4426950408889634
NT = (((1,), (1,)), ((), ()))
TN = (((0,), (0,)), ((), ()))
VMEM = pl.BlockSpec(memory_space=pltpu.VMEM)
SMEM = pl.BlockSpec(memory_space=pltpu.SMEM)
ANY = pl.BlockSpec(memory_space=pl.ANY)
HBM = pl.BlockSpec(memory_space=pltpu.HBM)


def params(mib):
    return pltpu.CompilerParams(vmem_limit_bytes=mib << 20)


def cost(flops, moved):
    return pl.CostEstimate(flops=flops, bytes_accessed=moved, transcendentals=0)


def shifted(value, axis, steps):
    count = lax.axis_size(axis)
    pairs = [(source, (source + steps) % count) for source in range(count)]
    return lax.ppermute(value, axis, pairs)


def rows(shape):
    return lax.broadcasted_iota(jnp.int32, shape, 0)


def block(index):
    return pl.ds(pl.multiple_of(index * BLOCK, BLOCK), BLOCK)


def power_kernel(kernels, out, held, sems):
    params_here, count = kernels.shape[0], kernels.shape[1] // 8
    copies = [
        pltpu.make_async_copy(kernels.at[p], held.at[p], sems.at[p])
        for p in range(params_here)
    ]
    for copy in copies:
        copy.start()
    lane = lax.broadcasted_iota(jnp.int32, (8, BLOCK), 1)
    tile = jnp.zeros((8, BLOCK), F32)
    for p in range(params_here):
        copies[p].wait()

        def add(i, totals):
            found = []
            for part in range(4):
                x = held[p, pl.ds(pl.multiple_of((i * 4 + part) * 8, 8), 8), :]
                found.append(totals[part] + x * x)
            return tuple(found)
        zero = jnp.zeros((8, BLOCK), F32)
        totals = lax.fori_loop(0, count // 4, add, (zero,) * 4, unroll=4)
        total = (totals[0] + totals[1]) + (totals[2] + totals[3])
        tile = jnp.where(lane == p, jnp.sum(total, axis=1, keepdims=True), tile)
    for peer in range(out.shape[0]):
        out[peer] = tile


def local_power(kernels, peers):
    return pl.pallas_call(
        power_kernel,
        out_shape=jax.ShapeDtypeStruct((peers, 8, BLOCK), F32),
        in_specs=[ANY],
        out_specs=VMEM,
        scratch_shapes=[
            pltpu.VMEM(kernels.shape, F32),
            pltpu.SemaphoreType.DMA((kernels.shape[0],)),
        ],
        compiler_params=params(16),
        cost_estimate=cost(2 * kernels.size, 4 * kernels.size),
    )(kernels)


def scale_kernel(npts, ranges, plan, rank, shots, power, kernels, *rest):
    outs, held, sems = rest[:-2], rest[-2], rest[-1]
    me = rank[0]
    span = held.shape[2]
    pieces = [(out, at, turn, side) for out, parts in zip(outs, plan) for at, (turn, side) in enumerate(parts)]
    copies = []
    for n, (_, _, turn, side) in enumerate(pieces):
        base = pl.multiple_of((lax.rem(me + turn, ranges) * 2 + side) * span, span)
        copies.append(pltpu.make_async_copy(
            kernels.at[:, pl.ds(base, span), :], held.at[n], sems.at[n]
        ))
        copies[-1].start()
    total = jnp.sum(power[...], axis=0)
    total = total + pltpu.roll(total, 2, 0)
    total = total + pltpu.roll(total, 4, 0)
    weight = jnp.int32(0)
    for event in range(shots.shape[0]):
        weight += shots[event]
    weight = jnp.full((8, BLOCK), weight, jnp.int32).astype(F32)
    row = rows((8, BLOCK))
    shot = jnp.where(
        row % 2 == 0,
        jnp.full((8, BLOCK), shots[2 * me], jnp.int32),
        jnp.full((8, BLOCK), shots[2 * me + 1], jnp.int32),
    ).astype(F32)
    scale = shot / (jnp.sqrt(total / npts + 1e-06) * weight)
    nparams = kernels.shape[0]
    factors = [jnp.broadcast_to(scale[:, p:p + 1], (8, BLOCK)) for p in range(nparams)]
    for n, (out, at, _, _) in enumerate(pieces):
        copies[n].wait()
        for p in range(nparams):
            def one(i, _):
                low = pl.multiple_of(i * 16, 16)
                x = held[n, p, pl.ds(low, 8), :] * factors[p]
                y = held[n, p, pl.ds(low + 8, 8), :] * factors[p]
                x = x + pltpu.roll(x, 7, 0)
                y = y + pltpu.roll(y, 1, 0)
                out[at * nparams + p, pl.ds(pl.multiple_of(i * 8, 8), 8), :] = jnp.where(row % 2 == 0, x, y)
                return 0
            lax.fori_loop(0, span // 16, one, 0, unroll=4)


def weighted(plan, rank, shots, power, kernels, npts, ranges):
    nparams = kernels.shape[0]
    span = kernels.shape[1] // (2 * ranges)
    count = sum(len(parts) for parts in plan)
    return pl.pallas_call(
        functools.partial(scale_kernel, npts, ranges, plan),
        out_shape=[
            jax.ShapeDtypeStruct((nparams * len(parts), span // 2, BLOCK), F32) for parts in plan
        ],
        in_specs=[SMEM, SMEM, VMEM, ANY],
        out_specs=[VMEM] * len(plan),
        scratch_shapes=[
            pltpu.VMEM((count, nparams, span, BLOCK), F32),
            pltpu.SemaphoreType.DMA((count,)),
        ],
        compiler_params=params(16),
        cost_estimate=cost(3 * kernels.size, 6 * kernels.size),
    )(rank, shots, power, kernels)


def source_rows(x):
    row = rows(x.shape)
    high = x.astype(BF).astype(F32)
    rest = x - high
    low = rest.astype(BF).astype(F32)
    first = jnp.where(row == 7, low, high)
    second = jnp.where(row == 3, rest - low, jnp.where(row == 7, 0.0, low))
    return jnp.concatenate([first, second], axis=0).astype(BF)


def target_rows(x):
    row = rows(x.shape)
    high = x.astype(BF).astype(F32)
    low = x - high
    first = jnp.where(row % 4 == 3, 1.0, jnp.where(row < 4, high, low))
    second = jnp.where(row == 7, 0.0, first)
    return jnp.concatenate([first, second], axis=0).astype(BF)


def field_rows(x):
    high = x.astype(BF).astype(F32)
    return jnp.concatenate([high, x - high], axis=0).astype(BF)


def coord_kernel(rank, send, coords, source_out, target_out, out, source, target, sems):
    targets = target.shape[0]
    start = rank[0] * targets
    npeer, cap = send.shape
    blocks = coords.shape[1] // BLOCK

    def point(index):
        x = (coords[:, block(index)] - 1.5) * (LOG2E ** 0.5)
        half = -0.5 * jnp.sum(x * x, axis=0, keepdims=True)
        return jnp.concatenate([x, half], axis=0)

    def sources(i, _):
        x = point(i)
        source[i] = source_rows(jnp.concatenate([x, x], axis=0))
        return 0
    lax.fori_loop(0, blocks, sources, 0, unroll=4)

    def aims(i, _):
        x = point(start + i)
        target[i] = target_rows(jnp.concatenate([x, x], axis=0))
        return 0
    lax.fori_loop(0, targets, aims, 0, unroll=4)
    copies = [
        pltpu.make_async_copy(source, source_out, sems.at[0]),
        pltpu.make_async_copy(target, target_out, sems.at[1]),
    ]
    for copy in copies:
        copy.start()
    for group in range(npeer):
        def pick(i, _):
            pair = [point(send[group, 2 * i]), point(send[group, 2 * i + 1])]
            out[group * (cap // 2) + i] = jnp.concatenate(pair, axis=0)
            return 0
        lax.fori_loop(0, cap // 2, pick, 0, unroll=4)
    for copy in copies:
        copy.wait()


def coord_tables(rank, send, coords, targets):
    blocks = coords.shape[1] // BLOCK
    return pl.pallas_call(
        coord_kernel,
        out_shape=[
            jax.ShapeDtypeStruct((blocks, 16, BLOCK), BF),
            jax.ShapeDtypeStruct((targets, 16, BLOCK), BF),
            jax.ShapeDtypeStruct((send.size // 2, 8, BLOCK), F32),
        ],
        in_specs=[SMEM, SMEM, VMEM],
        out_specs=[HBM, HBM, VMEM],
        scratch_shapes=[
            pltpu.VMEM((blocks, 16, BLOCK), BF),
            pltpu.VMEM((targets, 16, BLOCK), BF),
            pltpu.SemaphoreType.DMA((2,)),
        ],
        compiler_params=params(16),
        cost_estimate=cost(coords.size * 30, coords.size * 12),
    )(rank, send, coords)


def place(index):
    inner = index & 7
    return index - inner + 2 * (inner & 3) + (inner >> 2)


def gather_kernel(rank, send, coords, *rest):
    parts, outs, full = rest[:8], rest[8:-1], rest[-1]
    half = parts[0].shape[1]
    blocks = 8 * half
    me = rank[0]
    for turn, part in enumerate(parts):
        base = (lax.rem(me + turn // 2, 4) * 2 + turn % 2) * half
        for p in range(7):
            def store(i, _):
                at = pl.multiple_of(i * 8, 8)
                full[pl.ds(pl.multiple_of(p * blocks + base + at, 8), 8), :] = part[p, pl.ds(at, 8), :]
                return 0
            lax.fori_loop(0, half // 8, store, 0, unroll=True)

    def ones(i, _):
        full[pl.ds(pl.multiple_of(7 * blocks + i * 8, 8), 8), :] = jnp.ones((8, BLOCK), F32)
        return 0
    lax.fori_loop(0, blocks // 8, ones, 0, unroll=8)
    npeer, cap = send.shape
    for group, out in enumerate(outs):
        def pick(i, _):
            out[i] = full[pl.ds(place(send[group, i]), 8, stride=blocks), :]
            return 0
        lax.fori_loop(0, cap, pick, 0, unroll=8)

        def copy(i, _):
            out[cap + i] = coords[group * (cap // 2) + i]
            return 0
        lax.fori_loop(0, cap // 2, copy, 0, unroll=8)


def gathered(rank, send, coords, parts):
    blocks = 8 * parts[0].shape[1]
    npeer, cap = send.shape
    *sends, full = pl.pallas_call(
        gather_kernel,
        out_shape=[jax.ShapeDtypeStruct((cap + cap // 2, 8, BLOCK), F32)] * npeer
        + [jax.ShapeDtypeStruct((8 * blocks, BLOCK), F32)],
        in_specs=[SMEM, SMEM, VMEM] + [VMEM] * 8,
        out_specs=[VMEM] * (npeer + 1),
        compiler_params=params(16),
    )(rank, send, coords, *parts)
    return sends, full


def smooth_kernel(lists, target_in, source_in, full, *rest):
    parts = rest[:-5]
    out, target, source, table, sems = rest[-5:]
    blocks, targets = source_in.shape[0], target.shape[0]
    copies = [
        pltpu.make_async_copy(source_in, source.at[pl.ds(0, blocks)], sems.at[0]),
        pltpu.make_async_copy(target_in, target, sems.at[1]),
    ]
    for copy in copies:
        copy.start()

    def build(i, _):
        table[i] = field_rows(full[pl.ds(place(i), 8, stride=blocks), :])
        return 0
    lax.fori_loop(0, blocks, build, 0, unroll=8)
    cap = parts[0].shape[0] * 2 // 3
    for group, part in enumerate(parts):
        base = blocks + group * cap

        def coords(i, _):
            x = part[cap + i]
            turned = pltpu.roll(x, 4, 0)
            row = rows(x.shape)
            source[base + 2 * i] = source_rows(jnp.where(row < 4, x, turned))
            source[base + 2 * i + 1] = source_rows(jnp.where(row < 4, turned, x))
            return 0
        lax.fori_loop(0, cap // 2, coords, 0, unroll=4)

        def fields(i, _):
            table[base + i] = field_rows(part[i])
            return 0
        lax.fori_loop(0, cap, fields, 0, unroll=8)
    none = blocks + len(parts) * cap
    source[none] = jnp.zeros((16, BLOCK), BF)
    table[none] = jnp.zeros((16, BLOCK), BF)
    for copy in copies:
        copy.wait()
    kmax = lists.shape[0]

    def one(b):
        slots = [lists[k, b] for k in range(kmax)]
        coords = jnp.concatenate([source[s] for s in slots], axis=1)
        power = lax.dot_general(target[b], coords, TN, preferred_element_type=F32)
        weight = jnp.exp2(power)
        high = weight.astype(BF)
        low = (weight - high.astype(F32)).astype(BF)
        field = jnp.concatenate([table[s] for s in slots], axis=1)
        sums = lax.dot_general(high, field, NT, preferred_element_type=F32)
        sums += lax.dot_general(low, field, NT, preferred_element_type=F32)
        sums = sums.T
        out[:, block(b)] = (sums[0:7] + sums[8:15]) / sums[7:8]

    def step(i, _):
        for turn in range(4):
            one(4 * i + turn)
        return 0
    lax.fori_loop(0, targets // 4, step, 0)


def smooth(lists, target, source, full, parts):
    targets = target.shape[0]
    size = source.shape[0] + len(parts) * (parts[0].shape[0] * 2 // 3) + 1
    return pl.pallas_call(
        smooth_kernel,
        out_shape=jax.ShapeDtypeStruct((7, targets * BLOCK), F32),
        in_specs=[SMEM, HBM, HBM, VMEM] + [VMEM] * len(parts),
        out_specs=VMEM,
        scratch_shapes=[
            pltpu.VMEM((targets, 16, BLOCK), BF),
            pltpu.VMEM((size, 16, BLOCK), BF),
            pltpu.VMEM((size, 16, BLOCK), BF),
            pltpu.SemaphoreType.DMA((2,)),
        ],
        compiler_params=params(24),
    )(lists, target, source, full, *parts)


def body(kernels, shots, coords, send_list, block_list, block_count):
    slices = lax.axis_size("cuts")
    ranges = lax.axis_size("event")
    events, nparams, points = kernels.shape
    blocks = points // BLOCK
    npeer, cap = send_list.shape[2:]
    targets = block_list.shape[1]
    rank = jnp.reshape(lax.axis_index("event"), (1,)).astype(jnp.int32)
    send = send_list.reshape(npeer, cap)
    kernels = kernels.transpose(1, 0, 2).reshape(nparams, events, blocks, BLOCK)
    kernels = kernels.transpose(0, 2, 1, 3).reshape(nparams, blocks * events, BLOCK)

    power = local_power(kernels, slices)
    coords, power = lax.optimization_barrier((coords, power))
    power = lax.all_to_all(power, "cuts", 0, 0)
    source, target, near_coord = coord_tables(rank, send, coords, targets)
    slot = jnp.arange(block_list.shape[2], dtype=jnp.int32)[:, None]
    lists = jnp.where(slot < block_count, block_list[0].T, blocks + npeer * cap)
    power, source, target, near_coord, lists = lax.optimization_barrier(
        (power, source, target, near_coord, lists)
    )
    npts = float(points * slices)
    to_right, to_left = weighted(
        (((2, 0), (1, 1)), ((2, 1), (3, 0))), rank, shots, power, kernels, npts, ranges
    )
    from_left = shifted(to_right, "event", 1)
    from_right = shifted(to_left, "event", -1)
    mine_a, mine_b, ahead_a, behind_b = weighted(
        (((0, 0),), ((0, 1),), ((1, 0),), ((3, 1),)), rank, shots, power, kernels, npts, ranges
    )
    left_a = shifted(ahead_a + from_left[:nparams], "event", 1)
    right_b = shifted(behind_b + from_right[:nparams], "event", -1)
    own_a = mine_a + left_a + from_right[nparams:]
    own_b = mine_b + right_b + from_left[nparams:]

    left_a = shifted(own_a, "event", 1)
    right_b = shifted(own_b, "event", -1)
    left_b = shifted(own_b, "event", 1)
    right_a = shifted(own_a, "event", -1)
    far_a = shifted(left_a, "event", 1)
    far_b = shifted(right_b, "event", -1)

    sends, full = gathered(
        rank, send, near_coord,
        (own_a, own_b, right_a, right_b, far_a, far_b, left_a, left_b),
    )
    parts = [shifted(x, "cuts", OFFSETS[g]) for g, x in enumerate(sends)]
    return smooth(lists, target, source, full, parts)


def solution(mesh):
    placed = (
        P("event", None, "cuts"),
        P(),
        P(None, "cuts"),
        P("cuts", "event", None, None),
        P("cuts", "event", None),
        P("cuts", "event"),
    )
    return jax.shard_map(
        body, mesh=mesh, in_specs=placed, out_specs=P(None, ("cuts", "event")), check_vma=False
    )
```

```python
import functools

import jax
import jax.numpy as jnp
from jax import lax
from jax.experimental import pallas as pl
from jax.experimental.pallas import tpu as pltpu
from jax.sharding import PartitionSpec as P

BLOCK = 128
OFFSETS = (1, -1, 2, -2, 3, -3)
BF = jnp.bfloat16
F32 = jnp.float32
LOG2E = 1.4426950408889634
NT = (((1,), (1,)), ((), ()))
TN = (((0,), (0,)), ((), ()))
VMEM = pl.BlockSpec(memory_space=pltpu.VMEM)
SMEM = pl.BlockSpec(memory_space=pltpu.SMEM)
HBM = pl.BlockSpec(memory_space=pltpu.HBM)


def params(mib):
    return pltpu.CompilerParams(vmem_limit_bytes=mib << 20)


def cost(flops, moved):
    return pl.CostEstimate(flops=flops, bytes_accessed=moved, transcendentals=0)


def shifted(value, axis, steps):
    count = lax.axis_size(axis)
    pairs = [(source, (source + steps) % count) for source in range(count)]
    return lax.ppermute(value, axis, pairs)


def held(x):
    return pltpu.with_memory_space_constraint(x, pltpu.HBM)


def rows(shape):
    return lax.broadcasted_iota(jnp.int32, shape, 0)


def block(index):
    return pl.ds(pl.multiple_of(index * BLOCK, BLOCK), BLOCK)


def power_kernel(kernels, out, local, sems):
    params_here, count = kernels.shape[0], kernels.shape[1] // 8
    copies = [
        pltpu.make_async_copy(kernels.at[p], local.at[p], sems.at[p])
        for p in range(params_here)
    ]
    for copy in copies:
        copy.start()
    lane = lax.broadcasted_iota(jnp.int32, (8, BLOCK), 1)
    tile = jnp.zeros((8, BLOCK), F32)
    for p in range(params_here):
        copies[p].wait()

        def add(i, totals):
            found = []
            for part in range(4):
                x = local[p, pl.ds(pl.multiple_of((i * 4 + part) * 8, 8), 8), :]
                found.append(totals[part] + x * x)
            return tuple(found)
        zero = jnp.zeros((8, BLOCK), F32)
        totals = lax.fori_loop(0, count // 4, add, (zero,) * 4, unroll=4)
        total = (totals[0] + totals[1]) + (totals[2] + totals[3])
        tile = jnp.where(lane == p, jnp.sum(total, axis=1, keepdims=True), tile)
    for peer in range(out.shape[0]):
        out[peer] = tile


def local_power(kernels, peers):
    return pl.pallas_call(
        power_kernel,
        out_shape=jax.ShapeDtypeStruct((peers, 8, BLOCK), F32),
        in_specs=[HBM],
        out_specs=VMEM,
        scratch_shapes=[
            pltpu.VMEM(kernels.shape, F32),
            pltpu.SemaphoreType.DMA((kernels.shape[0],)),
        ],
        compiler_params=params(16),
        cost_estimate=cost(2 * kernels.size, 4 * kernels.size),
    )(kernels)


def scale_kernel(npts, ranges, plan, rank, shots, power, kernels, *rest):
    outs, local, sems = rest[:-2], rest[-2], rest[-1]
    me = rank[0]
    span = local.shape[2]
    pieces = [(out, at, turn, side) for out, parts in zip(outs, plan) for at, (turn, side) in enumerate(parts)]
    copies = []
    for n, (_, _, turn, side) in enumerate(pieces):
        base = pl.multiple_of((lax.rem(me + turn, ranges) * 2 + side) * span, span)
        copies.append(pltpu.make_async_copy(
            kernels.at[:, pl.ds(base, span), :], local.at[n], sems.at[n]
        ))
        copies[-1].start()
    total = jnp.sum(power[...], axis=0)
    total = total + pltpu.roll(total, 2, 0)
    total = total + pltpu.roll(total, 4, 0)
    weight = jnp.int32(0)
    for event in range(shots.shape[0]):
        weight += shots[event]
    weight = jnp.full((8, BLOCK), weight, jnp.int32).astype(F32)
    row = rows((8, BLOCK))
    shot = jnp.where(
        row % 2 == 0,
        jnp.full((8, BLOCK), shots[2 * me], jnp.int32),
        jnp.full((8, BLOCK), shots[2 * me + 1], jnp.int32),
    ).astype(F32)
    scale = shot / (jnp.sqrt(total / npts + 1e-06) * weight)
    nparams = kernels.shape[0]
    factors = [jnp.broadcast_to(scale[:, p:p + 1], (8, BLOCK)) for p in range(nparams)]
    for n, (out, at, _, _) in enumerate(pieces):
        copies[n].wait()
        for p in range(nparams):
            def one(i, _):
                low = pl.multiple_of(i * 16, 16)
                x = local[n, p, pl.ds(low, 8), :] * factors[p]
                y = local[n, p, pl.ds(low + 8, 8), :] * factors[p]
                x = x + pltpu.roll(x, 7, 0)
                y = y + pltpu.roll(y, 1, 0)
                out[at * nparams + p, pl.ds(pl.multiple_of(i * 8, 8), 8), :] = jnp.where(row % 2 == 0, x, y)
                return 0
            lax.fori_loop(0, span // 16, one, 0, unroll=4)


def weighted(plan, rank, shots, power, kernels, npts, ranges):
    nparams = kernels.shape[0]
    span = kernels.shape[1] // (2 * ranges)
    count = sum(len(parts) for parts in plan)
    return pl.pallas_call(
        functools.partial(scale_kernel, npts, ranges, plan),
        out_shape=[
            jax.ShapeDtypeStruct((nparams * len(parts), span // 2, BLOCK), F32) for parts in plan
        ],
        in_specs=[SMEM, SMEM, VMEM, HBM],
        out_specs=[VMEM] * len(plan),
        scratch_shapes=[
            pltpu.VMEM((count, nparams, span, BLOCK), F32),
            pltpu.SemaphoreType.DMA((count,)),
        ],
        compiler_params=params(16),
        cost_estimate=cost(3 * kernels.size, 6 * kernels.size),
    )(rank, shots, power, kernels)


def source_rows(x):
    row = rows(x.shape)
    high = x.astype(BF).astype(F32)
    rest = x - high
    low = rest.astype(BF).astype(F32)
    first = jnp.where(row == 7, low, high)
    second = jnp.where(row == 3, rest - low, jnp.where(row == 7, 0.0, low))
    return jnp.concatenate([first, second], axis=0).astype(BF)


def target_rows(x):
    row = rows(x.shape)
    high = x.astype(BF).astype(F32)
    low = x - high
    first = jnp.where(row % 4 == 3, 1.0, jnp.where(row < 4, high, low))
    second = jnp.where(row == 7, 0.0, first)
    return jnp.concatenate([first, second], axis=0).astype(BF)


def field_rows(x):
    high = x.astype(BF).astype(F32)
    return jnp.concatenate([high, x - high], axis=0).astype(BF)


def coord_kernel(rank, send, coords, source_out, target_out, out, source, target, sems):
    targets = target.shape[0]
    start = rank[0] * targets
    npeer, cap = send.shape
    blocks = coords.shape[1] // BLOCK

    def point(index):
        x = (coords[:, block(index)] - 1.5) * (LOG2E ** 0.5)
        half = -0.5 * jnp.sum(x * x, axis=0, keepdims=True)
        return jnp.concatenate([x, half], axis=0)

    def sources(i, _):
        x = point(i)
        source[i] = source_rows(jnp.concatenate([x, x], axis=0))
        return 0
    lax.fori_loop(0, blocks, sources, 0, unroll=4)

    def aims(i, _):
        x = point(start + i)
        target[i] = target_rows(jnp.concatenate([x, x], axis=0))
        return 0
    lax.fori_loop(0, targets, aims, 0, unroll=4)
    copies = [
        pltpu.make_async_copy(source, source_out, sems.at[0]),
        pltpu.make_async_copy(target, target_out, sems.at[1]),
    ]
    for copy in copies:
        copy.start()
    for group in range(npeer):
        def pick(i, _):
            pair = [point(send[group, 2 * i]), point(send[group, 2 * i + 1])]
            out[group * (cap // 2) + i] = jnp.concatenate(pair, axis=0)
            return 0
        lax.fori_loop(0, cap // 2, pick, 0, unroll=4)
    for copy in copies:
        copy.wait()


def coord_tables(rank, send, coords, targets):
    blocks = coords.shape[1] // BLOCK
    return pl.pallas_call(
        coord_kernel,
        out_shape=[
            jax.ShapeDtypeStruct((blocks, 16, BLOCK), BF),
            jax.ShapeDtypeStruct((targets, 16, BLOCK), BF),
            jax.ShapeDtypeStruct((send.size // 2, 8, BLOCK), F32),
        ],
        in_specs=[SMEM, SMEM, VMEM],
        out_specs=[HBM, HBM, VMEM],
        scratch_shapes=[
            pltpu.VMEM((blocks, 16, BLOCK), BF),
            pltpu.VMEM((targets, 16, BLOCK), BF),
            pltpu.SemaphoreType.DMA((2,)),
        ],
        compiler_params=params(16),
        cost_estimate=cost(coords.size * 30, coords.size * 12),
    )(rank, send, coords)


def place(index):
    inner = index & 7
    return index - inner + 2 * (inner & 3) + (inner >> 2)


def gather_kernel(rank, send, coords, *rest):
    parts, outs, full, sem = rest[:8], rest[8:-2], rest[-2], rest[-1]
    npeer, cap = send.shape
    copies = []
    for group, out in enumerate(outs):
        copies.append(pltpu.make_async_copy(
            coords.at[pl.ds(group * (cap // 2), cap // 2)],
            out.at[pl.ds(cap, cap // 2)],
            sem.at[group],
        ))
        copies[-1].start()
    half = parts[0].shape[1]
    blocks = 8 * half
    me = rank[0]
    for turn, part in enumerate(parts):
        base = (lax.rem(me + turn // 2, 4) * 2 + turn % 2) * half
        for p in range(7):
            def store(i, _):
                at = pl.multiple_of(i * 8, 8)
                full[pl.ds(pl.multiple_of(p * blocks + base + at, 8), 8), :] = part[p, pl.ds(at, 8), :]
                return 0
            lax.fori_loop(0, half // 8, store, 0, unroll=True)

    def ones(i, _):
        full[pl.ds(pl.multiple_of(7 * blocks + i * 8, 8), 8), :] = jnp.ones((8, BLOCK), F32)
        return 0
    lax.fori_loop(0, blocks // 8, ones, 0, unroll=8)
    for group, out in enumerate(outs):
        def pick(i, _):
            out[i] = full[pl.ds(place(send[group, i]), 8, stride=blocks), :]
            return 0
        lax.fori_loop(0, cap, pick, 0, unroll=8)
    for copy in copies:
        copy.wait()


def gathered(rank, send, coords, parts):
    blocks = 8 * parts[0].shape[1]
    npeer, cap = send.shape
    *sends, full = pl.pallas_call(
        gather_kernel,
        out_shape=[jax.ShapeDtypeStruct((cap + cap // 2, 8, BLOCK), F32)] * npeer
        + [jax.ShapeDtypeStruct((8 * blocks, BLOCK), F32)],
        in_specs=[SMEM, SMEM, HBM] + [VMEM] * 8,
        out_specs=[VMEM] * (npeer + 1),
        scratch_shapes=[pltpu.SemaphoreType.DMA((npeer,))],
        compiler_params=params(16),
    )(rank, send, held(coords), *parts)
    return sends, full


def smooth_kernel(lists, target_in, source_in, full, *rest):
    parts = rest[:-5]
    out, target, source, table, sems = rest[-5:]
    blocks, targets = source_in.shape[0], target.shape[0]
    copies = [
        pltpu.make_async_copy(source_in, source.at[pl.ds(0, blocks)], sems.at[0]),
        pltpu.make_async_copy(target_in, target, sems.at[1]),
    ]
    for copy in copies:
        copy.start()

    def build(i, _):
        table[i] = field_rows(full[pl.ds(place(i), 8, stride=blocks), :])
        return 0
    lax.fori_loop(0, blocks, build, 0, unroll=8)
    cap = parts[0].shape[0] * 2 // 3
    for group, part in enumerate(parts):
        base = blocks + group * cap

        def coords(i, _):
            x = part[cap + i]
            turned = pltpu.roll(x, 4, 0)
            row = rows(x.shape)
            source[base + 2 * i] = source_rows(jnp.where(row < 4, x, turned))
            source[base + 2 * i + 1] = source_rows(jnp.where(row < 4, turned, x))
            return 0
        lax.fori_loop(0, cap // 2, coords, 0, unroll=4)

        def fields(i, _):
            table[base + i] = field_rows(part[i])
            return 0
        lax.fori_loop(0, cap, fields, 0, unroll=8)
    none = blocks + len(parts) * cap
    source[none] = jnp.zeros((16, BLOCK), BF)
    table[none] = jnp.zeros((16, BLOCK), BF)
    for copy in copies:
        copy.wait()
    kmax = lists.shape[0]

    def one(b):
        slots = [lists[k, b] for k in range(kmax)]
        coords = jnp.concatenate([source[s] for s in slots], axis=1)
        power = lax.dot_general(target[b], coords, TN, preferred_element_type=F32)
        weight = jnp.exp2(power)
        high = weight.astype(BF)
        low = (weight - high.astype(F32)).astype(BF)
        field = jnp.concatenate([table[s] for s in slots], axis=1)
        sums = lax.dot_general(
            jnp.concatenate([high, low], axis=1),
            jnp.concatenate([field, field], axis=1),
            NT,
            preferred_element_type=F32,
        ).T
        out[:, block(b)] = (sums[0:7] + sums[8:15]) / sums[7:8]

    def step(i, _):
        for turn in range(4):
            one(4 * i + turn)
        return 0
    lax.fori_loop(0, targets // 4, step, 0)


def smooth(lists, target, source, full, parts):
    targets = target.shape[0]
    size = source.shape[0] + len(parts) * (parts[0].shape[0] * 2 // 3) + 1
    return pl.pallas_call(
        smooth_kernel,
        out_shape=jax.ShapeDtypeStruct((7, targets * BLOCK), F32),
        in_specs=[SMEM, HBM, HBM, VMEM] + [VMEM] * len(parts),
        out_specs=VMEM,
        scratch_shapes=[
            pltpu.VMEM((targets, 16, BLOCK), BF),
            pltpu.VMEM((size, 16, BLOCK), BF),
            pltpu.VMEM((size, 16, BLOCK), BF),
            pltpu.SemaphoreType.DMA((2,)),
        ],
        compiler_params=params(24),
    )(lists, held(target), held(source), full, *parts)


def body(kernels, shots, coords, send_list, block_list, block_count):
    slices = lax.axis_size("cuts")
    ranges = lax.axis_size("event")
    events, nparams, points = kernels.shape
    blocks = points // BLOCK
    npeer, cap = send_list.shape[2:]
    targets = block_list.shape[1]
    rank = jnp.reshape(lax.axis_index("event"), (1,)).astype(jnp.int32)
    send = send_list.reshape(npeer, cap)
    kernels = kernels.transpose(1, 0, 2).reshape(nparams, events, blocks, BLOCK)
    kernels = kernels.transpose(0, 2, 1, 3).reshape(nparams, blocks * events, BLOCK)
    kernels = held(kernels)

    power = local_power(kernels, slices)
    coords, power = lax.optimization_barrier((coords, power))
    power = lax.all_to_all(power, "cuts", 0, 0)
    source, target, near_coord = coord_tables(rank, send, coords, targets)
    slot = jnp.arange(block_list.shape[2], dtype=jnp.int32)[:, None]
    lists = jnp.where(slot < block_count, block_list[0].T, blocks + npeer * cap)
    power, source, target, near_coord, lists = lax.optimization_barrier(
        (power, source, target, near_coord, lists)
    )
    npts = float(points * slices)
    to_right, to_left = weighted(
        (((2, 0), (1, 1)), ((2, 1), (3, 0))), rank, shots, power, kernels, npts, ranges
    )
    from_left = shifted(to_right, "event", 1)
    from_right = shifted(to_left, "event", -1)
    mine_a, mine_b, ahead_a, behind_b = weighted(
        (((0, 0),), ((0, 1),), ((1, 0),), ((3, 1),)), rank, shots, power, kernels, npts, ranges
    )
    from_left, from_right = lax.optimization_barrier((from_left, from_right))
    left_a = shifted(ahead_a + from_left[:nparams], "event", 1)
    right_b = shifted(behind_b + from_right[:nparams], "event", -1)
    left_a, right_b = lax.optimization_barrier((left_a, right_b))
    own_a = mine_a + left_a + from_right[nparams:]
    own_b = mine_b + right_b + from_left[nparams:]

    left_a = shifted(own_a, "event", 1)
    right_b = shifted(own_b, "event", -1)
    left_b = shifted(own_b, "event", 1)
    right_a = shifted(own_a, "event", -1)
    far_a = shifted(left_a, "event", 1)
    far_b = shifted(right_b, "event", -1)

    sends, full = gathered(
        rank, send, near_coord,
        (own_a, own_b, right_a, right_b, far_a, far_b, left_a, left_b),
    )
    parts = [shifted(x, "cuts", OFFSETS[g]) for g, x in enumerate(sends)]
    return smooth(lists, target, source, full, parts)


def solution(mesh):
    placed = (
        P("event", None, "cuts"),
        P(),
        P(None, "cuts"),
        P("cuts", "event", None, None),
        P("cuts", "event", None),
        P("cuts", "event"),
    )
    return jax.shard_map(
        body, mesh=mesh, in_specs=placed, out_specs=P(None, ("cuts", "event")), check_vma=False
    )
```

```python
import functools

import jax
import jax.numpy as jnp
from jax import lax
from jax.experimental import pallas as pl
from jax.experimental.pallas import tpu as pltpu
from jax.sharding import PartitionSpec as P

BLOCK = 128
OFFSETS = (1, -1, 2, -2, 3, -3)
BF = jnp.bfloat16
F32 = jnp.float32
LOG2E = 1.4426950408889634
NT = (((1,), (1,)), ((), ()))
TN = (((0,), (0,)), ((), ()))
VMEM = pl.BlockSpec(memory_space=pltpu.VMEM)
SMEM = pl.BlockSpec(memory_space=pltpu.SMEM)
ANY = pl.BlockSpec(memory_space=pl.ANY)
HBM = pl.BlockSpec(memory_space=pltpu.HBM)


def params(mib):
    return pltpu.CompilerParams(vmem_limit_bytes=mib << 20)


def cost(flops, moved):
    return pl.CostEstimate(flops=flops, bytes_accessed=moved, transcendentals=0)


def shifted(value, axis, steps):
    count = lax.axis_size(axis)
    pairs = [(source, (source + steps) % count) for source in range(count)]
    return lax.ppermute(value, axis, pairs)


def held(x):
    return pltpu.with_memory_space_constraint(x, pltpu.HBM)


def rows(shape):
    return lax.broadcasted_iota(jnp.int32, shape, 0)


def block(index):
    return pl.ds(pl.multiple_of(index * BLOCK, BLOCK), BLOCK)


def power_kernel(kernels, out, local, sems):
    params_here, count = kernels.shape[0], kernels.shape[1] // 8
    copies = [
        pltpu.make_async_copy(kernels.at[p], local.at[p], sems.at[p])
        for p in range(params_here)
    ]
    for copy in copies:
        copy.start()
    lane = lax.broadcasted_iota(jnp.int32, (8, BLOCK), 1)
    tile = jnp.zeros((8, BLOCK), F32)
    for p in range(params_here):
        copies[p].wait()

        def add(i, totals):
            found = []
            for part in range(4):
                x = local[p, pl.ds(pl.multiple_of((i * 4 + part) * 8, 8), 8), :]
                found.append(totals[part] + x * x)
            return tuple(found)
        zero = jnp.zeros((8, BLOCK), F32)
        totals = lax.fori_loop(0, count // 4, add, (zero,) * 4, unroll=4)
        total = (totals[0] + totals[1]) + (totals[2] + totals[3])
        tile = jnp.where(lane == p, jnp.sum(total, axis=1, keepdims=True), tile)
    for peer in range(out.shape[0]):
        out[peer] = tile


def local_power(kernels, peers):
    return pl.pallas_call(
        power_kernel,
        out_shape=jax.ShapeDtypeStruct((peers, 8, BLOCK), F32),
        in_specs=[HBM],
        out_specs=VMEM,
        scratch_shapes=[
            pltpu.VMEM(kernels.shape, F32),
            pltpu.SemaphoreType.DMA((kernels.shape[0],)),
        ],
        compiler_params=params(16),
        cost_estimate=cost(2 * kernels.size, 4 * kernels.size),
    )(kernels)


def scale_kernel(npts, ranges, plan, rank, shots, power, kernels, ready, *rest):
    outs, local, sems = rest[:-2], rest[-2], rest[-1]
    me = rank[0]
    span = local.shape[2]
    pieces = [(out, at, turn, side) for out, parts in zip(outs, plan) for at, (turn, side) in enumerate(parts)]
    copies = []
    for n, (_, _, turn, side) in enumerate(pieces):
        base = pl.multiple_of((lax.rem(me + turn, ranges) * 2 + side) * span, span)
        copies.append(pltpu.make_async_copy(
            kernels.at[:, pl.ds(base, span), :], local.at[n], sems.at[n]
        ))
        copies[-1].start()
    total = jnp.sum(power[...], axis=0)
    total = total + pltpu.roll(total, 2, 0)
    total = total + pltpu.roll(total, 4, 0)
    weight = jnp.int32(0)
    for event in range(shots.shape[0]):
        weight += shots[event]
    weight = jnp.full((8, BLOCK), weight, jnp.int32).astype(F32)
    row = rows((8, BLOCK))
    shot = jnp.where(
        row % 2 == 0,
        jnp.full((8, BLOCK), shots[2 * me], jnp.int32),
        jnp.full((8, BLOCK), shots[2 * me + 1], jnp.int32),
    ).astype(F32)
    scale = shot / (jnp.sqrt(total / npts + 1e-06) * weight)
    nparams = kernels.shape[0]
    factors = [jnp.broadcast_to(scale[:, p:p + 1], (8, BLOCK)) for p in range(nparams)]
    for n, (out, at, _, _) in enumerate(pieces):
        copies[n].wait()
        for p in range(nparams):
            def one(i, _):
                low = pl.multiple_of(i * 16, 16)
                x = local[n, p, pl.ds(low, 8), :] * factors[p]
                y = local[n, p, pl.ds(low + 8, 8), :] * factors[p]
                x = x + pltpu.roll(x, 7, 0)
                y = y + pltpu.roll(y, 1, 0)
                out[at * nparams + p, pl.ds(pl.multiple_of(i * 8, 8), 8), :] = jnp.where(row % 2 == 0, x, y)
                return 0
            lax.fori_loop(0, span // 16, one, 0, unroll=4)


def weighted(plan, rank, shots, power, kernels, ready, npts, ranges):
    nparams = kernels.shape[0]
    span = kernels.shape[1] // (2 * ranges)
    count = sum(len(parts) for parts in plan)
    return pl.pallas_call(
        functools.partial(scale_kernel, npts, ranges, plan),
        out_shape=[
            jax.ShapeDtypeStruct((nparams * len(parts), span // 2, BLOCK), F32) for parts in plan
        ],
        in_specs=[SMEM, SMEM, VMEM, HBM, ANY],
        out_specs=[VMEM] * len(plan),
        scratch_shapes=[
            pltpu.VMEM((count, nparams, span, BLOCK), F32),
            pltpu.SemaphoreType.DMA((count,)),
        ],
        compiler_params=params(16),
        cost_estimate=cost(3 * kernels.size, 6 * kernels.size),
    )(rank, shots, power, kernels, ready)


def source_rows(x):
    row = rows(x.shape)
    high = x.astype(BF).astype(F32)
    rest = x - high
    low = rest.astype(BF).astype(F32)
    first = jnp.where(row == 7, low, high)
    second = jnp.where(row == 3, rest - low, jnp.where(row == 7, 0.0, low))
    return jnp.concatenate([first, second], axis=0).astype(BF)


def target_rows(x):
    row = rows(x.shape)
    high = x.astype(BF).astype(F32)
    low = x - high
    first = jnp.where(row % 4 == 3, 1.0, jnp.where(row < 4, high, low))
    second = jnp.where(row == 7, 0.0, first)
    return jnp.concatenate([first, second], axis=0).astype(BF)


def field_rows(x):
    high = x.astype(BF).astype(F32)
    return jnp.concatenate([high, x - high], axis=0).astype(BF)


def coord_kernel(rank, send, coords, source_out, target_out, out, token, source, target, sems):
    token[...] = jnp.zeros_like(token)
    targets = target.shape[0]
    start = rank[0] * targets
    npeer, cap = send.shape
    blocks = coords.shape[1] // BLOCK

    def point(index):
        x = (coords[:, block(index)] - 1.5) * (LOG2E ** 0.5)
        half = -0.5 * jnp.sum(x * x, axis=0, keepdims=True)
        return jnp.concatenate([x, half], axis=0)

    def sources(i, _):
        x = point(i)
        source[i] = source_rows(jnp.concatenate([x, x], axis=0))
        return 0
    lax.fori_loop(0, blocks, sources, 0, unroll=4)

    def aims(i, _):
        x = point(start + i)
        target[i] = target_rows(jnp.concatenate([x, x], axis=0))
        return 0
    lax.fori_loop(0, targets, aims, 0, unroll=4)
    copies = [
        pltpu.make_async_copy(source, source_out, sems.at[0]),
        pltpu.make_async_copy(target, target_out, sems.at[1]),
    ]
    for copy in copies:
        copy.start()
    for group in range(npeer):
        def pick(i, _):
            pair = [point(send[group, 2 * i]), point(send[group, 2 * i + 1])]
            out[group * (cap // 2) + i] = jnp.concatenate(pair, axis=0)
            return 0
        lax.fori_loop(0, cap // 2, pick, 0, unroll=4)
    for copy in copies:
        copy.wait()


def coord_tables(rank, send, coords, targets):
    blocks = coords.shape[1] // BLOCK
    return pl.pallas_call(
        coord_kernel,
        out_shape=[
            jax.ShapeDtypeStruct((blocks, 16, BLOCK), BF),
            jax.ShapeDtypeStruct((targets, 16, BLOCK), BF),
            jax.ShapeDtypeStruct((send.size // 2, 8, BLOCK), F32),
            jax.ShapeDtypeStruct((8, BLOCK), F32),
        ],
        in_specs=[SMEM, SMEM, VMEM],
        out_specs=[HBM, HBM, VMEM, VMEM],
        scratch_shapes=[
            pltpu.VMEM((blocks, 16, BLOCK), BF),
            pltpu.VMEM((targets, 16, BLOCK), BF),
            pltpu.SemaphoreType.DMA((2,)),
        ],
        compiler_params=params(16),
        cost_estimate=cost(coords.size * 30, coords.size * 12),
    )(rank, send, coords)


def place(index):
    inner = index & 7
    return index - inner + 2 * (inner & 3) + (inner >> 2)


def gather_kernel(rank, send, coords, ready, *rest):
    parts, outs, full, sem = rest[:8], rest[8:-2], rest[-2], rest[-1]
    npeer, cap = send.shape
    copies = []
    for group, out in enumerate(outs):
        copies.append(pltpu.make_async_copy(
            coords.at[pl.ds(group * (cap // 2), cap // 2)],
            out.at[pl.ds(cap, cap // 2)],
            sem.at[group],
        ))
        copies[-1].start()
    half = parts[0].shape[1]
    blocks = 8 * half
    me = rank[0]
    for turn, part in enumerate(parts):
        base = (lax.rem(me + turn // 2, 4) * 2 + turn % 2) * half
        for p in range(7):
            def store(i, _):
                at = pl.multiple_of(i * 8, 8)
                full[pl.ds(pl.multiple_of(p * blocks + base + at, 8), 8), :] = part[p, pl.ds(at, 8), :]
                return 0
            lax.fori_loop(0, half // 8, store, 0, unroll=True)

    def ones(i, _):
        full[pl.ds(pl.multiple_of(7 * blocks + i * 8, 8), 8), :] = jnp.ones((8, BLOCK), F32)
        return 0
    lax.fori_loop(0, blocks // 8, ones, 0, unroll=8)
    for group, out in enumerate(outs):
        def pick(i, _):
            out[i] = full[pl.ds(place(send[group, i]), 8, stride=blocks), :]
            return 0
        lax.fori_loop(0, cap, pick, 0, unroll=8)
    for copy in copies:
        copy.wait()


def gathered(rank, send, coords, ready, parts):
    blocks = 8 * parts[0].shape[1]
    npeer, cap = send.shape
    *sends, full = pl.pallas_call(
        gather_kernel,
        out_shape=[jax.ShapeDtypeStruct((cap + cap // 2, 8, BLOCK), F32)] * npeer
        + [jax.ShapeDtypeStruct((8 * blocks, BLOCK), F32)],
        in_specs=[SMEM, SMEM, HBM, ANY] + [VMEM] * 8,
        out_specs=[VMEM] * (npeer + 1),
        scratch_shapes=[pltpu.SemaphoreType.DMA((npeer,))],
        compiler_params=params(16),
    )(rank, send, held(coords), ready, *parts)
    return sends, full


TURNS = 4


def work_order(lists, counts, none):
    kmax, targets = lists.shape
    slot = jnp.arange(kmax, dtype=jnp.int32)[:, None]
    index = jnp.arange(targets, dtype=jnp.int32)
    key = counts[0] * targets + (targets - 1 - index)
    place_of = jnp.sum((key[None, :] > key[:, None]).astype(jnp.int32), axis=1)
    order = jnp.sum(jnp.where(place_of[:, None] == index[None, :], index[:, None], 0), axis=0)
    above = jnp.arange(kmax, kmax // 2 + 1, -1, dtype=jnp.int32)
    groups = jnp.sum((counts >= above[:, None]).astype(jnp.int32), axis=1)
    bounds = jnp.concatenate([
        (groups + TURNS - 1) // TURNS, jnp.full((1,), targets // TURNS, jnp.int32)
    ])
    return jnp.where(slot < counts, lists, none), order, bounds


def weigh(target, coords, field):
    power = lax.dot_general(target, coords, TN, preferred_element_type=F32)
    weight = jnp.exp2(power)
    high = weight.astype(BF)
    low = (weight - high.astype(F32)).astype(BF)
    return lax.dot_general(
        jnp.concatenate([high, low], axis=1), field, NT, preferred_element_type=F32
    ).T


def self_kernel(rank, source_in, target_in, own_a, own_b, out, source, target, sems):
    targets = target.shape[0]
    copies = [
        pltpu.make_async_copy(
            source_in.at[pl.ds(rank[0] * targets, targets)], source, sems.at[0]
        ),
        pltpu.make_async_copy(target_in, target, sems.at[1]),
    ]
    for copy in copies:
        copy.start()
    for copy in copies:
        copy.wait()
    half = targets // 2
    top = jnp.ones((1, BLOCK), F32)

    for side, own in enumerate((own_a, own_b)):
        def step(i, _):
            for turn in range(TURNS):
                at = TURNS * i + turn
                b = side * half + at
                x = own[pl.ds(place(at), 7, stride=half), :]
                field = field_rows(jnp.concatenate([x, top], axis=0))
                out[b] = weigh(target[b], source[b], jnp.concatenate([field, field], axis=1))
            return 0
        lax.fori_loop(0, half // TURNS, step, 0)


def self_sums(rank, source, target, own_a, own_b):
    targets = target.shape[0]
    return pl.pallas_call(
        self_kernel,
        out_shape=jax.ShapeDtypeStruct((targets, 16, BLOCK), F32),
        in_specs=[SMEM, HBM, HBM, VMEM, VMEM],
        out_specs=VMEM,
        scratch_shapes=[
            pltpu.VMEM((targets, 16, BLOCK), BF),
            pltpu.VMEM((targets, 16, BLOCK), BF),
            pltpu.SemaphoreType.DMA((2,)),
        ],
        compiler_params=params(16),
        cost_estimate=cost(5 * 10 ** 9, 10 ** 7),
    )(rank, held(source), held(target), own_a.reshape(-1, BLOCK), own_b.reshape(-1, BLOCK))


def smooth_kernel(lists, order, bounds, target_in, source_in, full, start, *rest):
    parts = rest[:-5]
    out, target, source, table, sems = rest[-5:]
    blocks, targets = source_in.shape[0], target.shape[0]
    copies = [
        pltpu.make_async_copy(source_in, source.at[pl.ds(0, blocks)], sems.at[0]),
        pltpu.make_async_copy(target_in, target, sems.at[1]),
    ]
    for copy in copies:
        copy.start()

    def build(i, _):
        table[i] = field_rows(full[pl.ds(place(i), 8, stride=blocks), :])
        return 0
    lax.fori_loop(0, blocks, build, 0, unroll=8)
    cap = parts[0].shape[0] * 2 // 3
    for group, part in enumerate(parts):
        base = blocks + group * cap

        def coords(i, _):
            x = part[cap + i]
            turned = pltpu.roll(x, 4, 0)
            row = rows(x.shape)
            source[base + 2 * i] = source_rows(jnp.where(row < 4, x, turned))
            source[base + 2 * i + 1] = source_rows(jnp.where(row < 4, turned, x))
            return 0
        lax.fori_loop(0, cap // 2, coords, 0, unroll=4)

        def fields(i, _):
            table[base + i] = field_rows(part[i])
            return 0
        lax.fori_loop(0, cap, fields, 0, unroll=8)
    none = blocks + len(parts) * cap
    source[none] = jnp.zeros((16, BLOCK), BF)
    table[none] = jnp.zeros((16, BLOCK), BF)
    for copy in copies:
        copy.wait()
    kmax = lists.shape[0]

    def one(b, count):
        slots = [lists[k, b] for k in range(1, 1 + count)]
        coords = jnp.concatenate([source[s] for s in slots], axis=1)
        field = jnp.concatenate([table[s] for s in slots] * 2, axis=1)
        total = weigh(target[b], coords, field) + start[b]
        out[:, block(b)] = (total[0:7] + total[8:15]) / total[7:8]

    first = 0
    for part, count in enumerate(range(kmax - 1, kmax // 2 - 1, -1)):
        def step(i, _):
            for turn in range(TURNS):
                one(order[TURNS * i + turn], count)
            return 0
        last = bounds[part]
        lax.fori_loop(first, last, step, 0)
        first = last


def smooth(lists, order, bounds, target, source, full, start, parts):
    targets = target.shape[0]
    size = source.shape[0] + len(parts) * (parts[0].shape[0] * 2 // 3) + 1
    return pl.pallas_call(
        smooth_kernel,
        out_shape=jax.ShapeDtypeStruct((7, targets * BLOCK), F32),
        in_specs=[SMEM, SMEM, SMEM, HBM, HBM, VMEM, VMEM] + [VMEM] * len(parts),
        out_specs=VMEM,
        scratch_shapes=[
            pltpu.VMEM((targets, 16, BLOCK), BF),
            pltpu.VMEM((size, 16, BLOCK), BF),
            pltpu.VMEM((size, 16, BLOCK), BF),
            pltpu.SemaphoreType.DMA((2,)),
        ],
        compiler_params=params(24),
    )(lists, order, bounds, held(target), held(source), full, start, *parts)


def body(kernels, shots, coords, send_list, block_list, block_count):
    slices = lax.axis_size("cuts")
    ranges = lax.axis_size("event")
    events, nparams, points = kernels.shape
    blocks = points // BLOCK
    npeer, cap = send_list.shape[2:]
    targets = block_list.shape[1]
    rank = jnp.reshape(lax.axis_index("event"), (1,)).astype(jnp.int32)
    send = send_list.reshape(npeer, cap)
    kernels = kernels.transpose(1, 0, 2).reshape(nparams, events, blocks, BLOCK)
    kernels = kernels.transpose(0, 2, 1, 3).reshape(nparams, blocks * events, BLOCK)
    kernels = held(kernels)

    power = local_power(kernels, slices)
    coords, power = lax.optimization_barrier((coords, power))
    power = lax.all_to_all(power, "cuts", 0, 0)
    source, target, near_coord, token = coord_tables(rank, send, coords, targets)
    lists, order, bounds = work_order(block_list[0].T, block_count, blocks + npeer * cap)
    npts = float(points * slices)
    across_a, across_b, ahead_b, behind_a = weighted(
        (((2, 0),), ((2, 1),), ((1, 1),), ((3, 0),)), rank, shots, power, kernels, token, npts, ranges
    )
    from_left = shifted(across_a, "event", 1)
    from_right = shifted(across_b, "event", -1)
    left_b = shifted(ahead_b, "event", 1)
    right_a = shifted(behind_a, "event", -1)
    mine_a, mine_b, ahead_a, behind_b = weighted(
        (((0, 0),), ((0, 1),), ((1, 0),), ((3, 1),)), rank, shots, power, kernels, token, npts, ranges
    )
    from_left, from_right, lists, order, bounds = lax.optimization_barrier(
        (from_left, from_right, lists, order, bounds)
    )
    left_a = shifted(ahead_a + from_left, "event", 1)
    right_b = shifted(behind_b + from_right, "event", -1)
    left_a, right_b, left_b, right_a = lax.optimization_barrier((left_a, right_b, left_b, right_a))
    own_a = mine_a + left_a + right_a
    own_b = mine_b + right_b + left_b

    left_a = shifted(own_a, "event", 1)
    right_b = shifted(own_b, "event", -1)
    left_b = shifted(own_b, "event", 1)
    right_a = shifted(own_a, "event", -1)
    far_a = shifted(left_a, "event", 1)
    far_b = shifted(right_b, "event", -1)
    start = self_sums(rank, source, target, own_a, own_b)

    sends, full = gathered(
        rank, send, near_coord, start,
        (own_a, own_b, right_a, right_b, far_a, far_b, left_a, left_b),
    )
    parts = [shifted(x, "cuts", OFFSETS[g]) for g, x in enumerate(sends)]
    return smooth(lists, order, bounds, target, source, full, start, parts)


def solution(mesh):
    placed = (
        P("event", None, "cuts"),
        P(),
        P(None, "cuts"),
        P("cuts", "event", None, None),
        P("cuts", "event", None),
        P("cuts", "event"),
    )
    return jax.shard_map(
        body, mesh=mesh, in_specs=placed, out_specs=P(None, ("cuts", "event")), check_vma=False
    )
```

```python
import functools

import jax
import jax.numpy as jnp
from jax import lax
from jax.experimental import pallas as pl
from jax.experimental.pallas import tpu as pltpu
from jax.sharding import PartitionSpec as P

BLOCK = 128
OFFSETS = (1, -1, 2, -2, 3, -3)
BF = jnp.bfloat16
F32 = jnp.float32
LOG2E = 1.4426950408889634
NT = (((1,), (1,)), ((), ()))
TN = (((0,), (0,)), ((), ()))
VMEM = pl.BlockSpec(memory_space=pltpu.VMEM)
SMEM = pl.BlockSpec(memory_space=pltpu.SMEM)
ANY = pl.BlockSpec(memory_space=pl.ANY)
HBM = pl.BlockSpec(memory_space=pltpu.HBM)


def params(mib):
    return pltpu.CompilerParams(vmem_limit_bytes=mib << 20)


def cost(flops, moved):
    return pl.CostEstimate(flops=flops, bytes_accessed=moved, transcendentals=0)


def shifted(value, axis, steps):
    count = lax.axis_size(axis)
    pairs = [(source, (source + steps) % count) for source in range(count)]
    return lax.ppermute(value, axis, pairs)


def held(x):
    return pltpu.with_memory_space_constraint(x, pltpu.HBM)


def rows(shape):
    return lax.broadcasted_iota(jnp.int32, shape, 0)


def block(index):
    return pl.ds(pl.multiple_of(index * BLOCK, BLOCK), BLOCK)


def power_kernel(kernels, out, local, sems):
    params_here, count = kernels.shape[0], kernels.shape[1] // 8
    copies = [
        pltpu.make_async_copy(kernels.at[p], local.at[p], sems.at[p])
        for p in range(params_here)
    ]
    for copy in copies:
        copy.start()
    lane = lax.broadcasted_iota(jnp.int32, (8, BLOCK), 1)
    tile = jnp.zeros((8, BLOCK), F32)
    for p in range(params_here):
        copies[p].wait()

        def add(i, totals):
            found = []
            for part in range(4):
                x = local[p, pl.ds(pl.multiple_of((i * 4 + part) * 8, 8), 8), :]
                found.append(totals[part] + x * x)
            return tuple(found)
        zero = jnp.zeros((8, BLOCK), F32)
        totals = lax.fori_loop(0, count // 4, add, (zero,) * 4, unroll=4)
        total = (totals[0] + totals[1]) + (totals[2] + totals[3])
        tile = jnp.where(lane == p, jnp.sum(total, axis=1, keepdims=True), tile)
    for peer in range(out.shape[0]):
        out[peer] = tile


def local_power(kernels, peers):
    return pl.pallas_call(
        power_kernel,
        out_shape=jax.ShapeDtypeStruct((peers, 8, BLOCK), F32),
        in_specs=[HBM],
        out_specs=VMEM,
        scratch_shapes=[
            pltpu.VMEM(kernels.shape, F32),
            pltpu.SemaphoreType.DMA((kernels.shape[0],)),
        ],
        compiler_params=params(16),
        cost_estimate=cost(2 * kernels.size, 4 * kernels.size),
    )(kernels)


def scale_kernel(npts, ranges, plan, rank, shots, power, kernels, ready, *rest):
    outs, local, sems = rest[:-2], rest[-2], rest[-1]
    me = rank[0]
    span = local.shape[2]
    pieces = [(out, at, turn, side) for out, parts in zip(outs, plan) for at, (turn, side) in enumerate(parts)]
    copies = []
    for n, (_, _, turn, side) in enumerate(pieces):
        base = pl.multiple_of((lax.rem(me + turn, ranges) * 2 + side) * span, span)
        copies.append(pltpu.make_async_copy(
            kernels.at[:, pl.ds(base, span), :], local.at[n], sems.at[n]
        ))
        copies[-1].start()
    total = jnp.sum(power[...], axis=0)
    total = total + pltpu.roll(total, 2, 0)
    total = total + pltpu.roll(total, 4, 0)
    weight = jnp.int32(0)
    for event in range(shots.shape[0]):
        weight += shots[event]
    weight = jnp.full((8, BLOCK), weight, jnp.int32).astype(F32)
    row = rows((8, BLOCK))
    shot = jnp.where(
        row % 2 == 0,
        jnp.full((8, BLOCK), shots[2 * me], jnp.int32),
        jnp.full((8, BLOCK), shots[2 * me + 1], jnp.int32),
    ).astype(F32)
    scale = shot / (jnp.sqrt(total / npts + 1e-06) * weight)
    nparams = kernels.shape[0]
    factors = [jnp.broadcast_to(scale[:, p:p + 1], (8, BLOCK)) for p in range(nparams)]
    for n, (out, at, _, _) in enumerate(pieces):
        copies[n].wait()
        for p in range(nparams):
            def one(i, _):
                low = pl.multiple_of(i * 16, 16)
                x = local[n, p, pl.ds(low, 8), :] * factors[p]
                y = local[n, p, pl.ds(low + 8, 8), :] * factors[p]
                x = x + pltpu.roll(x, 7, 0)
                y = y + pltpu.roll(y, 1, 0)
                out[at * nparams + p, pl.ds(pl.multiple_of(i * 8, 8), 8), :] = jnp.where(row % 2 == 0, x, y)
                return 0
            lax.fori_loop(0, span // 16, one, 0, unroll=4)


def weighted(plan, rank, shots, power, kernels, ready, npts, ranges):
    nparams = kernels.shape[0]
    span = kernels.shape[1] // (2 * ranges)
    count = sum(len(parts) for parts in plan)
    return pl.pallas_call(
        functools.partial(scale_kernel, npts, ranges, plan),
        out_shape=[
            jax.ShapeDtypeStruct((nparams * len(parts), span // 2, BLOCK), F32) for parts in plan
        ],
        in_specs=[SMEM, SMEM, VMEM, HBM, ANY],
        out_specs=[VMEM] * len(plan),
        scratch_shapes=[
            pltpu.VMEM((count, nparams, span, BLOCK), F32),
            pltpu.SemaphoreType.DMA((count,)),
        ],
        compiler_params=params(16),
        cost_estimate=cost(3 * kernels.size, 6 * kernels.size),
    )(rank, shots, power, kernels, ready)


def source_rows(x):
    row = rows(x.shape)
    high = x.astype(BF).astype(F32)
    rest = x - high
    low = rest.astype(BF).astype(F32)
    first = jnp.where(row == 7, low, high)
    second = jnp.where(row == 3, rest - low, jnp.where(row == 7, 0.0, low))
    return jnp.concatenate([first, second], axis=0).astype(BF)


def target_rows(x):
    row = rows(x.shape)
    high = x.astype(BF).astype(F32)
    low = x - high
    first = jnp.where(row % 4 == 3, 1.0, jnp.where(row < 4, high, low))
    second = jnp.where(row == 7, 0.0, first)
    return jnp.concatenate([first, second], axis=0).astype(BF)


def field_rows(x):
    high = x.astype(BF).astype(F32)
    return jnp.concatenate([high, x - high], axis=0).astype(BF)


def coord_kernel(rank, send, coords, source_out, target_out, out, token, source, target, sems):
    token[...] = jnp.zeros_like(token)
    targets = target.shape[0]
    start = rank[0] * targets
    npeer, cap = send.shape
    blocks = coords.shape[1] // BLOCK

    def point(index):
        x = (coords[:, block(index)] - 1.5) * (LOG2E ** 0.5)
        half = -0.5 * jnp.sum(x * x, axis=0, keepdims=True)
        return jnp.concatenate([x, half], axis=0)

    def sources(i, _):
        x = point(i)
        source[i] = source_rows(jnp.concatenate([x, x], axis=0))
        return 0
    lax.fori_loop(0, blocks, sources, 0, unroll=4)

    def aims(i, _):
        x = point(start + i)
        target[i] = target_rows(jnp.concatenate([x, x], axis=0))
        return 0
    lax.fori_loop(0, targets, aims, 0, unroll=4)
    copies = [
        pltpu.make_async_copy(source, source_out, sems.at[0]),
        pltpu.make_async_copy(target, target_out, sems.at[1]),
    ]
    for copy in copies:
        copy.start()
    for group in range(npeer):
        def pick(i, _):
            pair = [point(send[group, 2 * i]), point(send[group, 2 * i + 1])]
            out[group * (cap // 2) + i] = jnp.concatenate(pair, axis=0)
            return 0
        lax.fori_loop(0, cap // 2, pick, 0, unroll=4)
    for copy in copies:
        copy.wait()


def coord_tables(rank, send, coords, targets):
    blocks = coords.shape[1] // BLOCK
    return pl.pallas_call(
        coord_kernel,
        out_shape=[
            jax.ShapeDtypeStruct((blocks, 16, BLOCK), BF),
            jax.ShapeDtypeStruct((targets, 16, BLOCK), BF),
            jax.ShapeDtypeStruct((send.size // 2, 8, BLOCK), F32),
            jax.ShapeDtypeStruct((8, BLOCK), F32),
        ],
        in_specs=[SMEM, SMEM, VMEM],
        out_specs=[HBM, HBM, VMEM, VMEM],
        scratch_shapes=[
            pltpu.VMEM((blocks, 16, BLOCK), BF),
            pltpu.VMEM((targets, 16, BLOCK), BF),
            pltpu.SemaphoreType.DMA((2,)),
        ],
        compiler_params=params(16),
        cost_estimate=cost(coords.size * 30, coords.size * 12),
    )(rank, send, coords)


def place(index):
    inner = index & 7
    return index - inner + 2 * (inner & 3) + (inner >> 2)


def gather_kernel(rank, send, coords, ready, *rest):
    parts, outs, full, sem = rest[:8], rest[8:-2], rest[-2], rest[-1]
    npeer, cap = send.shape
    copies = []
    for group, out in enumerate(outs):
        copies.append(pltpu.make_async_copy(
            coords.at[pl.ds(group * (cap // 2), cap // 2)],
            out.at[pl.ds(cap, cap // 2)],
            sem.at[group],
        ))
        copies[-1].start()
    half = parts[0].shape[1]
    blocks = 8 * half
    me = rank[0]
    for turn, part in enumerate(parts):
        base = (lax.rem(me + turn // 2, 4) * 2 + turn % 2) * half
        for p in range(7):
            def store(i, _):
                at = pl.multiple_of(i * 8, 8)
                full[pl.ds(pl.multiple_of(p * blocks + base + at, 8), 8), :] = part[p, pl.ds(at, 8), :]
                return 0
            lax.fori_loop(0, half // 8, store, 0, unroll=True)

    def ones(i, _):
        full[pl.ds(pl.multiple_of(7 * blocks + i * 8, 8), 8), :] = jnp.ones((8, BLOCK), F32)
        return 0
    lax.fori_loop(0, blocks // 8, ones, 0, unroll=8)
    for group, out in enumerate(outs):
        def pick(i, _):
            out[i] = full[pl.ds(place(send[group, i]), 8, stride=blocks), :]
            return 0
        lax.fori_loop(0, cap, pick, 0, unroll=8)
    for copy in copies:
        copy.wait()


def gathered(rank, send, coords, ready, parts):
    blocks = 8 * parts[0].shape[1]
    npeer, cap = send.shape
    *sends, full = pl.pallas_call(
        gather_kernel,
        out_shape=[jax.ShapeDtypeStruct((cap + cap // 2, 8, BLOCK), F32)] * npeer
        + [jax.ShapeDtypeStruct((8 * blocks, BLOCK), F32)],
        in_specs=[SMEM, SMEM, HBM, ANY] + [VMEM] * 8,
        out_specs=[VMEM] * (npeer + 1),
        scratch_shapes=[pltpu.SemaphoreType.DMA((npeer,))],
        compiler_params=params(16),
    )(rank, send, held(coords), ready, *parts)
    return sends, full


TURNS = 8
SELVES = 16


def work_order(lists, counts, none):
    kmax, targets = lists.shape
    slot = jnp.arange(kmax, dtype=jnp.int32)[:, None]
    index = jnp.arange(targets, dtype=jnp.int32)
    key = counts[0] * targets + (targets - 1 - index)
    place_of = jnp.sum((key[None, :] > key[:, None]).astype(jnp.int32), axis=1)
    order = jnp.sum(jnp.where(place_of[:, None] == index[None, :], index[:, None], 0), axis=0)
    above = jnp.arange(kmax, kmax // 2 + 1, -1, dtype=jnp.int32)
    groups = jnp.sum((counts >= above[:, None]).astype(jnp.int32), axis=1)
    bounds = jnp.concatenate([
        (groups + TURNS - 1) // TURNS, jnp.full((1,), targets // TURNS, jnp.int32)
    ])
    return jnp.where(slot < counts, lists, none), order, bounds


def weigh(target, coords, field):
    power = lax.dot_general(target, coords, TN, preferred_element_type=F32)
    weight = jnp.exp2(power)
    high = weight.astype(BF)
    low = (weight - high.astype(F32)).astype(BF)
    return lax.dot_general(
        jnp.concatenate([high, low], axis=1), field, NT, preferred_element_type=F32
    ).T


def self_kernel(rank, source_in, target_in, own_a, own_b, out, source, target, sems):
    targets = target.shape[0]
    copies = [
        pltpu.make_async_copy(
            source_in.at[pl.ds(rank[0] * targets, targets)], source, sems.at[0]
        ),
        pltpu.make_async_copy(target_in, target, sems.at[1]),
    ]
    for copy in copies:
        copy.start()
    for copy in copies:
        copy.wait()
    half = targets // 2
    top = jnp.ones((1, BLOCK), F32)

    for side, own in enumerate((own_a, own_b)):
        def step(i, _):
            for turn in range(SELVES):
                at = SELVES * i + turn
                b = side * half + at
                x = own[pl.ds(place(at), 7, stride=half), :]
                field = field_rows(jnp.concatenate([x, top], axis=0))
                out[b] = weigh(target[b], source[b], jnp.concatenate([field, field], axis=1))
            return 0
        lax.fori_loop(0, half // SELVES, step, 0)


def self_sums(rank, source, target, own_a, own_b):
    targets = target.shape[0]
    return pl.pallas_call(
        self_kernel,
        out_shape=jax.ShapeDtypeStruct((targets, 16, BLOCK), F32),
        in_specs=[SMEM, HBM, HBM, VMEM, VMEM],
        out_specs=VMEM,
        scratch_shapes=[
            pltpu.VMEM((targets, 16, BLOCK), BF),
            pltpu.VMEM((targets, 16, BLOCK), BF),
            pltpu.SemaphoreType.DMA((2,)),
        ],
        compiler_params=params(16),
        cost_estimate=cost(5 * 10 ** 9, 10 ** 7),
    )(rank, held(source), held(target), own_a.reshape(-1, BLOCK), own_b.reshape(-1, BLOCK))


def smooth_kernel(lists, order, bounds, target_in, source_in, full, start, *rest):
    parts = rest[:-5]
    out, target, source, table, sems = rest[-5:]
    blocks, targets = source_in.shape[0], target.shape[0]
    copies = [
        pltpu.make_async_copy(source_in, source.at[pl.ds(0, blocks)], sems.at[0]),
        pltpu.make_async_copy(target_in, target, sems.at[1]),
    ]
    for copy in copies:
        copy.start()

    def build(i, _):
        table[i] = field_rows(full[pl.ds(place(i), 8, stride=blocks), :])
        return 0
    lax.fori_loop(0, blocks, build, 0, unroll=8)
    cap = parts[0].shape[0] * 2 // 3
    for group, part in enumerate(parts):
        base = blocks + group * cap

        def coords(i, _):
            x = part[cap + i]
            turned = pltpu.roll(x, 4, 0)
            row = rows(x.shape)
            source[base + 2 * i] = source_rows(jnp.where(row < 4, x, turned))
            source[base + 2 * i + 1] = source_rows(jnp.where(row < 4, turned, x))
            return 0
        lax.fori_loop(0, cap // 2, coords, 0, unroll=4)

        def fields(i, _):
            table[base + i] = field_rows(part[i])
            return 0
        lax.fori_loop(0, cap, fields, 0, unroll=8)
    none = blocks + len(parts) * cap
    source[none] = jnp.zeros((16, BLOCK), BF)
    table[none] = jnp.zeros((16, BLOCK), BF)
    for copy in copies:
        copy.wait()
    kmax = lists.shape[0]

    def one(b, count):
        slots = [lists[k, b] for k in range(1, 1 + count)]
        coords = jnp.concatenate([source[s] for s in slots], axis=1)
        field = jnp.concatenate([table[s] for s in slots] * 2, axis=1)
        total = weigh(target[b], coords, field) + start[b]
        out[:, block(b)] = (total[0:7] + total[8:15]) / total[7:8]

    first = 0
    for part, count in enumerate(range(kmax - 1, kmax // 2 - 1, -1)):
        def step(i, _):
            for turn in range(TURNS):
                one(order[TURNS * i + turn], count)
            return 0
        last = bounds[part]
        lax.fori_loop(first, last, step, 0)
        first = last


def smooth(lists, order, bounds, target, source, full, start, parts):
    targets = target.shape[0]
    size = source.shape[0] + len(parts) * (parts[0].shape[0] * 2 // 3) + 1
    return pl.pallas_call(
        smooth_kernel,
        out_shape=jax.ShapeDtypeStruct((7, targets * BLOCK), F32),
        in_specs=[SMEM, SMEM, SMEM, HBM, HBM, VMEM, VMEM] + [VMEM] * len(parts),
        out_specs=VMEM,
        scratch_shapes=[
            pltpu.VMEM((targets, 16, BLOCK), BF),
            pltpu.VMEM((size, 16, BLOCK), BF),
            pltpu.VMEM((size, 16, BLOCK), BF),
            pltpu.SemaphoreType.DMA((2,)),
        ],
        compiler_params=params(24),
    )(lists, order, bounds, held(target), held(source), full, start, *parts)


def body(kernels, shots, coords, send_list, block_list, block_count):
    slices = lax.axis_size("cuts")
    ranges = lax.axis_size("event")
    events, nparams, points = kernels.shape
    blocks = points // BLOCK
    npeer, cap = send_list.shape[2:]
    targets = block_list.shape[1]
    rank = jnp.reshape(lax.axis_index("event"), (1,)).astype(jnp.int32)
    send = send_list.reshape(npeer, cap)
    kernels = kernels.transpose(1, 0, 2).reshape(nparams, events, blocks, BLOCK)
    kernels = kernels.transpose(0, 2, 1, 3).reshape(nparams, blocks * events, BLOCK)
    kernels = held(kernels)

    power = local_power(kernels, slices)
    coords, power = lax.optimization_barrier((coords, power))
    power = lax.all_to_all(power, "cuts", 0, 0)
    source, target, near_coord, token = coord_tables(rank, send, coords, targets)
    lists, order, bounds = work_order(block_list[0].T, block_count, blocks + npeer * cap)
    npts = float(points * slices)
    across_a, across_b, ahead_b, behind_a = weighted(
        (((2, 0),), ((2, 1),), ((1, 1),), ((3, 0),)), rank, shots, power, kernels, token, npts, ranges
    )
    from_left = shifted(across_a, "event", 1)
    from_right = shifted(across_b, "event", -1)
    left_b = shifted(ahead_b, "event", 1)
    right_a = shifted(behind_a, "event", -1)
    mine_a, mine_b, ahead_a, behind_b = weighted(
        (((0, 0),), ((0, 1),), ((1, 0),), ((3, 1),)), rank, shots, power, kernels, token, npts, ranges
    )
    from_left, from_right, lists, order, bounds = lax.optimization_barrier(
        (from_left, from_right, lists, order, bounds)
    )
    left_a = shifted(ahead_a + from_left, "event", 1)
    right_b = shifted(behind_b + from_right, "event", -1)
    left_a, right_b, left_b, right_a = lax.optimization_barrier((left_a, right_b, left_b, right_a))
    own_a = mine_a + left_a + right_a
    own_b = mine_b + right_b + left_b

    left_a = shifted(own_a, "event", 1)
    right_b = shifted(own_b, "event", -1)
    left_b = shifted(own_b, "event", 1)
    right_a = shifted(own_a, "event", -1)
    far_a = shifted(left_a, "event", 1)
    far_b = shifted(right_b, "event", -1)
    start = self_sums(rank, source, target, own_a, own_b)

    sends, full = gathered(
        rank, send, near_coord, start,
        (own_a, own_b, right_a, right_b, far_a, far_b, left_a, left_b),
    )
    parts = [shifted(x, "cuts", OFFSETS[g]) for g, x in enumerate(sends)]
    return smooth(lists, order, bounds, target, source, full, start, parts)


def solution(mesh):
    placed = (
        P("event", None, "cuts"),
        P(),
        P(None, "cuts"),
        P("cuts", "event", None, None),
        P("cuts", "event", None),
        P("cuts", "event"),
    )
    return jax.shard_map(
        body, mesh=mesh, in_specs=placed, out_specs=P(None, ("cuts", "event")), check_vma=False
    )
```

```python
import functools

import jax
import jax.numpy as jnp
from jax import lax
from jax.experimental import pallas as pl
from jax.experimental.pallas import tpu as pltpu
from jax.sharding import PartitionSpec as P

BLOCK = 128
OFFSETS = (1, -1, 2, -2, 3, -3)
BF = jnp.bfloat16
F32 = jnp.float32
LOG2E = 1.4426950408889634
NT = (((1,), (1,)), ((), ()))
TN = (((0,), (0,)), ((), ()))
VMEM = pl.BlockSpec(memory_space=pltpu.VMEM)
SMEM = pl.BlockSpec(memory_space=pltpu.SMEM)
ANY = pl.BlockSpec(memory_space=pl.ANY)
HBM = pl.BlockSpec(memory_space=pltpu.HBM)


def params(mib):
    return pltpu.CompilerParams(vmem_limit_bytes=mib << 20)


def cost(flops, moved):
    return pl.CostEstimate(flops=flops, bytes_accessed=moved, transcendentals=0)


def shifted(value, axis, steps):
    count = lax.axis_size(axis)
    pairs = [(source, (source + steps) % count) for source in range(count)]
    return lax.ppermute(value, axis, pairs)


def held(x):
    return pltpu.with_memory_space_constraint(x, pltpu.HBM)


def rows(shape):
    return lax.broadcasted_iota(jnp.int32, shape, 0)


def block(index):
    return pl.ds(pl.multiple_of(index * BLOCK, BLOCK), BLOCK)


def power_kernel(kernels, out, local, sems):
    params_here, count = kernels.shape[0], kernels.shape[1] // 8
    copies = [
        pltpu.make_async_copy(kernels.at[p], local.at[p], sems.at[p])
        for p in range(params_here)
    ]
    for copy in copies:
        copy.start()
    lane = lax.broadcasted_iota(jnp.int32, (8, BLOCK), 1)
    tile = jnp.zeros((8, BLOCK), F32)
    for p in range(params_here):
        copies[p].wait()

        def add(i, totals):
            found = []
            for part in range(4):
                x = local[p, pl.ds(pl.multiple_of((i * 4 + part) * 8, 8), 8), :]
                found.append(totals[part] + x * x)
            return tuple(found)
        zero = jnp.zeros((8, BLOCK), F32)
        totals = lax.fori_loop(0, count // 4, add, (zero,) * 4, unroll=4)
        total = (totals[0] + totals[1]) + (totals[2] + totals[3])
        tile = jnp.where(lane == p, jnp.sum(total, axis=1, keepdims=True), tile)
    for peer in range(out.shape[0]):
        out[peer] = tile


def local_power(kernels, peers):
    return pl.pallas_call(
        power_kernel,
        out_shape=jax.ShapeDtypeStruct((peers, 8, BLOCK), F32),
        in_specs=[HBM],
        out_specs=VMEM,
        scratch_shapes=[
            pltpu.VMEM(kernels.shape, F32),
            pltpu.SemaphoreType.DMA((kernels.shape[0],)),
        ],
        compiler_params=params(16),
        cost_estimate=cost(2 * kernels.size, 4 * kernels.size),
    )(kernels)


def scale_kernel(npts, ranges, plan, rank, shots, power, kernels, ready, *rest):
    outs, local, sems = rest[:-2], rest[-2], rest[-1]
    me = rank[0]
    span = local.shape[2]
    pieces = [(out, at, turn, side) for out, parts in zip(outs, plan) for at, (turn, side) in enumerate(parts)]
    copies = []
    for n, (_, _, turn, side) in enumerate(pieces):
        base = pl.multiple_of((lax.rem(me + turn, ranges) * 2 + side) * span, span)
        copies.append(pltpu.make_async_copy(
            kernels.at[:, pl.ds(base, span), :], local.at[n], sems.at[n]
        ))
        copies[-1].start()
    total = jnp.sum(power[...], axis=0)
    total = total + pltpu.roll(total, 2, 0)
    total = total + pltpu.roll(total, 4, 0)
    weight = jnp.int32(0)
    for event in range(shots.shape[0]):
        weight += shots[event]
    weight = jnp.full((8, BLOCK), weight, jnp.int32).astype(F32)
    row = rows((8, BLOCK))
    shot = jnp.where(
        row % 2 == 0,
        jnp.full((8, BLOCK), shots[2 * me], jnp.int32),
        jnp.full((8, BLOCK), shots[2 * me + 1], jnp.int32),
    ).astype(F32)
    scale = shot / (jnp.sqrt(total / npts + 1e-06) * weight)
    nparams = kernels.shape[0]
    factors = [jnp.broadcast_to(scale[:, p:p + 1], (8, BLOCK)) for p in range(nparams)]
    for n, (out, at, _, _) in enumerate(pieces):
        copies[n].wait()
        for p in range(nparams):
            def one(i, _):
                low = pl.multiple_of(i * 16, 16)
                x = local[n, p, pl.ds(low, 8), :] * factors[p]
                y = local[n, p, pl.ds(low + 8, 8), :] * factors[p]
                x = x + pltpu.roll(x, 7, 0)
                y = y + pltpu.roll(y, 1, 0)
                out[at * nparams + p, pl.ds(pl.multiple_of(i * 8, 8), 8), :] = jnp.where(row % 2 == 0, x, y)
                return 0
            lax.fori_loop(0, span // 16, one, 0, unroll=4)


def weighted(plan, rank, shots, power, kernels, ready, npts, ranges):
    nparams = kernels.shape[0]
    span = kernels.shape[1] // (2 * ranges)
    count = sum(len(parts) for parts in plan)
    return pl.pallas_call(
        functools.partial(scale_kernel, npts, ranges, plan),
        out_shape=[
            jax.ShapeDtypeStruct((nparams * len(parts), span // 2, BLOCK), F32) for parts in plan
        ],
        in_specs=[SMEM, SMEM, VMEM, HBM, ANY],
        out_specs=[VMEM] * len(plan),
        scratch_shapes=[
            pltpu.VMEM((count, nparams, span, BLOCK), F32),
            pltpu.SemaphoreType.DMA((count,)),
        ],
        compiler_params=params(16),
        cost_estimate=cost(3 * kernels.size, 6 * kernels.size),
    )(rank, shots, power, kernels, ready)


def source_rows(x):
    row = rows(x.shape)
    high = x.astype(BF).astype(F32)
    rest = x - high
    low = rest.astype(BF).astype(F32)
    first = jnp.where(row == 7, low, high)
    second = jnp.where(row == 3, rest - low, jnp.where(row == 7, 0.0, low))
    return jnp.concatenate([first, second], axis=0).astype(BF)


def target_rows(x):
    row = rows(x.shape)
    high = x.astype(BF).astype(F32)
    low = x - high
    first = jnp.where(row % 4 == 3, 1.0, jnp.where(row < 4, high, low))
    second = jnp.where(row == 7, 0.0, first)
    return jnp.concatenate([first, second], axis=0).astype(BF)


def field_rows(x):
    high = x.astype(BF).astype(F32)
    return jnp.concatenate([high, x - high], axis=0).astype(BF)


def point(coords, index):
    x = (coords[:, block(index)] - 1.5) * (LOG2E ** 0.5)
    half = -0.5 * jnp.sum(x * x, axis=0, keepdims=True)
    return jnp.concatenate([x, half], axis=0)


def coord_kernel(send, coords, source, out, token):
    token[...] = jnp.zeros_like(token)
    npeer, cap = send.shape
    blocks = coords.shape[1] // BLOCK

    def sources(i, _):
        x = point(coords, i)
        source[i] = source_rows(jnp.concatenate([x, x], axis=0))
        return 0
    lax.fori_loop(0, blocks, sources, 0, unroll=4)

    for group in range(npeer):
        def pick(i, _):
            pair = [point(coords, send[group, 2 * i + k]) for k in range(2)]
            out[group * (cap // 2) + i] = jnp.concatenate(pair, axis=0)
            return 0
        lax.fori_loop(0, cap // 2, pick, 0, unroll=4)


def coord_tables(send, coords):
    blocks = coords.shape[1] // BLOCK
    return pl.pallas_call(
        coord_kernel,
        out_shape=[
            jax.ShapeDtypeStruct((blocks, 16, BLOCK), BF),
            jax.ShapeDtypeStruct((send.size // 2, 8, BLOCK), F32),
            jax.ShapeDtypeStruct((8, BLOCK), F32),
        ],
        in_specs=[SMEM, VMEM],
        out_specs=[VMEM] * 3,
        compiler_params=params(16),
        cost_estimate=cost(coords.size * 30, coords.size * 12),
    )(send, coords)


def aim_kernel(rank, coords_in, out, coords, sem):
    targets, size = out.shape[0], coords.shape[1]
    copy = pltpu.make_async_copy(
        coords_in.at[:, pl.ds(pl.multiple_of(rank[0] * size, size), size)], coords, sem
    )
    copy.start()
    across = lax.broadcasted_iota(jnp.int32, (BLOCK, BLOCK), 1)
    same = jnp.where(rows((BLOCK, BLOCK)) == across, 1.0, 0.0).astype(BF)
    copy.wait()

    def step(i, _):
        x = point(coords, i)
        x = target_rows(jnp.concatenate([x, x], axis=0))
        out[i] = lax.dot_general(same, x, NT, preferred_element_type=F32).astype(BF)
        return 0
    lax.fori_loop(0, targets, step, 0, unroll=8)


def aims(rank, coords, targets):
    return pl.pallas_call(
        aim_kernel,
        out_shape=jax.ShapeDtypeStruct((targets, BLOCK, 16), BF),
        in_specs=[SMEM, HBM],
        out_specs=VMEM,
        scratch_shapes=[
            pltpu.VMEM((coords.shape[0], targets * BLOCK), F32),
            pltpu.SemaphoreType.DMA(()),
        ],
        compiler_params=params(16),
        cost_estimate=cost(2 * 10 ** 9, 10 ** 7),
    )(rank, held(coords))


def place(index):
    inner = index & 7
    return index - inner + 2 * (inner & 3) + (inner >> 2)


def gather_kernel(rank, send, coords, ready, *rest):
    parts, outs, full, sem = rest[:8], rest[8:-2], rest[-2], rest[-1]
    npeer, cap = send.shape
    copies = []
    for group, out in enumerate(outs):
        copies.append(pltpu.make_async_copy(
            coords.at[pl.ds(group * (cap // 2), cap // 2)],
            out.at[pl.ds(cap, cap // 2)],
            sem.at[group],
        ))
        copies[-1].start()
    half = parts[0].shape[1]
    blocks = 8 * half
    me = rank[0]
    for turn, part in enumerate(parts):
        base = (lax.rem(me + turn // 2, 4) * 2 + turn % 2) * half
        for p in range(7):
            def store(i, _):
                at = pl.multiple_of(i * 8, 8)
                full[pl.ds(pl.multiple_of(p * blocks + base + at, 8), 8), :] = part[p, pl.ds(at, 8), :]
                return 0
            lax.fori_loop(0, half // 8, store, 0, unroll=True)

    def ones(i, _):
        full[pl.ds(pl.multiple_of(7 * blocks + i * 8, 8), 8), :] = jnp.ones((8, BLOCK), F32)
        return 0
    lax.fori_loop(0, blocks // 8, ones, 0, unroll=8)
    for group, out in enumerate(outs):
        def pick(i, _):
            out[i] = full[pl.ds(place(send[group, i]), 8, stride=blocks), :]
            return 0
        lax.fori_loop(0, cap, pick, 0, unroll=8)
    for copy in copies:
        copy.wait()


def gathered(rank, send, coords, ready, parts):
    blocks = 8 * parts[0].shape[1]
    npeer, cap = send.shape
    *sends, full = pl.pallas_call(
        gather_kernel,
        out_shape=[jax.ShapeDtypeStruct((cap + cap // 2, 8, BLOCK), F32)] * npeer
        + [jax.ShapeDtypeStruct((8 * blocks, BLOCK), F32)],
        in_specs=[SMEM, SMEM, VMEM, ANY] + [VMEM] * 8,
        out_specs=[VMEM] * (npeer + 1),
        scratch_shapes=[pltpu.SemaphoreType.DMA((npeer,))],
        compiler_params=params(16),
    )(rank, send, coords, ready, *parts)
    return sends, full


TURNS = 8


def work_order(lists, counts, none):
    kmax, targets = lists.shape
    slot = jnp.arange(kmax, dtype=jnp.int32)[:, None]
    index = jnp.arange(targets, dtype=jnp.int32)
    key = counts[0] * targets + (targets - 1 - index)
    place_of = jnp.sum((key[None, :] > key[:, None]).astype(jnp.int32), axis=1)
    order = jnp.sum(jnp.where(place_of[:, None] == index[None, :], index[:, None], 0), axis=0)
    above = jnp.arange(kmax, kmax // 2 + 1, -1, dtype=jnp.int32)
    groups = jnp.sum((counts >= above[:, None]).astype(jnp.int32), axis=1)
    bounds = jnp.concatenate([
        (groups + TURNS - 1) // TURNS, jnp.full((1,), targets // TURNS, jnp.int32)
    ])
    return jnp.where(slot < counts, lists, none), order, bounds


def weigh(target, coords, field):
    power = jnp.dot(target, coords, preferred_element_type=F32)
    weight = jnp.exp2(power)
    high = weight.astype(BF)
    low = (weight - high.astype(F32)).astype(BF)
    return lax.dot_general(
        jnp.concatenate([high, low], axis=1), field, NT, preferred_element_type=F32
    )


def turned(parts):
    packed = None
    for at, part in enumerate(parts):
        size = part.shape[1]
        wide = jnp.concatenate([part, jnp.zeros((BLOCK, BLOCK - size), F32)], axis=1)
        wide = pltpu.roll(wide, size * at, 1) if at else wide
        packed = wide if packed is None else packed + wide
    return packed.T


def self_kernel(rank, source, target, own_a, own_b, out):
    targets = target.shape[0]
    first = rank[0] * targets
    half = targets // 2
    top = jnp.ones((1, BLOCK), F32)

    for side, own in enumerate((own_a, own_b)):
        def step(i, _):
            parts = []
            for turn in range(TURNS):
                at = TURNS * i + turn
                b = side * half + at
                x = own[pl.ds(place(at), 7, stride=half), :]
                field = field_rows(jnp.concatenate([x, top], axis=0))
                parts.append(weigh(target[b], source[first + b], jnp.concatenate([field, field], axis=1)))
            total = turned(parts)
            for turn in range(TURNS):
                out[side * half + TURNS * i + turn] = total[16 * turn:16 * turn + 16]
            return 0
        lax.fori_loop(0, half // TURNS, step, 0)


def self_sums(rank, source, target, own_a, own_b):
    targets = target.shape[0]
    return pl.pallas_call(
        self_kernel,
        out_shape=jax.ShapeDtypeStruct((targets, 16, BLOCK), F32),
        in_specs=[SMEM] + [VMEM] * 4,
        out_specs=VMEM,
        compiler_params=params(16),
        cost_estimate=cost(5 * 10 ** 9, 10 ** 7),
    )(rank, source, target, own_a.reshape(-1, BLOCK), own_b.reshape(-1, BLOCK))


def smooth_kernel(lists, order, bounds, target, source_in, full, start, *rest):
    parts = rest[:-4]
    out, source, table, sems = rest[-4:]
    blocks, targets = source_in.shape[0], target.shape[0]
    copies = [
        pltpu.make_async_copy(source_in, source.at[pl.ds(0, blocks)], sems.at[0]),
    ]
    for copy in copies:
        copy.start()

    def build(i, _):
        table[i] = field_rows(full[pl.ds(place(i), 8, stride=blocks), :])
        return 0
    lax.fori_loop(0, blocks, build, 0, unroll=8)
    cap = parts[0].shape[0] * 2 // 3
    for group, part in enumerate(parts):
        base = blocks + group * cap

        def coords(i, _):
            x = part[cap + i]
            turned = pltpu.roll(x, 4, 0)
            row = rows(x.shape)
            source[base + 2 * i] = source_rows(jnp.where(row < 4, x, turned))
            source[base + 2 * i + 1] = source_rows(jnp.where(row < 4, turned, x))
            return 0
        lax.fori_loop(0, cap // 2, coords, 0, unroll=4)

        def fields(i, _):
            table[base + i] = field_rows(part[i])
            return 0
        lax.fori_loop(0, cap, fields, 0, unroll=8)
    none = blocks + len(parts) * cap
    source[none] = jnp.zeros((16, BLOCK), BF)
    table[none] = jnp.zeros((16, BLOCK), BF)
    for copy in copies:
        copy.wait()
    kmax = lists.shape[0]

    def one(b, count):
        slots = [lists[k, b] for k in range(1, 1 + count)]
        coords = jnp.concatenate([source[s] for s in slots], axis=1)
        field = jnp.concatenate([table[s] for s in slots] * 2, axis=1)
        return weigh(target[b], coords, field)

    first = 0
    for part, count in enumerate(range(kmax - 1, kmax // 2 - 1, -1)):
        def step(i, _):
            aims = [order[TURNS * i + turn] for turn in range(TURNS)]
            sums = turned([one(b, count) for b in aims])
            for turn, b in enumerate(aims):
                total = sums[16 * turn:16 * turn + 16] + start[b]
                out[:, block(b)] = (total[0:7] + total[8:15]) / total[7:8]
            return 0
        last = bounds[part]
        lax.fori_loop(first, last, step, 0)
        first = last


def smooth(lists, order, bounds, target, source, full, start, parts):
    targets = target.shape[0]
    size = source.shape[0] + len(parts) * (parts[0].shape[0] * 2 // 3) + 1
    return pl.pallas_call(
        smooth_kernel,
        out_shape=jax.ShapeDtypeStruct((7, targets * BLOCK), F32),
        in_specs=[SMEM] * 3 + [VMEM] * 4 + [VMEM] * len(parts),
        out_specs=VMEM,
        scratch_shapes=[
            pltpu.VMEM((size, 16, BLOCK), BF),
            pltpu.VMEM((size, 16, BLOCK), BF),
            pltpu.SemaphoreType.DMA((1,)),
        ],
        compiler_params=params(24),
    )(lists, order, bounds, target, source, full, start, *parts)


def body(kernels, shots, coords, send_list, block_list, block_count):
    slices = lax.axis_size("cuts")
    ranges = lax.axis_size("event")
    events, nparams, points = kernels.shape
    blocks = points // BLOCK
    npeer, cap = send_list.shape[2:]
    targets = block_list.shape[1]
    rank = jnp.reshape(lax.axis_index("event"), (1,)).astype(jnp.int32)
    send = send_list.reshape(npeer, cap)
    kernels = kernels.transpose(1, 0, 2).reshape(nparams, events, blocks, BLOCK)
    kernels = kernels.transpose(0, 2, 1, 3).reshape(nparams, blocks * events, BLOCK)
    kernels = held(kernels)

    power = local_power(kernels, slices)
    coords, power = lax.optimization_barrier((coords, power))
    power = lax.all_to_all(power, "cuts", 0, 0)
    source, near_coord, token = coord_tables(send, coords)
    target = aims(rank, coords, targets)
    lists, order, bounds = work_order(block_list[0].T, block_count, blocks + npeer * cap)
    npts = float(points * slices)
    across_a, across_b, ahead_b, behind_a = weighted(
        (((2, 0),), ((2, 1),), ((1, 1),), ((3, 0),)), rank, shots, power, kernels, token, npts, ranges
    )
    from_left = shifted(across_a, "event", 1)
    from_right = shifted(across_b, "event", -1)
    left_b = shifted(ahead_b, "event", 1)
    right_a = shifted(behind_a, "event", -1)
    mine_a, mine_b, ahead_a, behind_b = weighted(
        (((0, 0),), ((0, 1),), ((1, 0),), ((3, 1),)), rank, shots, power, kernels, token, npts, ranges
    )
    from_left, from_right, lists, order, bounds = lax.optimization_barrier(
        (from_left, from_right, lists, order, bounds)
    )
    left_a = shifted(ahead_a + from_left, "event", 1)
    right_b = shifted(behind_b + from_right, "event", -1)
    left_a, right_b, left_b, right_a, target = lax.optimization_barrier(
        (left_a, right_b, left_b, right_a, target)
    )
    own_a = mine_a + left_a + right_a
    own_b = mine_b + right_b + left_b

    left_a = shifted(own_a, "event", 1)
    right_b = shifted(own_b, "event", -1)
    left_b = shifted(own_b, "event", 1)
    right_a = shifted(own_a, "event", -1)
    far_a = shifted(left_a, "event", 1)
    far_b = shifted(right_b, "event", -1)
    start = self_sums(rank, source, target, own_a, own_b)

    sends, full = gathered(
        rank, send, near_coord, start,
        (own_a, own_b, right_a, right_b, far_a, far_b, left_a, left_b),
    )
    parts = [shifted(x, "cuts", OFFSETS[g]) for g, x in enumerate(sends)]
    return smooth(lists, order, bounds, target, source, full, start, parts)


def solution(mesh):
    placed = (
        P("event", None, "cuts"),
        P(),
        P(None, "cuts"),
        P("cuts", "event", None, None),
        P("cuts", "event", None),
        P("cuts", "event"),
    )
    return jax.shard_map(
        body, mesh=mesh, in_specs=placed, out_specs=P(None, ("cuts", "event")), check_vma=False
    )
```

```python
import functools

import jax
import jax.numpy as jnp
from jax import lax
from jax.experimental import pallas as pl
from jax.experimental.pallas import tpu as pltpu
from jax.sharding import PartitionSpec as P

BLOCK = 128
OFFSETS = (1, -1, 2, -2, 3, -3)
BF = jnp.bfloat16
F32 = jnp.float32
LOG2E = 1.4426950408889634
NT = (((1,), (1,)), ((), ()))
TN = (((0,), (0,)), ((), ()))
VMEM = pl.BlockSpec(memory_space=pltpu.VMEM)
SMEM = pl.BlockSpec(memory_space=pltpu.SMEM)
ANY = pl.BlockSpec(memory_space=pl.ANY)
HBM = pl.BlockSpec(memory_space=pltpu.HBM)


def params(mib):
    return pltpu.CompilerParams(vmem_limit_bytes=mib << 20)


def cost(flops, moved):
    return pl.CostEstimate(flops=flops, bytes_accessed=moved, transcendentals=0)


def shifted(value, axis, steps):
    count = lax.axis_size(axis)
    pairs = [(source, (source + steps) % count) for source in range(count)]
    return lax.ppermute(value, axis, pairs)


def held(x):
    return pltpu.with_memory_space_constraint(x, pltpu.HBM)


def rows(shape):
    return lax.broadcasted_iota(jnp.int32, shape, 0)


def block(index):
    return pl.ds(pl.multiple_of(index * BLOCK, BLOCK), BLOCK)


def power_kernel(kernels, out, local, sems):
    params_here, count = kernels.shape[0], kernels.shape[1] // 8
    copies = [
        pltpu.make_async_copy(kernels.at[p], local.at[p], sems.at[p])
        for p in range(params_here)
    ]
    for copy in copies:
        copy.start()
    lane = lax.broadcasted_iota(jnp.int32, (8, BLOCK), 1)
    tile = jnp.zeros((8, BLOCK), F32)
    for p in range(params_here):
        copies[p].wait()

        def add(i, totals):
            found = []
            for part in range(4):
                x = local[p, pl.ds(pl.multiple_of((i * 4 + part) * 8, 8), 8), :]
                found.append(totals[part] + x * x)
            return tuple(found)
        zero = jnp.zeros((8, BLOCK), F32)
        totals = lax.fori_loop(0, count // 4, add, (zero,) * 4, unroll=4)
        total = (totals[0] + totals[1]) + (totals[2] + totals[3])
        tile = jnp.where(lane == p, jnp.sum(total, axis=1, keepdims=True), tile)
    for peer in range(out.shape[0]):
        out[peer] = tile


def local_power(kernels, peers):
    return pl.pallas_call(
        power_kernel,
        out_shape=jax.ShapeDtypeStruct((peers, 8, BLOCK), F32),
        in_specs=[HBM],
        out_specs=VMEM,
        scratch_shapes=[
            pltpu.VMEM(kernels.shape, F32),
            pltpu.SemaphoreType.DMA((kernels.shape[0],)),
        ],
        compiler_params=params(16),
        cost_estimate=cost(2 * kernels.size, 4 * kernels.size),
    )(kernels)


def scale_kernel(npts, ranges, plan, rank, shots, power, kernels, ready, *rest):
    outs, local, sems = rest[:-2], rest[-2], rest[-1]
    me = rank[0]
    span = local.shape[2]
    pieces = [(out, at, turn, side) for out, parts in zip(outs, plan) for at, (turn, side) in enumerate(parts)]
    copies = []
    for n, (_, _, turn, side) in enumerate(pieces):
        base = pl.multiple_of((lax.rem(me + turn, ranges) * 2 + side) * span, span)
        copies.append(pltpu.make_async_copy(
            kernels.at[:, pl.ds(base, span), :], local.at[n], sems.at[n]
        ))
        copies[-1].start()
    total = jnp.sum(power[...], axis=0)
    total = total + pltpu.roll(total, 2, 0)
    total = total + pltpu.roll(total, 4, 0)
    weight = jnp.int32(0)
    for event in range(shots.shape[0]):
        weight += shots[event]
    weight = jnp.full((8, BLOCK), weight, jnp.int32).astype(F32)
    row = rows((8, BLOCK))
    shot = jnp.where(
        row % 2 == 0,
        jnp.full((8, BLOCK), shots[2 * me], jnp.int32),
        jnp.full((8, BLOCK), shots[2 * me + 1], jnp.int32),
    ).astype(F32)
    scale = shot / (jnp.sqrt(total / npts + 1e-06) * weight)
    nparams = kernels.shape[0]
    factors = [jnp.broadcast_to(scale[:, p:p + 1], (8, BLOCK)) for p in range(nparams)]
    for n, (out, at, _, _) in enumerate(pieces):
        copies[n].wait()
        for p in range(nparams):
            def one(i, _):
                low = pl.multiple_of(i * 16, 16)
                x = local[n, p, pl.ds(low, 8), :] * factors[p]
                y = local[n, p, pl.ds(low + 8, 8), :] * factors[p]
                x = x + pltpu.roll(x, 7, 0)
                y = y + pltpu.roll(y, 1, 0)
                out[at * nparams + p, pl.ds(pl.multiple_of(i * 8, 8), 8), :] = jnp.where(row % 2 == 0, x, y)
                return 0
            lax.fori_loop(0, span // 16, one, 0, unroll=4)


def weighted(plan, rank, shots, power, kernels, ready, npts, ranges):
    nparams = kernels.shape[0]
    span = kernels.shape[1] // (2 * ranges)
    count = sum(len(parts) for parts in plan)
    return pl.pallas_call(
        functools.partial(scale_kernel, npts, ranges, plan),
        out_shape=[
            jax.ShapeDtypeStruct((nparams * len(parts), span // 2, BLOCK), F32) for parts in plan
        ],
        in_specs=[SMEM, SMEM, VMEM, HBM, ANY],
        out_specs=[VMEM] * len(plan),
        scratch_shapes=[
            pltpu.VMEM((count, nparams, span, BLOCK), F32),
            pltpu.SemaphoreType.DMA((count,)),
        ],
        compiler_params=params(16),
        cost_estimate=cost(3 * kernels.size, 6 * kernels.size),
    )(rank, shots, power, kernels, ready)


def source_rows(x):
    row = rows(x.shape)
    high = x.astype(BF).astype(F32)
    rest = x - high
    low = rest.astype(BF).astype(F32)
    first = jnp.where(row == 7, low, high)
    second = jnp.where(row == 3, rest - low, jnp.where(row == 7, 0.0, low))
    return jnp.concatenate([first, second], axis=0).astype(BF)


def target_rows(x):
    row = rows(x.shape)
    high = x.astype(BF).astype(F32)
    low = x - high
    first = jnp.where(row % 4 == 3, 1.0, jnp.where(row < 4, high, low))
    second = jnp.where(row == 7, 0.0, first)
    return jnp.concatenate([first, second], axis=0).astype(BF)


def field_rows(x):
    high = x.astype(BF).astype(F32)
    return jnp.concatenate([high, x - high], axis=0).astype(BF)


def point(coords, index):
    x = (coords[:, block(index)] - 1.5) * (LOG2E ** 0.5)
    half = -0.5 * jnp.sum(x * x, axis=0, keepdims=True)
    return jnp.concatenate([x, half], axis=0)


def coord_kernel(send, coords, source, out, token):
    token[...] = jnp.zeros_like(token)
    npeer, cap = send.shape
    blocks = coords.shape[1] // BLOCK

    def sources(i, _):
        x = point(coords, i)
        source[i] = source_rows(jnp.concatenate([x, x], axis=0))
        return 0
    lax.fori_loop(0, blocks, sources, 0, unroll=4)

    for group in range(npeer):
        def pick(i, _):
            pair = [point(coords, send[group, 2 * i + k]) for k in range(2)]
            out[group * (cap // 2) + i] = jnp.concatenate(pair, axis=0)
            return 0
        lax.fori_loop(0, cap // 2, pick, 0, unroll=4)


def coord_tables(send, coords):
    blocks = coords.shape[1] // BLOCK
    return pl.pallas_call(
        coord_kernel,
        out_shape=[
            jax.ShapeDtypeStruct((blocks, 16, BLOCK), BF),
            jax.ShapeDtypeStruct((send.size // 2, 8, BLOCK), F32),
            jax.ShapeDtypeStruct((8, BLOCK), F32),
        ],
        in_specs=[SMEM, VMEM],
        out_specs=[VMEM] * 3,
        compiler_params=params(16),
        cost_estimate=cost(coords.size * 30, coords.size * 12),
    )(send, coords)


TURNS = 8


def aim_kernel(rank, order, coords_in, near, sorted_out, coords, target, sem):
    groups, size = near.shape[0], coords.shape[1]
    copy = pltpu.make_async_copy(
        coords_in.at[:, pl.ds(pl.multiple_of(rank[0] * size, size), size)], coords, sem
    )
    copy.start()
    across = lax.broadcasted_iota(jnp.int32, (BLOCK, BLOCK), 1)
    same = jnp.where(rows((BLOCK, BLOCK)) == across, 1.0, 0.0).astype(BF)
    copy.wait()

    def turn(parts):
        x = jnp.concatenate(parts, axis=0)
        return lax.dot_general(same, x, NT, preferred_element_type=F32).astype(BF)

    def natural(i, _):
        parts = []
        for k in range(TURNS):
            x = point(coords, TURNS * i + k)
            parts.append(target_rows(jnp.concatenate([x, x], axis=0)))
            target[TURNS * i + k] = parts[-1]
        near[i] = turn(parts)
        return 0
    lax.fori_loop(0, groups, natural, 0, unroll=2)

    def by_count(i, _):
        sorted_out[i] = turn([target[order[TURNS * i + k]] for k in range(TURNS)])
        return 0
    lax.fori_loop(0, groups, by_count, 0, unroll=4)


def aims(rank, order, coords):
    targets = order.shape[0]
    return pl.pallas_call(
        aim_kernel,
        out_shape=[jax.ShapeDtypeStruct((targets // TURNS, BLOCK, BLOCK), BF)] * 2,
        in_specs=[SMEM, SMEM, HBM],
        out_specs=[VMEM] * 2,
        scratch_shapes=[
            pltpu.VMEM((coords.shape[0], targets * BLOCK), F32),
            pltpu.VMEM((targets, 16, BLOCK), BF),
            pltpu.SemaphoreType.DMA(()),
        ],
        compiler_params=params(16),
        cost_estimate=cost(2 * 10 ** 9, 10 ** 7),
    )(rank, order, held(coords))


def place(index):
    inner = index & 7
    return index - inner + 2 * (inner & 3) + (inner >> 2)


def gather_kernel(rank, send, coords, ready, *rest):
    parts, outs, full, sem = rest[:8], rest[8:-2], rest[-2], rest[-1]
    npeer, cap = send.shape
    copies = []
    for group, out in enumerate(outs):
        copies.append(pltpu.make_async_copy(
            coords.at[pl.ds(group * (cap // 2), cap // 2)],
            out.at[pl.ds(cap, cap // 2)],
            sem.at[group],
        ))
        copies[-1].start()
    half = parts[0].shape[1]
    blocks = 8 * half
    me = rank[0]
    for turn, part in enumerate(parts):
        base = (lax.rem(me + turn // 2, 4) * 2 + turn % 2) * half
        for p in range(7):
            def store(i, _):
                at = pl.multiple_of(i * 8, 8)
                full[pl.ds(pl.multiple_of(p * blocks + base + at, 8), 8), :] = part[p, pl.ds(at, 8), :]
                return 0
            lax.fori_loop(0, half // 8, store, 0, unroll=True)

    def ones(i, _):
        full[pl.ds(pl.multiple_of(7 * blocks + i * 8, 8), 8), :] = jnp.ones((8, BLOCK), F32)
        return 0
    lax.fori_loop(0, blocks // 8, ones, 0, unroll=8)
    for group, out in enumerate(outs):
        def pick(i, _):
            out[i] = full[pl.ds(place(send[group, i]), 8, stride=blocks), :]
            return 0
        lax.fori_loop(0, cap, pick, 0, unroll=8)
    for copy in copies:
        copy.wait()


def gathered(rank, send, coords, ready, parts):
    blocks = 8 * parts[0].shape[1]
    npeer, cap = send.shape
    *sends, full = pl.pallas_call(
        gather_kernel,
        out_shape=[jax.ShapeDtypeStruct((cap + cap // 2, 8, BLOCK), F32)] * npeer
        + [jax.ShapeDtypeStruct((8 * blocks, BLOCK), F32)],
        in_specs=[SMEM, SMEM, VMEM, ANY] + [VMEM] * 8,
        out_specs=[VMEM] * (npeer + 1),
        scratch_shapes=[pltpu.SemaphoreType.DMA((npeer,))],
        compiler_params=params(16),
    )(rank, send, coords, ready, *parts)
    return sends, full


def work_order(lists, counts, none):
    kmax, targets = lists.shape
    slot = jnp.arange(kmax, dtype=jnp.int32)[:, None]
    index = jnp.arange(targets, dtype=jnp.int32)
    key = counts[0] * targets + (targets - 1 - index)
    place_of = jnp.sum((key[None, :] > key[:, None]).astype(jnp.int32), axis=1)
    order = jnp.sum(jnp.where(place_of[:, None] == index[None, :], index[:, None], 0), axis=0)
    above = jnp.arange(kmax, kmax // 2 + 1, -1, dtype=jnp.int32)
    groups = jnp.sum((counts >= above[:, None]).astype(jnp.int32), axis=1)
    bounds = jnp.concatenate([
        (groups + TURNS - 1) // TURNS, jnp.full((1,), targets // TURNS, jnp.int32)
    ])
    return jnp.where(slot < counts, lists, none), order, bounds


def lifted(x, at):
    none = jnp.zeros_like(x)
    return jnp.concatenate([x if turn == at else none for turn in range(TURNS)], axis=0)


def weights(target, coords):
    columns = [lifted(x, at) for at, some in enumerate(coords) for x in some]
    power = jnp.dot(target, jnp.concatenate(columns, axis=1), preferred_element_type=F32)
    weight = jnp.exp2(power)
    high = weight.astype(BF)
    return high, (weight - high.astype(F32)).astype(BF)


def summed(weight, field):
    return lax.dot_general(weight, field, NT, preferred_element_type=F32)


def turned(parts):
    packed = None
    for at, part in enumerate(parts):
        size = part.shape[1]
        wide = jnp.concatenate([part, jnp.zeros((BLOCK, BLOCK - size), F32)], axis=1)
        wide = pltpu.roll(wide, size * at, 1) if at else wide
        packed = wide if packed is None else packed + wide
    return packed.T


def self_kernel(rank, source, target, own_a, own_b, out):
    targets = out.shape[0]
    first = rank[0] * targets
    half = targets // 2
    top = jnp.ones((1, BLOCK), F32)

    for side, own in enumerate((own_a, own_b)):
        def step(i, _):
            base = side * half + TURNS * i
            coords, fields, parts = [], [], []
            for turn in range(TURNS):
                coords.append([source[first + base + turn]])
                x = own[pl.ds(place(TURNS * i + turn), 7, stride=half), :]
                field = lifted(field_rows(jnp.concatenate([x, top], axis=0)), turn)
                fields += [field, field]
            high, low = weights(target[side * (half // TURNS) + i], coords)
            for turn in range(TURNS):
                at = slice(turn * BLOCK, (turn + 1) * BLOCK)
                parts += [high[:, at], low[:, at]]
            total = summed(jnp.concatenate(parts, axis=1), jnp.concatenate(fields, axis=1)).T
            for turn in range(TURNS):
                out[side * half + TURNS * i + turn] = total[16 * turn:16 * turn + 16]
            return 0
        lax.fori_loop(0, half // TURNS, step, 0)


def self_sums(rank, source, target, own_a, own_b):
    targets = target.shape[0] * TURNS
    return pl.pallas_call(
        self_kernel,
        out_shape=jax.ShapeDtypeStruct((targets, 16, BLOCK), F32),
        in_specs=[SMEM] + [VMEM] * 4,
        out_specs=VMEM,
        compiler_params=params(16),
        cost_estimate=cost(5 * 10 ** 9, 10 ** 7),
    )(rank, source, target, own_a.reshape(-1, BLOCK), own_b.reshape(-1, BLOCK))


def smooth_kernel(lists, order, bounds, target, source_in, full, start, *rest):
    parts = rest[:-4]
    out, source, table, sems = rest[-4:]
    blocks, targets = source_in.shape[0], start.shape[0]
    copies = [
        pltpu.make_async_copy(source_in, source.at[pl.ds(0, blocks)], sems.at[0]),
    ]
    for copy in copies:
        copy.start()

    def build(i, _):
        table[i] = field_rows(full[pl.ds(place(i), 8, stride=blocks), :])
        return 0
    lax.fori_loop(0, blocks, build, 0, unroll=8)
    cap = parts[0].shape[0] * 2 // 3
    for group, part in enumerate(parts):
        base = blocks + group * cap

        def coords(i, _):
            x = part[cap + i]
            turned = pltpu.roll(x, 4, 0)
            row = rows(x.shape)
            source[base + 2 * i] = source_rows(jnp.where(row < 4, x, turned))
            source[base + 2 * i + 1] = source_rows(jnp.where(row < 4, turned, x))
            return 0
        lax.fori_loop(0, cap // 2, coords, 0, unroll=4)

        def fields(i, _):
            table[base + i] = field_rows(part[i])
            return 0
        lax.fori_loop(0, cap, fields, 0, unroll=8)
    none = blocks + len(parts) * cap
    source[none] = jnp.zeros((16, BLOCK), BF)
    table[none] = jnp.zeros((16, BLOCK), BF)
    for copy in copies:
        copy.wait()
    kmax = lists.shape[0]

    first = 0
    for part, count in enumerate(range(kmax - 1, kmax // 2 - 1, -1)):
        def step(i, _):
            aims = [order[TURNS * i + turn] for turn in range(TURNS)]
            slots = [[lists[k, b] for k in range(1, 1 + count)] for b in aims]
            high, low = weights(target[i], [[source[s] for s in some] for some in slots])
            parts = []
            for turn, some in enumerate(slots):
                at = slice(turn * count * BLOCK, (turn + 1) * count * BLOCK)
                parts.append(summed(
                    jnp.concatenate([high[:, at], low[:, at]], axis=1),
                    jnp.concatenate([table[s] for s in some] * 2, axis=1),
                ))
            sums = turned(parts)
            for turn, b in enumerate(aims):
                total = sums[16 * turn:16 * turn + 16] + start[b]
                out[:, block(b)] = (total[0:7] + total[8:15]) / total[7:8]
            return 0
        last = bounds[part]
        lax.fori_loop(first, last, step, 0)
        first = last


def smooth(lists, order, bounds, target, source, full, start, parts):
    targets = start.shape[0]
    size = source.shape[0] + len(parts) * (parts[0].shape[0] * 2 // 3) + 1
    return pl.pallas_call(
        smooth_kernel,
        out_shape=jax.ShapeDtypeStruct((7, targets * BLOCK), F32),
        in_specs=[SMEM] * 3 + [VMEM] * 4 + [VMEM] * len(parts),
        out_specs=VMEM,
        scratch_shapes=[
            pltpu.VMEM((size, 16, BLOCK), BF),
            pltpu.VMEM((size, 16, BLOCK), BF),
            pltpu.SemaphoreType.DMA((1,)),
        ],
        compiler_params=params(24),
    )(lists, order, bounds, target, source, full, start, *parts)


def body(kernels, shots, coords, send_list, block_list, block_count):
    slices = lax.axis_size("cuts")
    ranges = lax.axis_size("event")
    events, nparams, points = kernels.shape
    blocks = points // BLOCK
    npeer, cap = send_list.shape[2:]
    targets = block_list.shape[1]
    rank = jnp.reshape(lax.axis_index("event"), (1,)).astype(jnp.int32)
    send = send_list.reshape(npeer, cap)
    kernels = kernels.transpose(1, 0, 2).reshape(nparams, events, blocks, BLOCK)
    kernels = kernels.transpose(0, 2, 1, 3).reshape(nparams, blocks * events, BLOCK)
    kernels = held(kernels)

    power = local_power(kernels, slices)
    coords, power = lax.optimization_barrier((coords, power))
    power = lax.all_to_all(power, "cuts", 0, 0)
    source, near_coord, token = coord_tables(send, coords)
    lists, order, bounds = work_order(block_list[0].T, block_count, blocks + npeer * cap)
    npts = float(points * slices)
    across_a, across_b, ahead_b, behind_a = weighted(
        (((2, 0),), ((2, 1),), ((1, 1),), ((3, 0),)), rank, shots, power, kernels, token, npts, ranges
    )
    from_left = shifted(across_a, "event", 1)
    from_right = shifted(across_b, "event", -1)
    left_b = shifted(ahead_b, "event", 1)
    right_a = shifted(behind_a, "event", -1)
    mine_a, mine_b, ahead_a, behind_b = weighted(
        (((0, 0),), ((0, 1),), ((1, 0),), ((3, 1),)), rank, shots, power, kernels, token, npts, ranges
    )
    from_left, from_right, lists, order, bounds = lax.optimization_barrier(
        (from_left, from_right, lists, order, bounds)
    )
    target, target_by_count = aims(rank, order, coords)
    left_a = shifted(ahead_a + from_left, "event", 1)
    right_b = shifted(behind_b + from_right, "event", -1)
    left_a, right_b, left_b, right_a, target, target_by_count = lax.optimization_barrier(
        (left_a, right_b, left_b, right_a, target, target_by_count)
    )
    own_a = mine_a + left_a + right_a
    own_b = mine_b + right_b + left_b

    left_a = shifted(own_a, "event", 1)
    right_b = shifted(own_b, "event", -1)
    left_b = shifted(own_b, "event", 1)
    right_a = shifted(own_a, "event", -1)
    far_a = shifted(left_a, "event", 1)
    far_b = shifted(right_b, "event", -1)
    start = self_sums(rank, source, target, own_a, own_b)

    sends, full = gathered(
        rank, send, near_coord, start,
        (own_a, own_b, right_a, right_b, far_a, far_b, left_a, left_b),
    )
    parts = [shifted(x, "cuts", OFFSETS[g]) for g, x in enumerate(sends)]
    return smooth(lists, order, bounds, target_by_count, source, full, start, parts)


def solution(mesh):
    placed = (
        P("event", None, "cuts"),
        P(),
        P(None, "cuts"),
        P("cuts", "event", None, None),
        P("cuts", "event", None),
        P("cuts", "event"),
    )
    return jax.shard_map(
        body, mesh=mesh, in_specs=placed, out_specs=P(None, ("cuts", "event")), check_vma=False
    )
```

```python
import functools

import jax
import jax.numpy as jnp
from jax import lax
from jax.experimental import pallas as pl
from jax.experimental.pallas import tpu as pltpu
from jax.sharding import PartitionSpec as P

BLOCK = 128
BF = jnp.bfloat16
F32 = jnp.float32
LOG2E = 1.4426950408889634
NT = (((1,), (1,)), ((), ()))
TN = (((0,), (0,)), ((), ()))
VMEM = pl.BlockSpec(memory_space=pltpu.VMEM)
SMEM = pl.BlockSpec(memory_space=pltpu.SMEM)
ANY = pl.BlockSpec(memory_space=pl.ANY)
HBM = pl.BlockSpec(memory_space=pltpu.HBM)


def params(mib):
    return pltpu.CompilerParams(vmem_limit_bytes=mib << 20)


def cost(flops, moved):
    return pl.CostEstimate(flops=flops, bytes_accessed=moved, transcendentals=0)


def shifted(value, axis, steps):
    count = lax.axis_size(axis)
    pairs = [(source, (source + steps) % count) for source in range(count)]
    return lax.ppermute(value, axis, pairs)


def swapped(value, axis, steps):
    count = lax.axis_size(axis)
    pairs = [(source, (source + (steps if source % 2 == 0 else -steps)) % count) for source in range(count)]
    return lax.ppermute(value, axis, pairs)


def held(x):
    return pltpu.with_memory_space_constraint(x, pltpu.HBM)


def rows(shape):
    return lax.broadcasted_iota(jnp.int32, shape, 0)


def block(index):
    return pl.ds(pl.multiple_of(index * BLOCK, BLOCK), BLOCK)


def power_kernel(kernels, out, local, sems):
    params_here, count = kernels.shape[0], kernels.shape[1] // 8
    copies = [
        pltpu.make_async_copy(kernels.at[p], local.at[p], sems.at[p])
        for p in range(params_here)
    ]
    for copy in copies:
        copy.start()
    lane = lax.broadcasted_iota(jnp.int32, (8, BLOCK), 1)
    tile = jnp.zeros((8, BLOCK), F32)
    for p in range(params_here):
        copies[p].wait()

        def add(i, totals):
            found = []
            for part in range(4):
                x = local[p, pl.ds(pl.multiple_of((i * 4 + part) * 8, 8), 8), :]
                found.append(totals[part] + x * x)
            return tuple(found)
        zero = jnp.zeros((8, BLOCK), F32)
        totals = lax.fori_loop(0, count // 4, add, (zero,) * 4, unroll=4)
        total = (totals[0] + totals[1]) + (totals[2] + totals[3])
        tile = jnp.where(lane == p, jnp.sum(total, axis=1, keepdims=True), tile)
    for peer in range(out.shape[0]):
        out[peer] = tile


def local_power(kernels, peers):
    return pl.pallas_call(
        power_kernel,
        out_shape=jax.ShapeDtypeStruct((peers, 8, BLOCK), F32),
        in_specs=[HBM],
        out_specs=VMEM,
        scratch_shapes=[
            pltpu.VMEM(kernels.shape, F32),
            pltpu.SemaphoreType.DMA((kernels.shape[0],)),
        ],
        compiler_params=params(16),
        cost_estimate=cost(2 * kernels.size, 4 * kernels.size),
    )(kernels)


def scale_kernel(npts, ranges, plan, rank, shots, power, kernels, ready, *rest):
    outs, local, sems = rest[:-2], rest[-2], rest[-1]
    me = rank[0]
    span = local.shape[2]
    pieces = [(out, at, turn, side) for out, parts in zip(outs, plan) for at, (turn, side) in enumerate(parts)]
    copies = []
    for n, (_, _, turn, side) in enumerate(pieces):
        base = pl.multiple_of((lax.rem(me + turn, ranges) * 2 + side) * span, span)
        copies.append(pltpu.make_async_copy(
            kernels.at[:, pl.ds(base, span), :], local.at[n], sems.at[n]
        ))
        copies[-1].start()
    total = jnp.sum(power[...], axis=0)
    total = total + pltpu.roll(total, 2, 0)
    total = total + pltpu.roll(total, 4, 0)
    weight = jnp.int32(0)
    for event in range(shots.shape[0]):
        weight += shots[event]
    weight = jnp.full((8, BLOCK), weight, jnp.int32).astype(F32)
    row = rows((8, BLOCK))
    shot = jnp.where(
        row % 2 == 0,
        jnp.full((8, BLOCK), shots[2 * me], jnp.int32),
        jnp.full((8, BLOCK), shots[2 * me + 1], jnp.int32),
    ).astype(F32)
    scale = shot / (jnp.sqrt(total / npts + 1e-06) * weight)
    nparams = kernels.shape[0]
    factors = [jnp.broadcast_to(scale[:, p:p + 1], (8, BLOCK)) for p in range(nparams)]
    for n, (out, at, _, _) in enumerate(pieces):
        copies[n].wait()
        for p in range(nparams):
            def one(i, _):
                low = pl.multiple_of(i * 16, 16)
                x = local[n, p, pl.ds(low, 8), :] * factors[p]
                y = local[n, p, pl.ds(low + 8, 8), :] * factors[p]
                x = x + pltpu.roll(x, 7, 0)
                y = y + pltpu.roll(y, 1, 0)
                out[at * nparams + p, pl.ds(pl.multiple_of(i * 8, 8), 8), :] = jnp.where(row % 2 == 0, x, y)
                return 0
            lax.fori_loop(0, span // 16, one, 0, unroll=4)


def weighted(plan, rank, shots, power, kernels, ready, npts, ranges):
    nparams = kernels.shape[0]
    span = kernels.shape[1] // (2 * ranges)
    count = sum(len(parts) for parts in plan)
    return pl.pallas_call(
        functools.partial(scale_kernel, npts, ranges, plan),
        out_shape=[
            jax.ShapeDtypeStruct((nparams * len(parts), span // 2, BLOCK), F32) for parts in plan
        ],
        in_specs=[SMEM, SMEM, VMEM, HBM, ANY],
        out_specs=[VMEM] * len(plan),
        scratch_shapes=[
            pltpu.VMEM((count, nparams, span, BLOCK), F32),
            pltpu.SemaphoreType.DMA((count,)),
        ],
        compiler_params=params(16),
        cost_estimate=cost(3 * kernels.size, 6 * kernels.size),
    )(rank, shots, power, kernels, ready)


def source_rows(x):
    row = rows(x.shape)
    high = x.astype(BF).astype(F32)
    rest = x - high
    low = rest.astype(BF).astype(F32)
    first = jnp.where(row == 7, low, high)
    second = jnp.where(row == 3, rest - low, jnp.where(row == 7, 0.0, low))
    return jnp.concatenate([first, second], axis=0).astype(BF)


def target_rows(x):
    row = rows(x.shape)
    high = x.astype(BF).astype(F32)
    low = x - high
    first = jnp.where(row % 4 == 3, 1.0, jnp.where(row < 4, high, low))
    second = jnp.where(row == 7, 0.0, first)
    return jnp.concatenate([first, second], axis=0).astype(BF)


def field_rows(x):
    high = x.astype(BF).astype(F32)
    return jnp.concatenate([high, x - high], axis=0).astype(BF)


def point(coords, index):
    x = (coords[:, block(index)] - 1.5) * (LOG2E ** 0.5)
    half = -0.5 * jnp.sum(x * x, axis=0, keepdims=True)
    return jnp.concatenate([x, half], axis=0)


def coord_kernel(send, coords, source, out, token):
    token[...] = jnp.zeros_like(token)
    npeer, cap = send.shape
    blocks = coords.shape[1] // BLOCK

    def sources(i, _):
        x = point(coords, i)
        source[i] = source_rows(jnp.concatenate([x, x], axis=0))
        return 0
    lax.fori_loop(0, blocks, sources, 0, unroll=4)

    for group in range(npeer):
        def pick(i, _):
            pair = [point(coords, send[group, 2 * i + k]) for k in range(2)]
            out[group * (cap // 2) + i] = jnp.concatenate(pair, axis=0)
            return 0
        lax.fori_loop(0, cap // 2, pick, 0, unroll=4)


def coord_tables(send, coords):
    blocks = coords.shape[1] // BLOCK
    return pl.pallas_call(
        coord_kernel,
        out_shape=[
            jax.ShapeDtypeStruct((blocks, 16, BLOCK), BF),
            jax.ShapeDtypeStruct((send.size // 2, 8, BLOCK), F32),
            jax.ShapeDtypeStruct((8, BLOCK), F32),
        ],
        in_specs=[SMEM, VMEM],
        out_specs=[VMEM] * 3,
        compiler_params=params(16),
        cost_estimate=cost(coords.size * 30, coords.size * 12),
    )(send, coords)


TURNS = 8


def aim_kernel(rank, order, coords_in, near, sorted_out, coords, target, sem):
    groups, size = near.shape[0], coords.shape[1]
    copy = pltpu.make_async_copy(
        coords_in.at[:, pl.ds(pl.multiple_of(rank[0] * size, size), size)], coords, sem
    )
    copy.start()
    across = lax.broadcasted_iota(jnp.int32, (BLOCK, BLOCK), 1)
    same = jnp.where(rows((BLOCK, BLOCK)) == across, 1.0, 0.0).astype(BF)
    copy.wait()

    def turn(parts):
        x = jnp.concatenate(parts, axis=0)
        return lax.dot_general(same, x, NT, preferred_element_type=F32).astype(BF)

    def natural(i, _):
        parts = []
        for k in range(TURNS):
            x = point(coords, TURNS * i + k)
            parts.append(target_rows(jnp.concatenate([x, x], axis=0)))
            target[TURNS * i + k] = parts[-1]
        near[i] = turn(parts)
        return 0
    lax.fori_loop(0, groups, natural, 0, unroll=2)

    def by_count(i, _):
        sorted_out[i] = turn([target[order[TURNS * i + k]] for k in range(TURNS)])
        return 0
    lax.fori_loop(0, groups, by_count, 0, unroll=4)


def aims(rank, order, coords):
    targets = order.shape[0]
    return pl.pallas_call(
        aim_kernel,
        out_shape=[jax.ShapeDtypeStruct((targets // TURNS, BLOCK, BLOCK), BF)] * 2,
        in_specs=[SMEM, SMEM, HBM],
        out_specs=[VMEM] * 2,
        scratch_shapes=[
            pltpu.VMEM((coords.shape[0], targets * BLOCK), F32),
            pltpu.VMEM((targets, 16, BLOCK), BF),
            pltpu.SemaphoreType.DMA(()),
        ],
        compiler_params=params(16),
        cost_estimate=cost(2 * 10 ** 9, 10 ** 7),
    )(rank, order, held(coords))


def place(index):
    inner = index & 7
    return index - inner + 2 * (inner & 3) + (inner >> 2)


def gather_kernel(rank, core, send, coords, ready, *rest):
    parts, (down, up, far, near, full, sem) = rest[:8], rest[8:]
    npeer, cap = send.shape
    side = core[0]
    lot = cap + cap // 2
    plan = (
        (down, 0, 3), (down, lot, 1 + 4 * side), (up, 0, 2), (up, lot, 4 - 4 * side),
        (far, 0, 5 - side), (near, 0, side),
    )
    copies = []
    for at, (out, base, group) in enumerate(plan):
        copies.append(pltpu.make_async_copy(
            coords.at[pl.ds(group * (cap // 2), cap // 2)],
            out.at[pl.ds(base + cap, cap // 2)],
            sem.at[at],
        ))
        copies[-1].start()
    half = parts[0].shape[1]
    blocks = 8 * half
    me = rank[0]
    for turn, part in enumerate(parts):
        base = (lax.rem(me + turn // 2, 4) * 2 + turn % 2) * half
        for p in range(7):
            def store(i, _):
                at = pl.multiple_of(i * 8, 8)
                full[pl.ds(pl.multiple_of(p * blocks + base + at, 8), 8), :] = part[p, pl.ds(at, 8), :]
                return 0
            lax.fori_loop(0, half // 8, store, 0, unroll=True)

    def ones(i, _):
        full[pl.ds(pl.multiple_of(7 * blocks + i * 8, 8), 8), :] = jnp.ones((8, BLOCK), F32)
        return 0
    lax.fori_loop(0, blocks // 8, ones, 0, unroll=8)
    for out, base, group in plan:
        def pick(i, _):
            out[base + i] = full[pl.ds(place(send[group, i]), 8, stride=blocks), :]
            return 0
        lax.fori_loop(0, cap, pick, 0, unroll=8)
    for copy in copies:
        copy.wait()


def gathered(rank, core, send, coords, ready, parts):
    blocks = 8 * parts[0].shape[1]
    npeer, cap = send.shape
    lot = cap + cap // 2
    return pl.pallas_call(
        gather_kernel,
        out_shape=[jax.ShapeDtypeStruct((n * lot, 8, BLOCK), F32) for n in (2, 2, 1, 1)]
        + [jax.ShapeDtypeStruct((8 * blocks, BLOCK), F32)],
        in_specs=[SMEM, SMEM, SMEM, VMEM, ANY] + [VMEM] * 8,
        out_specs=[VMEM] * 5,
        scratch_shapes=[pltpu.SemaphoreType.DMA((npeer,))],
        compiler_params=params(16),
    )(rank, core, send, coords, ready, *parts)


def table_kernel(full, table):
    blocks = table.shape[0]

    def build(i, _):
        table[i] = field_rows(full[pl.ds(place(i), 8, stride=blocks), :])
        return 0
    lax.fori_loop(0, blocks, build, 0, unroll=8)


def local_table(full):
    return pl.pallas_call(
        table_kernel,
        out_shape=jax.ShapeDtypeStruct((full.shape[0] // 8, 16, BLOCK), BF),
        in_specs=[VMEM],
        out_specs=VMEM,
        compiler_params=params(16),
        cost_estimate=cost(2 * 10 ** 9, 10 ** 7),
    )(full)


def work_order(lists, counts, none):
    kmax, targets = lists.shape
    slot = jnp.arange(kmax, dtype=jnp.int32)[:, None]
    index = jnp.arange(targets, dtype=jnp.int32)
    key = counts[0] * targets + (targets - 1 - index)
    place_of = jnp.sum((key[None, :] > key[:, None]).astype(jnp.int32), axis=1)
    order = jnp.sum(jnp.where(place_of[:, None] == index[None, :], index[:, None], 0), axis=0)
    above = jnp.arange(kmax, kmax // 2 + 1, -1, dtype=jnp.int32)
    groups = jnp.sum((counts >= above[:, None]).astype(jnp.int32), axis=1)
    bounds = jnp.concatenate([
        (groups + TURNS - 1) // TURNS, jnp.full((1,), targets // TURNS, jnp.int32)
    ])
    return jnp.where(slot < counts, lists, none), order, bounds


def lifted(x, at):
    none = jnp.zeros_like(x)
    return jnp.concatenate([x if turn == at else none for turn in range(TURNS)], axis=0)


def weights(target, coords):
    columns = [lifted(x, at) for at, some in enumerate(coords) for x in some]
    power = jnp.dot(target, jnp.concatenate(columns, axis=1), preferred_element_type=F32)
    weight = jnp.exp2(power)
    high = weight.astype(BF)
    return high, (weight - high.astype(F32)).astype(BF)


def summed(weight, field):
    return lax.dot_general(weight, field, NT, preferred_element_type=F32)


def turned(parts):
    packed = None
    for at, part in enumerate(parts):
        size = part.shape[1]
        wide = jnp.concatenate([part, jnp.zeros((BLOCK, BLOCK - size), F32)], axis=1)
        wide = pltpu.roll(wide, size * at, 1) if at else wide
        packed = wide if packed is None else packed + wide
    return packed.T


def self_kernel(side, rank, source, target, own, out):
    half = out.shape[0]
    first = (rank[0] * 2 + side) * half
    top = jnp.ones((1, BLOCK), F32)

    def step(i, _):
        coords, fields, parts = [], [], []
        for turn in range(TURNS):
            at = TURNS * i + turn
            coords.append([source[first + at]])
            x = own[pl.ds(place(at), 7, stride=half), :]
            field = lifted(field_rows(jnp.concatenate([x, top], axis=0)), turn)
            fields += [field, field]
        high, low = weights(target[side * (half // TURNS) + i], coords)
        for turn in range(TURNS):
            at = slice(turn * BLOCK, (turn + 1) * BLOCK)
            parts += [high[:, at], low[:, at]]
        total = summed(jnp.concatenate(parts, axis=1), jnp.concatenate(fields, axis=1)).T
        for turn in range(TURNS):
            out[TURNS * i + turn] = total[16 * turn:16 * turn + 16]
        return 0
    lax.fori_loop(0, half // TURNS, step, 0)


def self_sums(side, rank, source, target, own):
    half = own.shape[1]
    return pl.pallas_call(
        functools.partial(self_kernel, side),
        out_shape=jax.ShapeDtypeStruct((half, 16, BLOCK), F32),
        in_specs=[SMEM] + [VMEM] * 3,
        out_specs=VMEM,
        compiler_params=params(16),
        cost_estimate=cost(3 * 10 ** 9, 10 ** 7),
    )(rank, source, target, own.reshape(-1, BLOCK))


def smooth_kernel(core, lists, order, bounds, target, source_in, table_in, first_half, second_half, *rest):
    parts = rest[:-5]
    out, source, table, start, sems = rest[-5:]
    blocks, half = source_in.shape[0], first_half.shape[0]
    copies = [
        pltpu.make_async_copy(source_in, source.at[pl.ds(0, blocks)], sems.at[0]),
        pltpu.make_async_copy(table_in, table.at[pl.ds(0, blocks)], sems.at[1]),
        pltpu.make_async_copy(first_half, start.at[pl.ds(0, half)], sems.at[2]),
        pltpu.make_async_copy(second_half, start.at[pl.ds(half, half)], sems.at[3]),
    ]
    for copy in copies:
        copy.start()
    side = core[0]
    cap = parts[-1].shape[0] * 2 // 3
    groups = (3, 2, 4 + side, 1 - side, 5 - 4 * side, 4 * side)
    for part, group in zip(parts, groups):
        base = blocks + group * cap

        def coords(i, _):
            x = part[cap + i]
            turned = pltpu.roll(x, 4, 0)
            row = rows(x.shape)
            source[base + 2 * i] = source_rows(jnp.where(row < 4, x, turned))
            source[base + 2 * i + 1] = source_rows(jnp.where(row < 4, turned, x))
            return 0
        lax.fori_loop(0, cap // 2, coords, 0, unroll=4)

        def fields(i, _):
            table[base + i] = field_rows(part[i])
            return 0
        lax.fori_loop(0, cap, fields, 0, unroll=8)
    none = blocks + len(parts) * cap
    source[none] = jnp.zeros((16, BLOCK), BF)
    table[none] = jnp.zeros((16, BLOCK), BF)
    for copy in copies:
        copy.wait()
    kmax = lists.shape[0]

    first = 0
    for part, count in enumerate(range(kmax - 1, kmax // 2 - 1, -1)):
        def step(i, _):
            aims = [order[TURNS * i + turn] for turn in range(TURNS)]
            slots = [[lists[k, b] for k in range(1, 1 + count)] for b in aims]
            high, low = weights(target[i], [[source[s] for s in some] for some in slots])
            parts = []
            for turn, some in enumerate(slots):
                at = slice(turn * count * BLOCK, (turn + 1) * count * BLOCK)
                parts.append(summed(
                    jnp.concatenate([high[:, at], low[:, at]], axis=1),
                    jnp.concatenate([table[s] for s in some] * 2, axis=1),
                ))
            sums = turned(parts)
            for turn, b in enumerate(aims):
                total = sums[16 * turn:16 * turn + 16] + start[b]
                out[:, block(b)] = (total[0:7] + total[8:15]) / total[7:8]
            return 0
        last = bounds[part]
        lax.fori_loop(first, last, step, 0)
        first = last


def smooth(core, lists, order, bounds, target, source, table, first_half, second_half, parts):
    targets = order.shape[0]
    size = source.shape[0] + len(parts) * (parts[-1].shape[0] * 2 // 3) + 1
    return pl.pallas_call(
        smooth_kernel,
        out_shape=jax.ShapeDtypeStruct((7, targets * BLOCK), F32),
        in_specs=[SMEM] * 4 + [VMEM] * (5 + len(parts)),
        out_specs=VMEM,
        scratch_shapes=[
            pltpu.VMEM((size, 16, BLOCK), BF),
            pltpu.VMEM((size, 16, BLOCK), BF),
            pltpu.VMEM((targets, 16, BLOCK), F32),
            pltpu.SemaphoreType.DMA((4,)),
        ],
        compiler_params=params(24),
    )(core, lists, order, bounds, target, source, table, first_half, second_half, *parts)


def body(kernels, shots, coords, send_list, block_list, block_count):
    slices = lax.axis_size("cuts")
    ranges = lax.axis_size("event")
    events, nparams, points = kernels.shape
    blocks = points // BLOCK
    npeer, cap = send_list.shape[2:]
    targets = block_list.shape[1]
    rank = jnp.reshape(lax.axis_index("event"), (1,)).astype(jnp.int32)
    core = jnp.reshape(lax.axis_index("cuts") % 2, (1,)).astype(jnp.int32)
    send = send_list.reshape(npeer, cap)
    kernels = kernels.transpose(1, 0, 2).reshape(nparams, events, blocks, BLOCK)
    kernels = kernels.transpose(0, 2, 1, 3).reshape(nparams, blocks * events, BLOCK)
    kernels = held(kernels)

    power = local_power(kernels, slices)
    coords, power = lax.optimization_barrier((coords, power))
    power = lax.all_to_all(power, "cuts", 0, 0)
    source, near_coord, token = coord_tables(send, coords)
    lists, order, bounds = work_order(block_list[0].T, block_count, blocks + npeer * cap)
    npts = float(points * slices)
    across_a, across_b, ahead_b, behind_a = weighted(
        (((2, 0),), ((2, 1),), ((1, 1),), ((3, 0),)), rank, shots, power, kernels, token, npts, ranges
    )
    from_left = shifted(across_a, "event", 1)
    from_right = shifted(across_b, "event", -1)
    left_b = shifted(ahead_b, "event", 1)
    right_a = shifted(behind_a, "event", -1)
    mine_a, mine_b, ahead_a, behind_b = weighted(
        (((0, 0),), ((0, 1),), ((1, 0),), ((3, 1),)), rank, shots, power, kernels, token, npts, ranges
    )
    from_left, from_right, lists, order, bounds = lax.optimization_barrier(
        (from_left, from_right, lists, order, bounds)
    )
    target, target_by_count = aims(rank, order, coords)
    left_a = shifted(ahead_a + from_left, "event", 1)
    right_b = shifted(behind_b + from_right, "event", -1)
    left_a, right_b, left_b, right_a, target, target_by_count = lax.optimization_barrier(
        (left_a, right_b, left_b, right_a, target, target_by_count)
    )
    own_a = mine_a + left_a + right_a
    own_b = mine_b + right_b + left_b

    left_a = shifted(own_a, "event", 1)
    right_b = shifted(own_b, "event", -1)
    left_b = shifted(own_b, "event", 1)
    right_a = shifted(own_a, "event", -1)
    first_half = self_sums(0, rank, source, target, own_a)
    left_a, right_b, first_half = lax.optimization_barrier((left_a, right_b, first_half))
    far_a = shifted(left_a, "event", 1)
    far_b = shifted(right_b, "event", -1)
    second_half = self_sums(1, rank, source, target, own_b)

    down, up, far, near, full = gathered(
        rank, core, send, near_coord, second_half,
        (own_a, own_b, right_a, right_b, far_a, far_b, left_a, left_b),
    )
    lot = near.shape[0]
    near = swapped(near, "cuts", 1)
    down = shifted(down, "cuts", -2)
    up = shifted(up, "cuts", 2)
    far = swapped(far, "cuts", -3)
    table = local_table(full)
    parts = (
        down, up, far, near, swapped(down[lot:], "cuts", 1), swapped(up[lot:], "cuts", 1)
    )
    return smooth(
        core, lists, order, bounds, target_by_count, source, table, first_half, second_half, parts
    )


def solution(mesh):
    placed = (
        P("event", None, "cuts"),
        P(),
        P(None, "cuts"),
        P("cuts", "event", None, None),
        P("cuts", "event", None),
        P("cuts", "event"),
    )
    return jax.shard_map(
        body, mesh=mesh, in_specs=placed, out_specs=P(None, ("cuts", "event")), check_vma=False
    )
```

```python
import functools

import jax
import jax.numpy as jnp
from jax import lax
from jax.experimental import pallas as pl
from jax.experimental.pallas import tpu as pltpu
from jax.sharding import PartitionSpec as P

BLOCK = 128
BF = jnp.bfloat16
F32 = jnp.float32
LOG2E = 1.4426950408889634
NT = (((1,), (1,)), ((), ()))
TN = (((0,), (0,)), ((), ()))
VMEM = pl.BlockSpec(memory_space=pltpu.VMEM)
SMEM = pl.BlockSpec(memory_space=pltpu.SMEM)
ANY = pl.BlockSpec(memory_space=pl.ANY)
HBM = pl.BlockSpec(memory_space=pltpu.HBM)


def params(mib):
    return pltpu.CompilerParams(vmem_limit_bytes=mib << 20)


def cost(flops, moved):
    return pl.CostEstimate(flops=flops, bytes_accessed=moved, transcendentals=0)


def shifted(value, axis, steps):
    count = lax.axis_size(axis)
    pairs = [(source, (source + steps) % count) for source in range(count)]
    return lax.ppermute(value, axis, pairs)


def swapped(value, axis, steps):
    count = lax.axis_size(axis)
    pairs = [(source, (source + (steps if source % 2 == 0 else -steps)) % count) for source in range(count)]
    return lax.ppermute(value, axis, pairs)


def held(x):
    return pltpu.with_memory_space_constraint(x, pltpu.HBM)


def rows(shape):
    return lax.broadcasted_iota(jnp.int32, shape, 0)


def block(index):
    return pl.ds(pl.multiple_of(index * BLOCK, BLOCK), BLOCK)


def power_kernel(kernels, out, local, sems):
    params_here, count = kernels.shape[0], kernels.shape[1] // 8
    copies = [
        pltpu.make_async_copy(kernels.at[p], local.at[p], sems.at[p])
        for p in range(params_here)
    ]
    for copy in copies:
        copy.start()
    lane = lax.broadcasted_iota(jnp.int32, (8, BLOCK), 1)
    tile = jnp.zeros((8, BLOCK), F32)
    for p in range(params_here):
        copies[p].wait()

        def add(i, totals):
            found = []
            for part in range(4):
                x = local[p, pl.ds(pl.multiple_of((i * 4 + part) * 8, 8), 8), :]
                found.append(totals[part] + x * x)
            return tuple(found)
        zero = jnp.zeros((8, BLOCK), F32)
        totals = lax.fori_loop(0, count // 4, add, (zero,) * 4, unroll=4)
        total = (totals[0] + totals[1]) + (totals[2] + totals[3])
        tile = jnp.where(lane == p, jnp.sum(total, axis=1, keepdims=True), tile)
    for peer in range(out.shape[0]):
        out[peer] = tile


def local_power(kernels, peers):
    return pl.pallas_call(
        power_kernel,
        out_shape=jax.ShapeDtypeStruct((peers, 8, BLOCK), F32),
        in_specs=[HBM],
        out_specs=VMEM,
        scratch_shapes=[
            pltpu.VMEM(kernels.shape, F32),
            pltpu.SemaphoreType.DMA((kernels.shape[0],)),
        ],
        compiler_params=params(16),
        cost_estimate=cost(2 * kernels.size, 4 * kernels.size),
    )(kernels)


def scale_kernel(npts, ranges, plan, rank, shots, power, kernels, ready, *rest):
    outs, local, sems = rest[:-2], rest[-2], rest[-1]
    me = rank[0]
    span = local.shape[2]
    pieces = [(out, at, turn, side) for out, parts in zip(outs, plan) for at, (turn, side) in enumerate(parts)]
    copies = []
    for n, (_, _, turn, side) in enumerate(pieces):
        base = pl.multiple_of((lax.rem(me + turn, ranges) * 2 + side) * span, span)
        copies.append(pltpu.make_async_copy(
            kernels.at[:, pl.ds(base, span), :], local.at[n], sems.at[n]
        ))
        copies[-1].start()
    total = jnp.sum(power[...], axis=0)
    total = total + pltpu.roll(total, 2, 0)
    total = total + pltpu.roll(total, 4, 0)
    weight = jnp.int32(0)
    for event in range(shots.shape[0]):
        weight += shots[event]
    weight = jnp.full((8, BLOCK), weight, jnp.int32).astype(F32)
    row = rows((8, BLOCK))
    shot = jnp.where(
        row % 2 == 0,
        jnp.full((8, BLOCK), shots[2 * me], jnp.int32),
        jnp.full((8, BLOCK), shots[2 * me + 1], jnp.int32),
    ).astype(F32)
    scale = shot / (jnp.sqrt(total / npts + 1e-06) * weight)
    nparams = kernels.shape[0]
    factors = [jnp.broadcast_to(scale[:, p:p + 1], (8, BLOCK)) for p in range(nparams)]
    for n, (out, at, _, _) in enumerate(pieces):
        copies[n].wait()
        for p in range(nparams):
            def one(i, _):
                low = pl.multiple_of(i * 16, 16)
                x = local[n, p, pl.ds(low, 8), :] * factors[p]
                y = local[n, p, pl.ds(low + 8, 8), :] * factors[p]
                x = x + pltpu.roll(x, 7, 0)
                y = y + pltpu.roll(y, 1, 0)
                out[at * nparams + p, pl.ds(pl.multiple_of(i * 8, 8), 8), :] = jnp.where(row % 2 == 0, x, y)
                return 0
            lax.fori_loop(0, span // 16, one, 0, unroll=4)


def weighted(plan, rank, shots, power, kernels, ready, npts, ranges):
    nparams = kernels.shape[0]
    span = kernels.shape[1] // (2 * ranges)
    count = sum(len(parts) for parts in plan)
    return pl.pallas_call(
        functools.partial(scale_kernel, npts, ranges, plan),
        out_shape=[
            jax.ShapeDtypeStruct((nparams * len(parts), span // 2, BLOCK), F32) for parts in plan
        ],
        in_specs=[SMEM, SMEM, VMEM, HBM, ANY],
        out_specs=[VMEM] * len(plan),
        scratch_shapes=[
            pltpu.VMEM((count, nparams, span, BLOCK), F32),
            pltpu.SemaphoreType.DMA((count,)),
        ],
        compiler_params=params(16),
        cost_estimate=cost(3 * kernels.size, 6 * kernels.size),
    )(rank, shots, power, kernels, ready)


def source_rows(x):
    row = rows(x.shape)
    high = x.astype(BF).astype(F32)
    rest = x - high
    low = rest.astype(BF).astype(F32)
    first = jnp.where(row == 7, low, high)
    second = jnp.where(row == 3, rest - low, jnp.where(row == 7, 0.0, low))
    return jnp.concatenate([first, second], axis=0).astype(BF)


def target_rows(x):
    row = rows(x.shape)
    high = x.astype(BF).astype(F32)
    low = x - high
    first = jnp.where(row % 4 == 3, 1.0, jnp.where(row < 4, high, low))
    second = jnp.where(row == 7, 0.0, first)
    return jnp.concatenate([first, second], axis=0).astype(BF)


def field_rows(x):
    high = x.astype(BF).astype(F32)
    return jnp.concatenate([high, x - high], axis=0).astype(BF)


def point(coords, index):
    x = (coords[:, block(index)] - 1.5) * (LOG2E ** 0.5)
    half = -0.5 * jnp.sum(x * x, axis=0, keepdims=True)
    return jnp.concatenate([x, half], axis=0)


def coord_kernel(send, coords, source, out, token):
    token[...] = jnp.zeros_like(token)
    npeer, cap = send.shape
    blocks = coords.shape[1] // BLOCK

    def sources(i, _):
        x = point(coords, i)
        source[i] = source_rows(jnp.concatenate([x, x], axis=0))
        return 0
    lax.fori_loop(0, blocks, sources, 0, unroll=4)
    source[blocks] = jnp.zeros((16, BLOCK), BF)

    for group in range(npeer):
        def pick(i, _):
            pair = [point(coords, send[group, 2 * i + k]) for k in range(2)]
            out[group * (cap // 2) + i] = jnp.concatenate(pair, axis=0)
            return 0
        lax.fori_loop(0, cap // 2, pick, 0, unroll=4)


def coord_tables(send, coords):
    blocks = coords.shape[1] // BLOCK
    return pl.pallas_call(
        coord_kernel,
        out_shape=[
            jax.ShapeDtypeStruct((blocks + 1, 16, BLOCK), BF),
            jax.ShapeDtypeStruct((send.size // 2, 8, BLOCK), F32),
            jax.ShapeDtypeStruct((8, BLOCK), F32),
        ],
        in_specs=[SMEM, VMEM],
        out_specs=[VMEM] * 3,
        compiler_params=params(16),
        cost_estimate=cost(coords.size * 30, coords.size * 12),
    )(send, coords)


TURNS = 8


def aim_kernel(rank, near_order, far_order, coords_in, plain, near, far, coords, target, sem):
    groups, size = plain.shape[0], coords.shape[1]
    copy = pltpu.make_async_copy(
        coords_in.at[:, pl.ds(pl.multiple_of(rank[0] * size, size), size)], coords, sem
    )
    copy.start()
    across = lax.broadcasted_iota(jnp.int32, (BLOCK, BLOCK), 1)
    same = jnp.where(rows((BLOCK, BLOCK)) == across, 1.0, 0.0).astype(BF)
    copy.wait()

    def turn(parts):
        x = jnp.concatenate(parts, axis=0)
        return lax.dot_general(same, x, NT, preferred_element_type=F32).astype(BF)

    def natural(i, _):
        parts = []
        for k in range(TURNS):
            x = point(coords, TURNS * i + k)
            parts.append(target_rows(jnp.concatenate([x, x], axis=0)))
            target[TURNS * i + k] = parts[-1]
        plain[i] = turn(parts)
        return 0
    lax.fori_loop(0, groups, natural, 0, unroll=2)

    def by_count(i, _):
        near[i] = turn([target[near_order[TURNS * i + k]] for k in range(TURNS)])
        far[i] = turn([target[far_order[TURNS * i + k]] for k in range(TURNS)])
        return 0
    lax.fori_loop(0, groups, by_count, 0, unroll=4)


def aims(rank, near_order, far_order, coords):
    targets = near_order.shape[0]
    return pl.pallas_call(
        aim_kernel,
        out_shape=[jax.ShapeDtypeStruct((targets // TURNS, BLOCK, BLOCK), BF)] * 3,
        in_specs=[SMEM, SMEM, SMEM, HBM],
        out_specs=[VMEM] * 3,
        scratch_shapes=[
            pltpu.VMEM((coords.shape[0], targets * BLOCK), F32),
            pltpu.VMEM((targets, 16, BLOCK), BF),
            pltpu.SemaphoreType.DMA(()),
        ],
        compiler_params=params(16),
        cost_estimate=cost(2 * 10 ** 9, 10 ** 7),
    )(rank, near_order, far_order, held(coords))


def place(index):
    inner = index & 7
    return index - inner + 2 * (inner & 3) + (inner >> 2)


def gather_kernel(rank, core, send, coords, ready, *rest):
    parts, (down, up, far, near, full, sem) = rest[:8], rest[8:]
    npeer, cap = send.shape
    side = core[0]
    lot = cap + cap // 2
    plan = (
        (down, 0, 3), (down, lot, 1 + 4 * side), (up, 0, 2), (up, lot, 4 - 4 * side),
        (far, 0, 5 - side), (near, 0, side),
    )
    copies = []
    for at, (out, base, group) in enumerate(plan):
        copies.append(pltpu.make_async_copy(
            coords.at[pl.ds(group * (cap // 2), cap // 2)],
            out.at[pl.ds(base + cap, cap // 2)],
            sem.at[at],
        ))
        copies[-1].start()
    half = parts[0].shape[1]
    blocks = 8 * half
    me = rank[0]
    for turn, part in enumerate(parts):
        base = (lax.rem(me + turn // 2, 4) * 2 + turn % 2) * half
        for p in range(7):
            def store(i, _):
                at = pl.multiple_of(i * 8, 8)
                full[pl.ds(pl.multiple_of(p * blocks + base + at, 8), 8), :] = part[p, pl.ds(at, 8), :]
                return 0
            lax.fori_loop(0, half // 8, store, 0, unroll=True)

    def ones(i, _):
        full[pl.ds(pl.multiple_of(7 * blocks + i * 8, 8), 8), :] = jnp.ones((8, BLOCK), F32)
        return 0
    lax.fori_loop(0, blocks // 8, ones, 0, unroll=8)
    for out, base, group in plan:
        def pick(i, _):
            out[base + i] = full[pl.ds(place(send[group, i]), 8, stride=blocks), :]
            return 0
        lax.fori_loop(0, cap, pick, 0, unroll=8)
    for copy in copies:
        copy.wait()


def gathered(rank, core, send, coords, ready, parts):
    blocks = 8 * parts[0].shape[1]
    npeer, cap = send.shape
    lot = cap + cap // 2
    return pl.pallas_call(
        gather_kernel,
        out_shape=[jax.ShapeDtypeStruct((n * lot, 8, BLOCK), F32) for n in (2, 2, 1, 1)]
        + [jax.ShapeDtypeStruct((8 * blocks, BLOCK), F32)],
        in_specs=[SMEM, SMEM, SMEM, VMEM, ANY] + [VMEM] * 8,
        out_specs=[VMEM] * 5,
        scratch_shapes=[pltpu.SemaphoreType.DMA((npeer,))],
        compiler_params=params(16),
    )(rank, core, send, coords, ready, *parts)


def table_kernel(full, table):
    blocks = table.shape[0] - 1
    table[blocks] = jnp.zeros((16, BLOCK), BF)

    def build(i, _):
        table[i] = field_rows(full[pl.ds(place(i), 8, stride=blocks), :])
        return 0
    lax.fori_loop(0, blocks, build, 0, unroll=8)


def local_table(full):
    return pl.pallas_call(
        table_kernel,
        out_shape=jax.ShapeDtypeStruct((full.shape[0] // 8 + 1, 16, BLOCK), BF),
        in_specs=[VMEM],
        out_specs=VMEM,
        compiler_params=params(16),
        cost_estimate=cost(2 * 10 ** 9, 10 ** 7),
    )(full)


SIZES = (7, 5, 4, 3, 2, 1)


def work_order(slots, wanted, none, every):
    kmax, targets = slots.shape
    index = jnp.arange(targets, dtype=jnp.int32)
    found = wanted.astype(jnp.int32)
    position = jnp.cumsum(found, axis=0) - found
    seat = jnp.arange(kmax, dtype=jnp.int32)[:, None, None]
    taken = (position[None] == seat) & wanted[None]
    counts = jnp.sum(found, axis=0)
    lists = jnp.sum(jnp.where(taken, slots[None], 0), axis=1)
    lists = jnp.where(seat[:, 0] < counts, lists, none)
    key = counts * targets + (targets - 1 - index)
    rank = jnp.sum((key[None, :] > key[:, None]).astype(jnp.int32), axis=1)
    order = jnp.sum(jnp.where(rank[:, None] == index[None, :], index[:, None], 0), axis=0)
    above = jnp.array(SIZES[1:] + (-1 if every else 0,), jnp.int32)
    groups = jnp.sum((counts > above[:, None]).astype(jnp.int32), axis=1)
    return lists, order, (groups + TURNS - 1) // TURNS


def lifted(x, at):
    none = jnp.zeros_like(x)
    return jnp.concatenate([x if turn == at else none for turn in range(TURNS)], axis=0)


def weights(target, coords):
    columns = [lifted(x, at) for at, some in enumerate(coords) for x in some]
    power = jnp.dot(target, jnp.concatenate(columns, axis=1), preferred_element_type=F32)
    weight = jnp.exp2(power)
    high = weight.astype(BF)
    return high, (weight - high.astype(F32)).astype(BF)


def summed(weight, field):
    return lax.dot_general(weight, field, NT, preferred_element_type=F32)


def turned(parts):
    packed = None
    for at, part in enumerate(parts):
        size = part.shape[1]
        wide = jnp.concatenate([part, jnp.zeros((BLOCK, BLOCK - size), F32)], axis=1)
        wide = pltpu.roll(wide, size * at, 1) if at else wide
        packed = wide if packed is None else packed + wide
    return packed.T


def self_kernel(side, rank, source, target, own, out):
    half = out.shape[0]
    first = (rank[0] * 2 + side) * half
    top = jnp.ones((1, BLOCK), F32)

    def step(i, _):
        coords, fields, parts = [], [], []
        for turn in range(TURNS):
            at = TURNS * i + turn
            coords.append([source[first + at]])
            x = own[pl.ds(place(at), 7, stride=half), :]
            field = lifted(field_rows(jnp.concatenate([x, top], axis=0)), turn)
            fields += [field, field]
        high, low = weights(target[side * (half // TURNS) + i], coords)
        for turn in range(TURNS):
            at = slice(turn * BLOCK, (turn + 1) * BLOCK)
            parts += [high[:, at], low[:, at]]
        total = summed(jnp.concatenate(parts, axis=1), jnp.concatenate(fields, axis=1)).T
        for turn in range(TURNS):
            out[TURNS * i + turn] = total[16 * turn:16 * turn + 16]
        return 0
    lax.fori_loop(0, half // TURNS, step, 0)


def self_sums(side, rank, source, target, own):
    half = own.shape[1]
    return pl.pallas_call(
        functools.partial(self_kernel, side),
        out_shape=jax.ShapeDtypeStruct((half, 16, BLOCK), F32),
        in_specs=[SMEM] + [VMEM] * 3,
        out_specs=VMEM,
        compiler_params=params(16),
        cost_estimate=cost(3 * 10 ** 9, 10 ** 7),
    )(rank, source, target, own.reshape(-1, BLOCK))


def each_group(lists, order, bounds, target, source, table, use):
    first = 0
    for part, count in enumerate(SIZES):
        def step(i, _):
            chosen = [order[TURNS * i + turn] for turn in range(TURNS)]
            slots = [[lists[k, b] for k in range(count)] for b in chosen]
            high, low = weights(target[i], [[source[s] for s in some] for some in slots])
            parts = []
            for turn, some in enumerate(slots):
                at = slice(turn * count * BLOCK, (turn + 1) * count * BLOCK)
                parts.append(summed(
                    jnp.concatenate([high[:, at], low[:, at]], axis=1),
                    jnp.concatenate([table[s] for s in some] * 2, axis=1),
                ))
            sums = turned(parts)
            for turn, b in enumerate(chosen):
                use(b, sums[16 * turn:16 * turn + 16])
            return 0
        last = bounds[part]
        lax.fori_loop(first, last, step, 0)
        first = last


def near_kernel(lists, order, bounds, target, source, table, first_half, second_half, out):
    half = first_half.shape[0]

    def copy(i, _):
        out[i] = first_half[i]
        out[half + i] = second_half[i]
        return 0
    lax.fori_loop(0, half, copy, 0, unroll=8)

    def use(b, sums):
        out[b] += sums
    each_group(lists, order, bounds, target, source, table, use)


def near_sums(lists, order, bounds, target, source, table, first_half, second_half):
    return pl.pallas_call(
        near_kernel,
        out_shape=jax.ShapeDtypeStruct((order.shape[0], 16, BLOCK), F32),
        in_specs=[SMEM] * 3 + [VMEM] * 5,
        out_specs=VMEM,
        compiler_params=params(16),
        cost_estimate=cost(8 * 10 ** 9, 10 ** 7),
    )(lists, order, bounds, target, source, table, first_half, second_half)


def far_kernel(core, lists, order, bounds, target, start, *rest):
    parts = rest[:-3]
    out, source, table = rest[-3:]
    side = core[0]
    cap = parts[-1].shape[0] * 2 // 3
    groups = (3, 2, 4 + side, 1 - side, 5 - 4 * side, 4 * side)
    for part, group in zip(parts, groups):
        base = group * cap

        def coords(i, _):
            x = part[cap + i]
            turned = pltpu.roll(x, 4, 0)
            row = rows(x.shape)
            source[base + 2 * i] = source_rows(jnp.where(row < 4, x, turned))
            source[base + 2 * i + 1] = source_rows(jnp.where(row < 4, turned, x))
            return 0
        lax.fori_loop(0, cap // 2, coords, 0, unroll=4)

        def fields(i, _):
            table[base + i] = field_rows(part[i])
            return 0
        lax.fori_loop(0, cap, fields, 0, unroll=8)
    none = len(parts) * cap
    source[none] = jnp.zeros((16, BLOCK), BF)
    table[none] = jnp.zeros((16, BLOCK), BF)

    def use(b, sums):
        total = sums + start[b]
        out[:, block(b)] = (total[0:7] + total[8:15]) / total[7:8]
    each_group(lists, order, bounds, target, source, table, use)


def far_sums(core, lists, order, bounds, target, start, parts):
    size = len(parts) * (parts[-1].shape[0] * 2 // 3) + 1
    return pl.pallas_call(
        far_kernel,
        out_shape=jax.ShapeDtypeStruct((7, order.shape[0] * BLOCK), F32),
        in_specs=[SMEM] * 4 + [VMEM] * (2 + len(parts)),
        out_specs=VMEM,
        scratch_shapes=[pltpu.VMEM((size, 16, BLOCK), BF)] * 2,
        compiler_params=params(16),
    )(core, lists, order, bounds, target, start, *parts)


def body(kernels, shots, coords, send_list, block_list, block_count):
    slices = lax.axis_size("cuts")
    ranges = lax.axis_size("event")
    events, nparams, points = kernels.shape
    blocks = points // BLOCK
    npeer, cap = send_list.shape[2:]
    targets = block_list.shape[1]
    rank = jnp.reshape(lax.axis_index("event"), (1,)).astype(jnp.int32)
    core = jnp.reshape(lax.axis_index("cuts") % 2, (1,)).astype(jnp.int32)
    send = send_list.reshape(npeer, cap)
    kernels = kernels.transpose(1, 0, 2).reshape(nparams, events, blocks, BLOCK)
    kernels = kernels.transpose(0, 2, 1, 3).reshape(nparams, blocks * events, BLOCK)
    kernels = held(kernels)

    power = local_power(kernels, slices)
    coords, power = lax.optimization_barrier((coords, power))
    power = lax.all_to_all(power, "cuts", 0, 0)
    source, near_coord, token = coord_tables(send, coords)
    slots = block_list[0].T[1:]
    live = jnp.arange(1, block_list.shape[2], dtype=jnp.int32)[:, None] < block_count
    near_work = work_order(slots, live & (slots < blocks), blocks, False)
    far_work = work_order(slots - blocks, live & (slots >= blocks), npeer * cap, True)
    npts = float(points * slices)
    across_a, across_b, ahead_b, behind_a = weighted(
        (((2, 0),), ((2, 1),), ((1, 1),), ((3, 0),)), rank, shots, power, kernels, token, npts, ranges
    )
    from_left = shifted(across_a, "event", 1)
    from_right = shifted(across_b, "event", -1)
    left_b = shifted(ahead_b, "event", 1)
    right_a = shifted(behind_a, "event", -1)
    mine_a, mine_b, ahead_a, behind_b = weighted(
        (((0, 0),), ((0, 1),), ((1, 0),), ((3, 1),)), rank, shots, power, kernels, token, npts, ranges
    )
    from_left, from_right, near_work, far_work = lax.optimization_barrier(
        (from_left, from_right, near_work, far_work)
    )
    aimed = aims(rank, near_work[1], far_work[1], coords)
    left_a = shifted(ahead_a + from_left, "event", 1)
    right_b = shifted(behind_b + from_right, "event", -1)
    left_a, right_b, left_b, right_a, aimed = lax.optimization_barrier(
        (left_a, right_b, left_b, right_a, aimed)
    )
    target, near_target, far_target = aimed
    own_a = mine_a + left_a + right_a
    own_b = mine_b + right_b + left_b

    left_a = shifted(own_a, "event", 1)
    right_b = shifted(own_b, "event", -1)
    left_b = shifted(own_b, "event", 1)
    right_a = shifted(own_a, "event", -1)
    first_half = self_sums(0, rank, source, target, own_a)
    left_a, right_b, first_half = lax.optimization_barrier((left_a, right_b, first_half))
    far_a = shifted(left_a, "event", 1)
    far_b = shifted(right_b, "event", -1)
    second_half = self_sums(1, rank, source, target, own_b)

    down, up, far, near, full = gathered(
        rank, core, send, near_coord, second_half,
        (own_a, own_b, right_a, right_b, far_a, far_b, left_a, left_b),
    )
    lot = near.shape[0]
    near = swapped(near, "cuts", 1)
    down = shifted(down, "cuts", -2)
    up = shifted(up, "cuts", 2)
    far = swapped(far, "cuts", -3)
    table = local_table(full)
    start = near_sums(*near_work, near_target, source, table, first_half, second_half)
    down, up, start = lax.optimization_barrier((down, up, start))
    parts = (
        down, up, far, near, swapped(down[lot:], "cuts", 1), swapped(up[lot:], "cuts", 1)
    )
    return far_sums(core, *far_work, far_target, start, parts)


def solution(mesh):
    placed = (
        P("event", None, "cuts"),
        P(),
        P(None, "cuts"),
        P("cuts", "event", None, None),
        P("cuts", "event", None),
        P("cuts", "event"),
    )
    return jax.shard_map(
        body, mesh=mesh, in_specs=placed, out_specs=P(None, ("cuts", "event")), check_vma=False
    )
```

```python
import functools

import jax
import jax.numpy as jnp
from jax import lax
from jax.experimental import pallas as pl
from jax.experimental.pallas import tpu as pltpu
from jax.sharding import PartitionSpec as P

BLOCK = 128
BF = jnp.bfloat16
F32 = jnp.float32
LOG2E = 1.4426950408889634
NT = (((1,), (1,)), ((), ()))
TN = (((0,), (0,)), ((), ()))
VMEM = pl.BlockSpec(memory_space=pltpu.VMEM)
SMEM = pl.BlockSpec(memory_space=pltpu.SMEM)
ANY = pl.BlockSpec(memory_space=pl.ANY)
HBM = pl.BlockSpec(memory_space=pltpu.HBM)


def params(mib):
    return pltpu.CompilerParams(vmem_limit_bytes=mib << 20)


def cost(flops, moved):
    return pl.CostEstimate(flops=flops, bytes_accessed=moved, transcendentals=0)


def shifted(value, axis, steps):
    count = lax.axis_size(axis)
    pairs = [(source, (source + steps) % count) for source in range(count)]
    return lax.ppermute(value, axis, pairs)


def swapped(value, axis, steps):
    count = lax.axis_size(axis)
    pairs = [(source, (source + (steps if source % 2 == 0 else -steps)) % count) for source in range(count)]
    return lax.ppermute(value, axis, pairs)


def held(x):
    return pltpu.with_memory_space_constraint(x, pltpu.HBM)


def rows(shape):
    return lax.broadcasted_iota(jnp.int32, shape, 0)


def block(index):
    return pl.ds(pl.multiple_of(index * BLOCK, BLOCK), BLOCK)


def power_kernel(kernels, out, local, sems):
    params_here, count = kernels.shape[0], kernels.shape[1] // 8
    copies = [
        pltpu.make_async_copy(kernels.at[p], local.at[p], sems.at[p])
        for p in range(params_here)
    ]
    for copy in copies:
        copy.start()
    lane = lax.broadcasted_iota(jnp.int32, (8, BLOCK), 1)
    tile = jnp.zeros((8, BLOCK), F32)
    for p in range(params_here):
        copies[p].wait()

        def add(i, totals):
            found = []
            for part in range(4):
                x = local[p, pl.ds(pl.multiple_of((i * 4 + part) * 8, 8), 8), :]
                found.append(totals[part] + x * x)
            return tuple(found)
        zero = jnp.zeros((8, BLOCK), F32)
        totals = lax.fori_loop(0, count // 4, add, (zero,) * 4, unroll=4)
        total = (totals[0] + totals[1]) + (totals[2] + totals[3])
        tile = jnp.where(lane == p, jnp.sum(total, axis=1, keepdims=True), tile)
    for peer in range(out.shape[0]):
        out[peer] = tile


def local_power(kernels, peers):
    return pl.pallas_call(
        power_kernel,
        out_shape=jax.ShapeDtypeStruct((peers, 8, BLOCK), F32),
        in_specs=[HBM],
        out_specs=VMEM,
        scratch_shapes=[
            pltpu.VMEM(kernels.shape, F32),
            pltpu.SemaphoreType.DMA((kernels.shape[0],)),
        ],
        compiler_params=params(16),
        cost_estimate=cost(2 * kernels.size, 4 * kernels.size),
    )(kernels)


def scale_kernel(npts, ranges, plan, rank, shots, power, kernels, ready, *rest):
    outs, local, sems = rest[:-2], rest[-2], rest[-1]
    me = rank[0]
    span = local.shape[2]
    pieces = [(out, at, turn, side) for out, parts in zip(outs, plan) for at, (turn, side) in enumerate(parts)]
    copies = []
    for n, (_, _, turn, side) in enumerate(pieces):
        base = pl.multiple_of((lax.rem(me + turn, ranges) * 2 + side) * span, span)
        copies.append(pltpu.make_async_copy(
            kernels.at[:, pl.ds(base, span), :], local.at[n], sems.at[n]
        ))
        copies[-1].start()
    total = jnp.sum(power[...], axis=0)
    total = total + pltpu.roll(total, 2, 0)
    total = total + pltpu.roll(total, 4, 0)
    weight = jnp.int32(0)
    for event in range(shots.shape[0]):
        weight += shots[event]
    weight = jnp.full((8, BLOCK), weight, jnp.int32).astype(F32)
    row = rows((8, BLOCK))
    shot = jnp.where(
        row % 2 == 0,
        jnp.full((8, BLOCK), shots[2 * me], jnp.int32),
        jnp.full((8, BLOCK), shots[2 * me + 1], jnp.int32),
    ).astype(F32)
    scale = shot / (jnp.sqrt(total / npts + 1e-06) * weight)
    nparams = kernels.shape[0]
    factors = [jnp.broadcast_to(scale[:, p:p + 1], (8, BLOCK)) for p in range(nparams)]
    for n, (out, at, _, _) in enumerate(pieces):
        copies[n].wait()
        for p in range(nparams):
            def one(i, _):
                low = pl.multiple_of(i * 16, 16)
                x = local[n, p, pl.ds(low, 8), :] * factors[p]
                y = local[n, p, pl.ds(low + 8, 8), :] * factors[p]
                x = x + pltpu.roll(x, 7, 0)
                y = y + pltpu.roll(y, 1, 0)
                out[at * nparams + p, pl.ds(pl.multiple_of(i * 8, 8), 8), :] = jnp.where(row % 2 == 0, x, y)
                return 0
            lax.fori_loop(0, span // 16, one, 0, unroll=4)


def weighted(plan, rank, shots, power, kernels, ready, npts, ranges):
    nparams = kernels.shape[0]
    span = kernels.shape[1] // (2 * ranges)
    count = sum(len(parts) for parts in plan)
    return pl.pallas_call(
        functools.partial(scale_kernel, npts, ranges, plan),
        out_shape=[
            jax.ShapeDtypeStruct((nparams * len(parts), span // 2, BLOCK), F32) for parts in plan
        ],
        in_specs=[SMEM, SMEM, VMEM, HBM, ANY],
        out_specs=[VMEM] * len(plan),
        scratch_shapes=[
            pltpu.VMEM((count, nparams, span, BLOCK), F32),
            pltpu.SemaphoreType.DMA((count,)),
        ],
        compiler_params=params(16),
        cost_estimate=cost(3 * kernels.size, 6 * kernels.size),
    )(rank, shots, power, kernels, ready)


def source_rows(x):
    row = rows(x.shape)
    high = x.astype(BF).astype(F32)
    rest = x - high
    low = rest.astype(BF).astype(F32)
    first = jnp.where(row == 7, low, high)
    second = jnp.where(row == 3, rest - low, jnp.where(row == 7, 0.0, low))
    return jnp.concatenate([first, second], axis=0).astype(BF)


def target_rows(x):
    row = rows(x.shape)
    high = x.astype(BF).astype(F32)
    low = x - high
    first = jnp.where(row % 4 == 3, 1.0, jnp.where(row < 4, high, low))
    second = jnp.where(row == 7, 0.0, first)
    return jnp.concatenate([first, second], axis=0).astype(BF)


def field_rows(x):
    high = x.astype(BF).astype(F32)
    return jnp.concatenate([high, x - high], axis=0).astype(BF)


def point(coords, index):
    x = (coords[:, block(index)] - 1.5) * (LOG2E ** 0.5)
    half = -0.5 * jnp.sum(x * x, axis=0, keepdims=True)
    return jnp.concatenate([x, half], axis=0)


def coord_kernel(send, coords, source, out, token):
    token[...] = jnp.zeros_like(token)
    npeer, cap = send.shape
    blocks = coords.shape[1] // BLOCK

    def sources(i, _):
        x = point(coords, i)
        source[i] = source_rows(jnp.concatenate([x, x], axis=0))
        return 0
    lax.fori_loop(0, blocks, sources, 0, unroll=4)
    source[blocks] = jnp.zeros((16, BLOCK), BF)

    for group in range(npeer):
        def pick(i, _):
            pair = [point(coords, send[group, 2 * i + k]) for k in range(2)]
            out[group * (cap // 2) + i] = jnp.concatenate(pair, axis=0)
            return 0
        lax.fori_loop(0, cap // 2, pick, 0, unroll=4)


def coord_tables(send, coords):
    blocks = coords.shape[1] // BLOCK
    return pl.pallas_call(
        coord_kernel,
        out_shape=[
            jax.ShapeDtypeStruct((blocks + 1, 16, BLOCK), BF),
            jax.ShapeDtypeStruct((send.size // 2, 8, BLOCK), F32),
            jax.ShapeDtypeStruct((8, BLOCK), F32),
        ],
        in_specs=[SMEM, VMEM],
        out_specs=[VMEM] * 3,
        compiler_params=params(16),
        cost_estimate=cost(coords.size * 30, coords.size * 12),
    )(send, coords)


TURNS = 8


def aim_kernel(rank, near_order, far_order, coords_in, plain, near, far, coords, target, sem):
    groups, size = plain.shape[0], coords.shape[1]
    copy = pltpu.make_async_copy(
        coords_in.at[:, pl.ds(pl.multiple_of(rank[0] * size, size), size)], coords, sem
    )
    copy.start()
    across = lax.broadcasted_iota(jnp.int32, (BLOCK, BLOCK), 1)
    same = jnp.where(rows((BLOCK, BLOCK)) == across, 1.0, 0.0).astype(BF)
    copy.wait()

    def turn(parts):
        x = jnp.concatenate(parts, axis=0)
        return lax.dot_general(same, x, NT, preferred_element_type=F32).astype(BF)

    def natural(i, _):
        parts = []
        for k in range(TURNS):
            x = point(coords, TURNS * i + k)
            parts.append(target_rows(jnp.concatenate([x, x], axis=0)))
            target[TURNS * i + k] = parts[-1]
        plain[i] = turn(parts)
        return 0
    lax.fori_loop(0, groups, natural, 0, unroll=2)

    def by_count(i, _):
        near[i] = turn([target[near_order[TURNS * i + k]] for k in range(TURNS)])
        far[i] = turn([target[far_order[TURNS * i + k]] for k in range(TURNS)])
        return 0
    lax.fori_loop(0, groups, by_count, 0, unroll=4)


def aims(rank, near_order, far_order, coords):
    targets = near_order.shape[0]
    return pl.pallas_call(
        aim_kernel,
        out_shape=[jax.ShapeDtypeStruct((targets // TURNS, BLOCK, BLOCK), BF)] * 3,
        in_specs=[SMEM, SMEM, SMEM, HBM],
        out_specs=[VMEM] * 3,
        scratch_shapes=[
            pltpu.VMEM((coords.shape[0], targets * BLOCK), F32),
            pltpu.VMEM((targets, 16, BLOCK), BF),
            pltpu.SemaphoreType.DMA(()),
        ],
        compiler_params=params(16),
        cost_estimate=cost(2 * 10 ** 9, 10 ** 7),
    )(rank, near_order, far_order, held(coords))


def place(index):
    inner = index & 7
    return index - inner + 2 * (inner & 3) + (inner >> 2)


def gather_kernel(rank, core, send, coords, ready, *rest):
    parts, (down, up, far, near, full, sem) = rest[:8], rest[8:]
    npeer, cap = send.shape
    side = core[0]
    lot = cap + cap // 2
    plan = (
        (down, 0, 3), (down, lot, 1 + 4 * side), (up, 0, 2), (up, lot, 4 - 4 * side),
        (far, 0, 5 - side), (near, 0, side),
    )
    copies = []
    for at, (out, base, group) in enumerate(plan):
        copies.append(pltpu.make_async_copy(
            coords.at[pl.ds(group * (cap // 2), cap // 2)],
            out.at[pl.ds(base + cap, cap // 2)],
            sem.at[at],
        ))
        copies[-1].start()
    half = parts[0].shape[1]
    blocks = 8 * half
    me = rank[0]
    for turn, part in enumerate(parts):
        base = (lax.rem(me + turn // 2, 4) * 2 + turn % 2) * half
        for p in range(7):
            def store(i, _):
                at = pl.multiple_of(i * 8, 8)
                full[pl.ds(pl.multiple_of(p * blocks + base + at, 8), 8), :] = part[p, pl.ds(at, 8), :]
                return 0
            lax.fori_loop(0, half // 8, store, 0, unroll=True)

    def ones(i, _):
        full[pl.ds(pl.multiple_of(7 * blocks + i * 8, 8), 8), :] = jnp.ones((8, BLOCK), F32)
        return 0
    lax.fori_loop(0, blocks // 8, ones, 0, unroll=8)
    for out, base, group in plan:
        def pick(i, _):
            out[base + i] = full[pl.ds(place(send[group, i]), 8, stride=blocks), :]
            return 0
        lax.fori_loop(0, cap, pick, 0, unroll=8)
    for copy in copies:
        copy.wait()


def gathered(rank, core, send, coords, ready, parts):
    blocks = 8 * parts[0].shape[1]
    npeer, cap = send.shape
    lot = cap + cap // 2
    return pl.pallas_call(
        gather_kernel,
        out_shape=[jax.ShapeDtypeStruct((n * lot, 8, BLOCK), F32) for n in (2, 2, 1, 1)]
        + [jax.ShapeDtypeStruct((8 * blocks, BLOCK), F32)],
        in_specs=[SMEM, SMEM, SMEM, VMEM, ANY] + [VMEM] * 8,
        out_specs=[VMEM] * 5,
        scratch_shapes=[pltpu.SemaphoreType.DMA((npeer,))],
        compiler_params=params(16),
    )(rank, core, send, coords, ready, *parts)


def table_kernel(full, table):
    blocks = table.shape[0] - 1
    table[blocks] = jnp.zeros((16, BLOCK), BF)

    def build(i, _):
        table[i] = field_rows(full[pl.ds(place(i), 8, stride=blocks), :])
        return 0
    lax.fori_loop(0, blocks, build, 0, unroll=8)


def local_table(full):
    return pl.pallas_call(
        table_kernel,
        out_shape=jax.ShapeDtypeStruct((full.shape[0] // 8 + 1, 16, BLOCK), BF),
        in_specs=[VMEM],
        out_specs=VMEM,
        compiler_params=params(16),
        cost_estimate=cost(2 * 10 ** 9, 10 ** 7),
    )(full)


SIZES = (7, 5, 4, 3, 2, 1)


def work_order(slots, wanted, none, every):
    kmax, targets = slots.shape
    index = jnp.arange(targets, dtype=jnp.int32)
    found = wanted.astype(jnp.int32)
    position = jnp.cumsum(found, axis=0) - found
    seat = jnp.arange(kmax, dtype=jnp.int32)[:, None, None]
    taken = (position[None] == seat) & wanted[None]
    counts = jnp.sum(found, axis=0)
    lists = jnp.sum(jnp.where(taken, slots[None], 0), axis=1)
    lists = jnp.where(seat[:, 0] < counts, lists, none)
    key = counts * targets + (targets - 1 - index)
    rank = jnp.sum((key[None, :] > key[:, None]).astype(jnp.int32), axis=1)
    order = jnp.sum(jnp.where(rank[:, None] == index[None, :], index[:, None], 0), axis=0)
    above = jnp.array(SIZES[1:] + (-1 if every else 0,), jnp.int32)
    groups = jnp.sum((counts > above[:, None]).astype(jnp.int32), axis=1)
    return lists, order, (groups + TURNS - 1) // TURNS


def lifted(x, at):
    none = jnp.zeros_like(x)
    return jnp.concatenate([x if turn == at else none for turn in range(TURNS)], axis=0)


def weights(target, coords):
    columns = [lifted(x, at) for at, some in enumerate(coords) for x in some]
    power = jnp.dot(target, jnp.concatenate(columns, axis=1), preferred_element_type=F32)
    weight = jnp.exp2(power)
    high = weight.astype(BF)
    return high, (weight - high.astype(F32)).astype(BF)


def summed(weight, field):
    return lax.dot_general(weight, field, NT, preferred_element_type=F32)


def turned(parts):
    packed = None
    for at, part in enumerate(parts):
        size = part.shape[1]
        wide = jnp.concatenate([part, jnp.zeros((BLOCK, BLOCK - size), F32)], axis=1)
        wide = pltpu.roll(wide, size * at, 1) if at else wide
        packed = wide if packed is None else packed + wide
    return packed.T


def self_kernel(side, rank, source, target, own, out):
    half = out.shape[0]
    first = (rank[0] * 2 + side) * half
    top = jnp.ones((1, BLOCK), F32)

    def group(i):
        coords, fields, parts = [], [], []
        for turn in range(TURNS):
            at = TURNS * i + turn
            coords.append([source[first + at]])
            x = own[pl.ds(place(at), 7, stride=half), :]
            field = lifted(field_rows(jnp.concatenate([x, top], axis=0)), turn)
            fields += [field, field]
        high, low = weights(target[side * (half // TURNS) + i], coords)
        for turn in range(TURNS):
            at = slice(turn * BLOCK, (turn + 1) * BLOCK)
            parts += [high[:, at], low[:, at]]
        return summed(jnp.concatenate(parts, axis=1), jnp.concatenate(fields, axis=1)).T

    lots = 4

    def step(i, _):
        totals = [group(lots * i + lot) for lot in range(lots)]
        for lot, total in enumerate(totals):
            for turn in range(TURNS):
                out[TURNS * (lots * i + lot) + turn] = total[16 * turn:16 * turn + 16]
        return 0
    lax.fori_loop(0, half // TURNS // lots, step, 0)


def self_sums(side, rank, source, target, own):
    half = own.shape[1]
    return pl.pallas_call(
        functools.partial(self_kernel, side),
        out_shape=jax.ShapeDtypeStruct((half, 16, BLOCK), F32),
        in_specs=[SMEM] + [VMEM] * 3,
        out_specs=VMEM,
        compiler_params=params(16),
        cost_estimate=cost(3 * 10 ** 9, 10 ** 7),
    )(rank, source, target, own.reshape(-1, BLOCK))


def each_group(lists, order, bounds, target, source, table, use):
    first = jnp.int32(0)
    for part, count in enumerate(SIZES):
        def group(at):
            chosen = [order[TURNS * at + turn] for turn in range(TURNS)]
            slots = [[lists[k, b] for k in range(count)] for b in chosen]
            high, low = weights(target[at], [[source[s] for s in some] for some in slots])
            parts = []
            for turn, some in enumerate(slots):
                at = slice(turn * count * BLOCK, (turn + 1) * count * BLOCK)
                parts.append(summed(
                    jnp.concatenate([high[:, at], low[:, at]], axis=1),
                    jnp.concatenate([table[s] for s in some] * 2, axis=1),
                ))
            sums = turned(parts)
            return [(b, sums[16 * turn:16 * turn + 16]) for turn, b in enumerate(chosen)]

        shift = 0 if count > 3 else 1

        def step(i, base):
            found = []
            for lot in range(1 << shift):
                found += group(jnp.minimum(base + (i << shift) + lot, target.shape[0] - 1))
            for b, sums in found:
                use(b, sums)
            return base
        steps = jnp.maximum((bounds[part] - first + (1 << shift) - 1) >> shift, 0)
        lax.fori_loop(0, steps, step, first)
        first = first + (steps << shift)


def near_kernel(lists, order, bounds, target, source, table, first_half, second_half, out, start):
    half = first_half.shape[0]

    def copy(i, _):
        for base, part in ((0, first_half), (half, second_half)):
            x = part[i]
            out[base + i] = x
            start[base + i] = x
        return 0
    lax.fori_loop(0, half, copy, 0, unroll=8)

    def use(b, sums):
        out[b] = start[b] + sums
    each_group(lists, order, bounds, target, source, table, use)


def near_sums(lists, order, bounds, target, source, table, first_half, second_half):
    return pl.pallas_call(
        near_kernel,
        out_shape=jax.ShapeDtypeStruct((order.shape[0], 16, BLOCK), F32),
        in_specs=[SMEM] * 3 + [VMEM] * 5,
        out_specs=VMEM,
        scratch_shapes=[pltpu.VMEM((order.shape[0], 16, BLOCK), F32)],
        compiler_params=params(16),
        cost_estimate=cost(8 * 10 ** 9, 10 ** 7),
    )(lists, order, bounds, target, source, table, first_half, second_half)


def far_kernel(core, lists, order, bounds, target, start, *rest):
    parts = rest[:-3]
    out, source, table = rest[-3:]
    side = core[0]
    cap = parts[-1].shape[0] * 2 // 3
    groups = (3, 2, 4 + side, 1 - side, 5 - 4 * side, 4 * side)
    for part, group in zip(parts, groups):
        base = group * cap

        def coords(i, _):
            x = part[cap + i]
            turned = pltpu.roll(x, 4, 0)
            row = rows(x.shape)
            source[base + 2 * i] = source_rows(jnp.where(row < 4, x, turned))
            source[base + 2 * i + 1] = source_rows(jnp.where(row < 4, turned, x))
            return 0
        lax.fori_loop(0, cap // 2, coords, 0, unroll=4)

        def fields(i, _):
            table[base + i] = field_rows(part[i])
            return 0
        lax.fori_loop(0, cap, fields, 0, unroll=8)
    none = len(parts) * cap
    source[none] = jnp.zeros((16, BLOCK), BF)
    table[none] = jnp.zeros((16, BLOCK), BF)

    def use(b, sums):
        total = sums + start[b]
        out[:, block(b)] = (total[0:7] + total[8:15]) / total[7:8]
    each_group(lists, order, bounds, target, source, table, use)


def far_sums(core, lists, order, bounds, target, start, parts):
    size = len(parts) * (parts[-1].shape[0] * 2 // 3) + 1
    return pl.pallas_call(
        far_kernel,
        out_shape=jax.ShapeDtypeStruct((7, order.shape[0] * BLOCK), F32),
        in_specs=[SMEM] * 4 + [VMEM] * (2 + len(parts)),
        out_specs=VMEM,
        scratch_shapes=[pltpu.VMEM((size, 16, BLOCK), BF)] * 2,
        compiler_params=params(16),
    )(core, lists, order, bounds, target, start, *parts)


def body(kernels, shots, coords, send_list, block_list, block_count):
    slices = lax.axis_size("cuts")
    ranges = lax.axis_size("event")
    events, nparams, points = kernels.shape
    blocks = points // BLOCK
    npeer, cap = send_list.shape[2:]
    targets = block_list.shape[1]
    rank = jnp.reshape(lax.axis_index("event"), (1,)).astype(jnp.int32)
    core = jnp.reshape(lax.axis_index("cuts") % 2, (1,)).astype(jnp.int32)
    send = send_list.reshape(npeer, cap)
    kernels = kernels.transpose(1, 0, 2).reshape(nparams, events, blocks, BLOCK)
    kernels = kernels.transpose(0, 2, 1, 3).reshape(nparams, blocks * events, BLOCK)
    kernels = held(kernels)

    power = local_power(kernels, slices)
    coords, power = lax.optimization_barrier((coords, power))
    power = lax.all_to_all(power, "cuts", 0, 0)
    source, near_coord, token = coord_tables(send, coords)
    slots = block_list[0].T[1:]
    live = jnp.arange(1, block_list.shape[2], dtype=jnp.int32)[:, None] < block_count
    near_work = work_order(slots, live & (slots < blocks), blocks, False)
    far_work = work_order(slots - blocks, live & (slots >= blocks), npeer * cap, True)
    npts = float(points * slices)
    across_a, across_b, ahead_b, behind_a = weighted(
        (((2, 0),), ((2, 1),), ((1, 1),), ((3, 0),)), rank, shots, power, kernels, token, npts, ranges
    )
    from_left = shifted(across_a, "event", 1)
    from_right = shifted(across_b, "event", -1)
    left_b = shifted(ahead_b, "event", 1)
    right_a = shifted(behind_a, "event", -1)
    mine_a, mine_b, ahead_a, behind_b = weighted(
        (((0, 0),), ((0, 1),), ((1, 0),), ((3, 1),)), rank, shots, power, kernels, token, npts, ranges
    )
    from_left, from_right, near_work, far_work = lax.optimization_barrier(
        (from_left, from_right, near_work, far_work)
    )
    aimed = aims(rank, near_work[1], far_work[1], coords)
    left_a = shifted(ahead_a + from_left, "event", 1)
    right_b = shifted(behind_b + from_right, "event", -1)
    left_a, right_b, left_b, right_a, aimed = lax.optimization_barrier(
        (left_a, right_b, left_b, right_a, aimed)
    )
    target, near_target, far_target = aimed
    own_a = mine_a + left_a + right_a
    own_b = mine_b + right_b + left_b

    own_a, own_b = lax.optimization_barrier((own_a, own_b))
    left_a = shifted(own_a, "event", 1)
    right_b = shifted(own_b, "event", -1)
    left_b = shifted(own_b, "event", 1)
    right_a = shifted(own_a, "event", -1)
    first_half = self_sums(0, rank, source, target, own_a)
    left_a, right_b, first_half = lax.optimization_barrier((left_a, right_b, first_half))
    far_a = shifted(left_a, "event", 1)
    far_b = shifted(right_b, "event", -1)
    second_half = self_sums(1, rank, source, target, own_b)

    down, up, far, near, full = gathered(
        rank, core, send, near_coord, second_half,
        (own_a, own_b, right_a, right_b, far_a, far_b, left_a, left_b),
    )
    lot = near.shape[0]
    near = swapped(near, "cuts", 1)
    down = shifted(down, "cuts", -2)
    up = shifted(up, "cuts", 2)
    far = swapped(far, "cuts", -3)
    table = local_table(full)
    start = near_sums(*near_work, near_target, source, table, first_half, second_half)
    down, up, start = lax.optimization_barrier((down, up, start))
    parts = (
        down, up, far, near, swapped(down[lot:], "cuts", 1), swapped(up[lot:], "cuts", 1)
    )
    return far_sums(core, *far_work, far_target, start, parts)


def solution(mesh):
    placed = (
        P("event", None, "cuts"),
        P(),
        P(None, "cuts"),
        P("cuts", "event", None, None),
        P("cuts", "event", None),
        P("cuts", "event"),
    )
    return jax.shard_map(
        body, mesh=mesh, in_specs=placed, out_specs=P(None, ("cuts", "event")), check_vma=False
    )
```

```python
import functools

import jax
import jax.numpy as jnp
from jax import lax
from jax.experimental import pallas as pl
from jax.experimental.pallas import tpu as pltpu
from jax.sharding import PartitionSpec as P

BLOCK = 128
BF = jnp.bfloat16
F32 = jnp.float32
LOG2E = 1.4426950408889634
NT = (((1,), (1,)), ((), ()))
TN = (((0,), (0,)), ((), ()))
VMEM = pl.BlockSpec(memory_space=pltpu.VMEM)
SMEM = pl.BlockSpec(memory_space=pltpu.SMEM)
ANY = pl.BlockSpec(memory_space=pl.ANY)
HBM = pl.BlockSpec(memory_space=pltpu.HBM)


def params(mib):
    return pltpu.CompilerParams(vmem_limit_bytes=mib << 20)


def cost(flops, moved):
    return pl.CostEstimate(flops=flops, bytes_accessed=moved, transcendentals=0)


def shifted(value, axis, steps):
    count = lax.axis_size(axis)
    pairs = [(source, (source + steps) % count) for source in range(count)]
    return lax.ppermute(value, axis, pairs)


def swapped(value, axis, steps):
    count = lax.axis_size(axis)
    pairs = [(source, (source + (steps if source % 2 == 0 else -steps)) % count) for source in range(count)]
    return lax.ppermute(value, axis, pairs)


def held(x):
    return pltpu.with_memory_space_constraint(x, pltpu.HBM)


def rows(shape):
    return lax.broadcasted_iota(jnp.int32, shape, 0)


def block(index):
    return pl.ds(pl.multiple_of(index * BLOCK, BLOCK), BLOCK)


def power_kernel(kernels, out, local, sems):
    params_here, count = kernels.shape[0], kernels.shape[1] // 8
    copies = [
        pltpu.make_async_copy(kernels.at[p], local.at[p], sems.at[p])
        for p in range(params_here)
    ]
    for copy in copies:
        copy.start()
    lane = lax.broadcasted_iota(jnp.int32, (8, BLOCK), 1)
    tile = jnp.zeros((8, BLOCK), F32)
    for p in range(params_here):
        copies[p].wait()

        def add(i, totals):
            found = []
            for part in range(4):
                x = local[p, pl.ds(pl.multiple_of((i * 4 + part) * 8, 8), 8), :]
                found.append(totals[part] + x * x)
            return tuple(found)
        zero = jnp.zeros((8, BLOCK), F32)
        totals = lax.fori_loop(0, count // 4, add, (zero,) * 4, unroll=4)
        total = (totals[0] + totals[1]) + (totals[2] + totals[3])
        tile = jnp.where(lane == p, jnp.sum(total, axis=1, keepdims=True), tile)
    for peer in range(out.shape[0]):
        out[peer] = tile


def local_power(kernels, peers):
    return pl.pallas_call(
        power_kernel,
        out_shape=jax.ShapeDtypeStruct((peers, 8, BLOCK), F32),
        in_specs=[HBM],
        out_specs=VMEM,
        scratch_shapes=[
            pltpu.VMEM(kernels.shape, F32),
            pltpu.SemaphoreType.DMA((kernels.shape[0],)),
        ],
        compiler_params=params(16),
        cost_estimate=cost(2 * kernels.size, 4 * kernels.size),
    )(kernels)


def scale_kernel(npts, ranges, plan, rank, shots, power, kernels, ready, *rest):
    outs, local, sems = rest[:-2], rest[-2], rest[-1]
    me = rank[0]
    span = local.shape[2]
    pieces = [(out, at, turn, side) for out, parts in zip(outs, plan) for at, (turn, side) in enumerate(parts)]
    copies = []
    for n, (_, _, turn, side) in enumerate(pieces):
        base = pl.multiple_of((lax.rem(me + turn, ranges) * 2 + side) * span, span)
        copies.append(pltpu.make_async_copy(
            kernels.at[:, pl.ds(base, span), :], local.at[n], sems.at[n]
        ))
        copies[-1].start()
    total = jnp.sum(power[...], axis=0)
    total = total + pltpu.roll(total, 2, 0)
    total = total + pltpu.roll(total, 4, 0)
    weight = jnp.int32(0)
    for event in range(shots.shape[0]):
        weight += shots[event]
    weight = jnp.full((8, BLOCK), weight, jnp.int32).astype(F32)
    row = rows((8, BLOCK))
    shot = jnp.where(
        row % 2 == 0,
        jnp.full((8, BLOCK), shots[2 * me], jnp.int32),
        jnp.full((8, BLOCK), shots[2 * me + 1], jnp.int32),
    ).astype(F32)
    scale = shot / (jnp.sqrt(total / npts + 1e-06) * weight)
    nparams = kernels.shape[0]
    factors = [jnp.broadcast_to(scale[:, p:p + 1], (8, BLOCK)) for p in range(nparams)]
    for n, (out, at, _, _) in enumerate(pieces):
        copies[n].wait()
        for p in range(nparams):
            def one(i, _):
                low = pl.multiple_of(i * 16, 16)
                x = local[n, p, pl.ds(low, 8), :] * factors[p]
                y = local[n, p, pl.ds(low + 8, 8), :] * factors[p]
                x = x + pltpu.roll(x, 7, 0)
                y = y + pltpu.roll(y, 1, 0)
                out[at * nparams + p, pl.ds(pl.multiple_of(i * 8, 8), 8), :] = jnp.where(row % 2 == 0, x, y)
                return 0
            lax.fori_loop(0, span // 16, one, 0, unroll=4)


def weighted(plan, rank, shots, power, kernels, ready, npts, ranges):
    nparams = kernels.shape[0]
    span = kernels.shape[1] // (2 * ranges)
    count = sum(len(parts) for parts in plan)
    return pl.pallas_call(
        functools.partial(scale_kernel, npts, ranges, plan),
        out_shape=[
            jax.ShapeDtypeStruct((nparams * len(parts), span // 2, BLOCK), F32) for parts in plan
        ],
        in_specs=[SMEM, SMEM, VMEM, HBM, ANY],
        out_specs=[VMEM] * len(plan),
        scratch_shapes=[
            pltpu.VMEM((count, nparams, span, BLOCK), F32),
            pltpu.SemaphoreType.DMA((count,)),
        ],
        compiler_params=params(16),
        cost_estimate=cost(3 * kernels.size, 6 * kernels.size),
    )(rank, shots, power, kernels, ready)


def source_rows(x):
    row = rows(x.shape)
    high = x.astype(BF).astype(F32)
    rest = x - high
    low = rest.astype(BF).astype(F32)
    first = jnp.where(row == 7, low, high)
    second = jnp.where(row == 3, rest - low, jnp.where(row == 7, 0.0, low))
    return jnp.concatenate([first, second], axis=0).astype(BF)


def target_rows(x):
    row = rows(x.shape)
    high = x.astype(BF).astype(F32)
    low = x - high
    first = jnp.where(row % 4 == 3, 1.0, jnp.where(row < 4, high, low))
    second = jnp.where(row == 7, 0.0, first)
    return jnp.concatenate([first, second], axis=0).astype(BF)


def field_rows(x):
    high = x.astype(BF).astype(F32)
    return jnp.concatenate([high, x - high], axis=0).astype(BF)


def point(coords, index):
    x = (coords[:, block(index)] - 1.5) * (LOG2E ** 0.5)
    half = -0.5 * jnp.sum(x * x, axis=0, keepdims=True)
    return jnp.concatenate([x, half], axis=0)


def coord_kernel(send, coords, source, out, token):
    token[...] = jnp.zeros_like(token)
    npeer, cap = send.shape
    blocks = coords.shape[1] // BLOCK

    def sources(i, _):
        x = point(coords, i)
        source[i] = source_rows(jnp.concatenate([x, x], axis=0))
        return 0
    lax.fori_loop(0, blocks, sources, 0, unroll=4)
    source[blocks] = jnp.zeros((16, BLOCK), BF)

    for group in range(npeer):
        def pick(i, _):
            pair = [point(coords, send[group, 2 * i + k]) for k in range(2)]
            out[group * (cap // 2) + i] = jnp.concatenate(pair, axis=0)
            return 0
        lax.fori_loop(0, cap // 2, pick, 0, unroll=4)


def coord_tables(send, coords):
    blocks = coords.shape[1] // BLOCK
    return pl.pallas_call(
        coord_kernel,
        out_shape=[
            jax.ShapeDtypeStruct((blocks + 1, 16, BLOCK), BF),
            jax.ShapeDtypeStruct((send.size // 2, 8, BLOCK), F32),
            jax.ShapeDtypeStruct((8, BLOCK), F32),
        ],
        in_specs=[SMEM, VMEM],
        out_specs=[VMEM] * 3,
        compiler_params=params(16),
        cost_estimate=cost(coords.size * 30, coords.size * 12),
    )(send, coords)


TURNS = 8


def aim_kernel(rank, near_order, far_order, coords_in, plain, near, far, coords, target, sem):
    groups, size = plain.shape[0], coords.shape[1]
    copy = pltpu.make_async_copy(
        coords_in.at[:, pl.ds(pl.multiple_of(rank[0] * size, size), size)], coords, sem
    )
    copy.start()
    across = lax.broadcasted_iota(jnp.int32, (BLOCK, BLOCK), 1)
    same = jnp.where(rows((BLOCK, BLOCK)) == across, 1.0, 0.0).astype(BF)
    copy.wait()

    def turn(parts):
        x = jnp.concatenate(parts, axis=0)
        return lax.dot_general(same, x, NT, preferred_element_type=F32).astype(BF)

    def natural(i, _):
        parts = []
        for k in range(TURNS):
            x = point(coords, TURNS * i + k)
            parts.append(target_rows(jnp.concatenate([x, x], axis=0)))
            target[TURNS * i + k] = parts[-1]
        plain[i] = turn(parts)
        return 0
    lax.fori_loop(0, groups, natural, 0, unroll=2)

    def by_count(i, _):
        near[i] = turn([target[near_order[TURNS * i + k]] for k in range(TURNS)])
        far[i] = turn([target[far_order[TURNS * i + k]] for k in range(TURNS)])
        return 0
    lax.fori_loop(0, groups, by_count, 0, unroll=4)


def aims(rank, near_order, far_order, coords):
    targets = near_order.shape[0]
    return pl.pallas_call(
        aim_kernel,
        out_shape=[jax.ShapeDtypeStruct((targets // TURNS, BLOCK, BLOCK), BF)] * 3,
        in_specs=[SMEM, SMEM, SMEM, HBM],
        out_specs=[VMEM] * 3,
        scratch_shapes=[
            pltpu.VMEM((coords.shape[0], targets * BLOCK), F32),
            pltpu.VMEM((targets, 16, BLOCK), BF),
            pltpu.SemaphoreType.DMA(()),
        ],
        compiler_params=params(16),
        cost_estimate=cost(2 * 10 ** 9, 10 ** 7),
    )(rank, near_order, far_order, held(coords))


def place(index):
    inner = index & 7
    return index - inner + 2 * (inner & 3) + (inner >> 2)


def gather_kernel(rank, core, send, coords, ready, *rest):
    parts, (down, up, far, near, full, sem) = rest[:8], rest[8:]
    npeer, cap = send.shape
    side = core[0]
    lot = cap + cap // 2
    plan = (
        (down, 0, 3), (down, lot, 1 + 4 * side), (up, 0, 2), (up, lot, 4 - 4 * side),
        (far, 0, 5 - side), (near, 0, side),
    )
    copies = []
    for at, (out, base, group) in enumerate(plan):
        copies.append(pltpu.make_async_copy(
            coords.at[pl.ds(group * (cap // 2), cap // 2)],
            out.at[pl.ds(base + cap, cap // 2)],
            sem.at[at],
        ))
        copies[-1].start()
    half = parts[0].shape[1]
    blocks = 8 * half
    me = rank[0]
    for turn, part in enumerate(parts):
        base = (lax.rem(me + turn // 2, 4) * 2 + turn % 2) * half
        for p in range(7):
            def store(i, _):
                at = pl.multiple_of(i * 8, 8)
                full[pl.ds(pl.multiple_of(p * blocks + base + at, 8), 8), :] = part[p, pl.ds(at, 8), :]
                return 0
            lax.fori_loop(0, half // 8, store, 0, unroll=True)

    def ones(i, _):
        full[pl.ds(pl.multiple_of(7 * blocks + i * 8, 8), 8), :] = jnp.ones((8, BLOCK), F32)
        return 0
    lax.fori_loop(0, blocks // 8, ones, 0, unroll=8)
    for out, base, group in plan:
        def pick(i, _):
            out[base + i] = full[pl.ds(place(send[group, i]), 8, stride=blocks), :]
            return 0
        lax.fori_loop(0, cap, pick, 0, unroll=8)
    for copy in copies:
        copy.wait()


def gathered(rank, core, send, coords, ready, parts):
    blocks = 8 * parts[0].shape[1]
    npeer, cap = send.shape
    lot = cap + cap // 2
    return pl.pallas_call(
        gather_kernel,
        out_shape=[jax.ShapeDtypeStruct((n * lot, 8, BLOCK), F32) for n in (2, 2, 1, 1)]
        + [jax.ShapeDtypeStruct((8 * blocks, BLOCK), F32)],
        in_specs=[SMEM, SMEM, SMEM, VMEM, ANY] + [VMEM] * 8,
        out_specs=[VMEM] * 5,
        scratch_shapes=[pltpu.SemaphoreType.DMA((npeer,))],
        compiler_params=params(16),
    )(rank, core, send, coords, ready, *parts)


def table_kernel(full, table):
    blocks = table.shape[0] - 1
    table[blocks] = jnp.zeros((16, BLOCK), BF)

    def build(i, _):
        table[i] = field_rows(full[pl.ds(place(i), 8, stride=blocks), :])
        return 0
    lax.fori_loop(0, blocks, build, 0, unroll=8)


def local_table(full):
    return pl.pallas_call(
        table_kernel,
        out_shape=jax.ShapeDtypeStruct((full.shape[0] // 8 + 1, 16, BLOCK), BF),
        in_specs=[VMEM],
        out_specs=VMEM,
        compiler_params=params(16),
        cost_estimate=cost(2 * 10 ** 9, 10 ** 7),
    )(full)


SIZES = (7, 5, 4, 3, 2, 1)


def work_order(slots, wanted, none, every):
    kmax, targets = slots.shape
    index = jnp.arange(targets, dtype=jnp.int32)
    found = wanted.astype(jnp.int32)
    position = jnp.cumsum(found, axis=0) - found
    seat = jnp.arange(kmax, dtype=jnp.int32)[:, None, None]
    taken = (position[None] == seat) & wanted[None]
    counts = jnp.sum(found, axis=0)
    lists = jnp.sum(jnp.where(taken, slots[None], 0), axis=1)
    lists = jnp.where(seat[:, 0] < counts, lists, none)
    key = counts * targets + (targets - 1 - index)
    rank = jnp.sum((key[None, :] > key[:, None]).astype(jnp.int32), axis=1)
    order = jnp.sum(jnp.where(rank[:, None] == index[None, :], index[:, None], 0), axis=0)
    above = jnp.array(SIZES[1:] + (-1 if every else 0,), jnp.int32)
    groups = jnp.sum((counts > above[:, None]).astype(jnp.int32), axis=1)
    return lists, order, (groups + TURNS - 1) // TURNS


def lifted(x, at):
    none = jnp.zeros_like(x)
    return jnp.concatenate([x if turn == at else none for turn in range(TURNS)], axis=0)


def weights(target, coords):
    columns = [lifted(x, at) for at, some in enumerate(coords) for x in some]
    power = jnp.dot(target, jnp.concatenate(columns, axis=1), preferred_element_type=F32)
    weight = jnp.exp2(power)
    high = weight.astype(BF)
    return high, (weight - high.astype(F32)).astype(BF)


def summed(weight, field):
    return lax.dot_general(weight, field, NT, preferred_element_type=F32)


def turned(parts):
    packed = None
    for at, part in enumerate(parts):
        size = part.shape[1]
        wide = jnp.concatenate([part, jnp.zeros((BLOCK, BLOCK - size), F32)], axis=1)
        wide = pltpu.roll(wide, size * at, 1) if at else wide
        packed = wide if packed is None else packed + wide
    return packed.T


def self_kernel(side, rank, source, target, own, out):
    half = out.shape[0]
    first = (rank[0] * 2 + side) * half
    top = jnp.ones((1, BLOCK), F32)

    def group(i):
        coords, fields, parts = [], [], []
        for turn in range(TURNS):
            at = TURNS * i + turn
            coords.append([source[first + at]])
            x = own[pl.ds(place(at), 7, stride=half), :]
            field = lifted(field_rows(jnp.concatenate([x, top], axis=0)), turn)
            fields += [field, field]
        high, low = weights(target[side * (half // TURNS) + i], coords)
        for turn in range(TURNS):
            at = slice(turn * BLOCK, (turn + 1) * BLOCK)
            parts += [high[:, at], low[:, at]]
        return summed(jnp.concatenate(parts, axis=1), jnp.concatenate(fields, axis=1)).T

    lots = 4

    def step(i, _):
        totals = [group(lots * i + lot) for lot in range(lots)]
        for lot, total in enumerate(totals):
            for turn in range(TURNS):
                out[TURNS * (lots * i + lot) + turn] = total[16 * turn:16 * turn + 16]
        return 0
    lax.fori_loop(0, half // TURNS // lots, step, 0)


def self_sums(side, rank, source, target, own):
    half = own.shape[1]
    return pl.pallas_call(
        functools.partial(self_kernel, side),
        out_shape=jax.ShapeDtypeStruct((half, 16, BLOCK), F32),
        in_specs=[SMEM] + [VMEM] * 3,
        out_specs=VMEM,
        compiler_params=params(16),
        cost_estimate=cost(3 * 10 ** 9, 10 ** 7),
    )(rank, source, target, own.reshape(-1, BLOCK))


def each_group(lists, order, bounds, target, source, table, use):
    first = jnp.int32(0)
    for part, count in enumerate(SIZES):
        def group(at):
            chosen = [order[TURNS * at + turn] for turn in range(TURNS)]
            slots = [[lists[k, b] for k in range(count)] for b in chosen]
            high, low = weights(target[at], [[source[s] for s in some] for some in slots])
            parts = []
            for turn, some in enumerate(slots):
                at = slice(turn * count * BLOCK, (turn + 1) * count * BLOCK)
                parts.append(summed(
                    jnp.concatenate([high[:, at], low[:, at]], axis=1),
                    jnp.concatenate([table[s] for s in some] * 2, axis=1),
                ))
            sums = turned(parts)
            return [(b, sums[16 * turn:16 * turn + 16]) for turn, b in enumerate(chosen)]

        shift = 0 if count > 3 else 1

        def step(i, base):
            found = []
            for lot in range(1 << shift):
                found += group(jnp.minimum(base + (i << shift) + lot, target.shape[0] - 1))
            for b, sums in found:
                use(b, sums)
            return base
        steps = jnp.maximum((bounds[part] - first + (1 << shift) - 1) >> shift, 0)
        lax.fori_loop(0, steps, step, first)
        first = first + (steps << shift)


def near_kernel(lists, order, bounds, target, source, table, first_half, second_half, out, start):
    half = first_half.shape[0]

    def copy(i, _):
        for base, part in ((0, first_half), (half, second_half)):
            x = part[i]
            out[base + i] = x
            start[base + i] = x
        return 0
    lax.fori_loop(0, half, copy, 0, unroll=8)

    def use(b, sums):
        out[b] = start[b] + sums
    each_group(lists, order, bounds, target, source, table, use)


def near_sums(lists, order, bounds, target, source, table, first_half, second_half):
    return pl.pallas_call(
        near_kernel,
        out_shape=jax.ShapeDtypeStruct((order.shape[0], 16, BLOCK), F32),
        in_specs=[SMEM] * 3 + [VMEM] * 5,
        out_specs=VMEM,
        scratch_shapes=[pltpu.VMEM((order.shape[0], 16, BLOCK), F32)],
        compiler_params=params(16),
        cost_estimate=cost(8 * 10 ** 9, 10 ** 7),
    )(lists, order, bounds, target, source, table, first_half, second_half)


def far_kernel(core, lists, order, bounds, target, start, *rest):
    parts = rest[:-3]
    out, source, table = rest[-3:]
    side = core[0]
    cap = parts[-1].shape[0] * 2 // 3
    groups = (3, 2, 4 + side, 1 - side, 5 - 4 * side, 4 * side)
    for part, group in zip(parts, groups):
        base = group * cap

        def coords(i, _):
            x = part[cap + i]
            turned = pltpu.roll(x, 4, 0)
            row = rows(x.shape)
            source[base + 2 * i] = source_rows(jnp.where(row < 4, x, turned))
            source[base + 2 * i + 1] = source_rows(jnp.where(row < 4, turned, x))
            return 0
        lax.fori_loop(0, cap // 2, coords, 0, unroll=4)

        def fields(i, _):
            table[base + i] = field_rows(part[i])
            return 0
        lax.fori_loop(0, cap, fields, 0, unroll=8)
    none = len(parts) * cap
    source[none] = jnp.zeros((16, BLOCK), BF)
    table[none] = jnp.zeros((16, BLOCK), BF)

    def use(b, sums):
        total = sums + start[b]
        out[:, block(b)] = (total[0:7] + total[8:15]) / total[7:8]
    each_group(lists, order, bounds, target, source, table, use)


def far_sums(core, lists, order, bounds, target, start, parts):
    size = len(parts) * (parts[-1].shape[0] * 2 // 3) + 1
    return pl.pallas_call(
        far_kernel,
        out_shape=jax.ShapeDtypeStruct((7, order.shape[0] * BLOCK), F32),
        in_specs=[SMEM] * 4 + [VMEM] * (2 + len(parts)),
        out_specs=VMEM,
        scratch_shapes=[pltpu.VMEM((size, 16, BLOCK), BF)] * 2,
        compiler_params=params(16),
    )(core, lists, order, bounds, target, start, *parts)


def body(kernels, shots, coords, send_list, block_list, block_count):
    slices = lax.axis_size("cuts")
    ranges = lax.axis_size("event")
    events, nparams, points = kernels.shape
    blocks = points // BLOCK
    npeer, cap = send_list.shape[2:]
    targets = block_list.shape[1]
    rank = jnp.reshape(lax.axis_index("event"), (1,)).astype(jnp.int32)
    core = jnp.reshape(lax.axis_index("cuts") % 2, (1,)).astype(jnp.int32)
    send = send_list.reshape(npeer, cap)
    kernels = kernels.transpose(1, 0, 2).reshape(nparams, events, blocks, BLOCK)
    kernels = kernels.transpose(0, 2, 1, 3).reshape(nparams, blocks * events, BLOCK)
    kernels = held(kernels)

    power = local_power(kernels, slices)
    coords, power = lax.optimization_barrier((coords, power))
    power = lax.all_to_all(power, "cuts", 0, 0)
    source, near_coord, token = coord_tables(send, coords)
    slots = block_list[0].T[1:]
    live = jnp.arange(1, block_list.shape[2], dtype=jnp.int32)[:, None] < block_count
    near_work = work_order(slots, live & (slots < blocks), blocks, False)
    far_work = work_order(slots - blocks, live & (slots >= blocks), npeer * cap, True)
    npts = float(points * slices)
    across_a, across_b, ahead_b, behind_a = weighted(
        (((2, 0),), ((2, 1),), ((1, 1),), ((3, 0),)), rank, shots, power, kernels, token, npts, ranges
    )
    from_left = shifted(across_a, "event", 1)
    from_right = shifted(across_b, "event", -1)
    left_b = shifted(ahead_b, "event", 1)
    right_a = shifted(behind_a, "event", -1)
    mine_a, mine_b, ahead_a, behind_b = weighted(
        (((0, 0),), ((0, 1),), ((1, 0),), ((3, 1),)), rank, shots, power, kernels, token, npts, ranges
    )
    from_left, from_right, near_work, far_work = lax.optimization_barrier(
        (from_left, from_right, near_work, far_work)
    )
    aimed = aims(rank, near_work[1], far_work[1], coords)
    left_a = shifted(ahead_a + from_left, "event", 1)
    right_b = shifted(behind_b + from_right, "event", -1)
    left_a, right_b, left_b, right_a, aimed = lax.optimization_barrier(
        (left_a, right_b, left_b, right_a, aimed)
    )
    target, near_target, far_target = aimed
    own_a = mine_a + left_a + right_a
    own_b = mine_b + right_b + left_b

    left_a = shifted(own_a, "event", 1)
    right_b = shifted(own_b, "event", -1)
    first_half = self_sums(0, rank, source, target, own_a)
    second_half = self_sums(1, rank, source, target, own_b)
    left_a, right_b, own_a, own_b, first_half, second_half = lax.optimization_barrier(
        (left_a, right_b, own_a, own_b, first_half, second_half)
    )
    far_a = shifted(left_a, "event", 1)
    far_b = shifted(right_b, "event", -1)
    left_b = shifted(own_b, "event", 1)
    right_a = shifted(own_a, "event", -1)

    down, up, far, near, full = gathered(
        rank, core, send, near_coord, second_half,
        (own_a, own_b, right_a, right_b, far_a, far_b, left_a, left_b),
    )
    lot = near.shape[0]
    near = swapped(near, "cuts", 1)
    down = shifted(down, "cuts", -2)
    up = shifted(up, "cuts", 2)
    far = swapped(far, "cuts", -3)
    table = local_table(full)
    start = near_sums(*near_work, near_target, source, table, first_half, second_half)
    down, up, start = lax.optimization_barrier((down, up, start))
    parts = (
        down, up, far, near, swapped(down[lot:], "cuts", 1), swapped(up[lot:], "cuts", 1)
    )
    return far_sums(core, *far_work, far_target, start, parts)


def solution(mesh):
    placed = (
        P("event", None, "cuts"),
        P(),
        P(None, "cuts"),
        P("cuts", "event", None, None),
        P("cuts", "event", None),
        P("cuts", "event"),
    )
    return jax.shard_map(
        body, mesh=mesh, in_specs=placed, out_specs=P(None, ("cuts", "event")), check_vma=False
    )
```

```python
import functools

import jax
import jax.numpy as jnp
from jax import lax
from jax.experimental import pallas as pl
from jax.experimental.pallas import tpu as pltpu
from jax.sharding import PartitionSpec as P

BLOCK = 128
BF = jnp.bfloat16
F32 = jnp.float32
LOG2E = 1.4426950408889634
NT = (((1,), (1,)), ((), ()))
TN = (((0,), (0,)), ((), ()))
VMEM = pl.BlockSpec(memory_space=pltpu.VMEM)
SMEM = pl.BlockSpec(memory_space=pltpu.SMEM)
ANY = pl.BlockSpec(memory_space=pl.ANY)
HBM = pl.BlockSpec(memory_space=pltpu.HBM)


def params(mib):
    return pltpu.CompilerParams(vmem_limit_bytes=mib << 20)


def cost(flops, moved):
    return pl.CostEstimate(flops=flops, bytes_accessed=moved, transcendentals=0)


def shifted(value, axis, steps):
    count = lax.axis_size(axis)
    pairs = [(source, (source + steps) % count) for source in range(count)]
    return lax.ppermute(value, axis, pairs)


def swapped(value, axis, steps):
    count = lax.axis_size(axis)
    pairs = [(source, (source + (steps if source % 2 == 0 else -steps)) % count) for source in range(count)]
    return lax.ppermute(value, axis, pairs)


def held(x):
    return pltpu.with_memory_space_constraint(x, pltpu.HBM)


def rows(shape):
    return lax.broadcasted_iota(jnp.int32, shape, 0)


def block(index):
    return pl.ds(pl.multiple_of(index * BLOCK, BLOCK), BLOCK)


def power_kernel(kernels, out, local, sems):
    params_here, count = kernels.shape[0], kernels.shape[1] // 8
    copies = [
        pltpu.make_async_copy(kernels.at[p], local.at[p], sems.at[p])
        for p in range(params_here)
    ]
    for copy in copies:
        copy.start()
    lane = lax.broadcasted_iota(jnp.int32, (8, BLOCK), 1)
    tile = jnp.zeros((8, BLOCK), F32)
    for p in range(params_here):
        copies[p].wait()

        def add(i, totals):
            found = []
            for part in range(4):
                x = local[p, pl.ds(pl.multiple_of((i * 4 + part) * 8, 8), 8), :]
                found.append(totals[part] + x * x)
            return tuple(found)
        zero = jnp.zeros((8, BLOCK), F32)
        totals = lax.fori_loop(0, count // 4, add, (zero,) * 4, unroll=4)
        total = (totals[0] + totals[1]) + (totals[2] + totals[3])
        tile = jnp.where(lane == p, jnp.sum(total, axis=1, keepdims=True), tile)
    for peer in range(out.shape[0]):
        out[peer] = tile


def local_power(kernels, peers):
    return pl.pallas_call(
        power_kernel,
        out_shape=[
            jax.ShapeDtypeStruct((peers, 8, BLOCK), F32),
            jax.ShapeDtypeStruct(kernels.shape, F32),
        ],
        in_specs=[HBM],
        out_specs=[VMEM] * 2,
        scratch_shapes=[pltpu.SemaphoreType.DMA((kernels.shape[0],))],
        compiler_params=params(16),
        cost_estimate=cost(2 * kernels.size, 4 * kernels.size),
    )(kernels)


def scale_kernel(npts, ranges, plan, rank, shots, power, kernels, ready, *rest):
    outs = rest
    me = rank[0]
    span = kernels.shape[1] // (2 * ranges)
    pieces = [(out, at, turn, side) for out, parts in zip(outs, plan) for at, (turn, side) in enumerate(parts)]
    total = jnp.sum(power[...], axis=0)
    total = total + pltpu.roll(total, 2, 0)
    total = total + pltpu.roll(total, 4, 0)
    weight = jnp.int32(0)
    for event in range(shots.shape[0]):
        weight += shots[event]
    weight = jnp.full((8, BLOCK), weight, jnp.int32).astype(F32)
    row = rows((8, BLOCK))
    shot = jnp.where(
        row % 2 == 0,
        jnp.full((8, BLOCK), shots[2 * me], jnp.int32),
        jnp.full((8, BLOCK), shots[2 * me + 1], jnp.int32),
    ).astype(F32)
    scale = shot / (jnp.sqrt(total / npts + 1e-06) * weight)
    nparams = kernels.shape[0]
    factors = [jnp.broadcast_to(scale[:, p:p + 1], (8, BLOCK)) for p in range(nparams)]
    for out, at, turn, side in pieces:
        base = (lax.rem(me + turn, ranges) * 2 + side) * span
        for p in range(nparams):
            def one(i, _):
                low = pl.multiple_of(base + i * 16, 16)
                x = kernels[p, pl.ds(low, 8), :] * factors[p]
                y = kernels[p, pl.ds(low + 8, 8), :] * factors[p]
                x = x + pltpu.roll(x, 7, 0)
                y = y + pltpu.roll(y, 1, 0)
                out[at * nparams + p, pl.ds(pl.multiple_of(i * 8, 8), 8), :] = jnp.where(row % 2 == 0, x, y)
                return 0
            lax.fori_loop(0, span // 16, one, 0, unroll=4)


def weighted(plan, rank, shots, power, kernels, ready, npts, ranges):
    nparams = kernels.shape[0]
    span = kernels.shape[1] // (2 * ranges)
    return pl.pallas_call(
        functools.partial(scale_kernel, npts, ranges, plan),
        out_shape=[
            jax.ShapeDtypeStruct((nparams * len(parts), span // 2, BLOCK), F32) for parts in plan
        ],
        in_specs=[SMEM, SMEM, VMEM, VMEM, ANY],
        out_specs=[VMEM] * len(plan),
        compiler_params=params(16),
        cost_estimate=cost(3 * kernels.size, 6 * kernels.size),
    )(rank, shots, power, kernels, ready)


def source_rows(x):
    row = rows(x.shape)
    high = x.astype(BF).astype(F32)
    rest = x - high
    low = rest.astype(BF).astype(F32)
    first = jnp.where(row == 7, low, high)
    second = jnp.where(row == 3, rest - low, jnp.where(row == 7, 0.0, low))
    return jnp.concatenate([first, second], axis=0).astype(BF)


def target_rows(x):
    row = rows(x.shape)
    high = x.astype(BF).astype(F32)
    low = x - high
    first = jnp.where(row % 4 == 3, 1.0, jnp.where(row < 4, high, low))
    second = jnp.where(row == 7, 0.0, first)
    return jnp.concatenate([first, second], axis=0).astype(BF)


def field_rows(x):
    high = x.astype(BF).astype(F32)
    return jnp.concatenate([high, x - high], axis=0).astype(BF)


def point(coords, index):
    x = (coords[:, block(index)] - 1.5) * (LOG2E ** 0.5)
    half = -0.5 * jnp.sum(x * x, axis=0, keepdims=True)
    return jnp.concatenate([x, half], axis=0)


def coord_kernel(send, coords, source, out, token):
    token[...] = jnp.zeros_like(token)
    npeer, cap = send.shape
    blocks = coords.shape[1] // BLOCK

    def sources(i, _):
        x = point(coords, i)
        source[i] = source_rows(jnp.concatenate([x, x], axis=0))
        return 0
    lax.fori_loop(0, blocks, sources, 0, unroll=4)
    source[blocks] = jnp.zeros((16, BLOCK), BF)

    for group in range(npeer):
        def pick(i, _):
            pair = [point(coords, send[group, 2 * i + k]) for k in range(2)]
            out[group * (cap // 2) + i] = jnp.concatenate(pair, axis=0)
            return 0
        lax.fori_loop(0, cap // 2, pick, 0, unroll=4)


def coord_tables(send, coords):
    blocks = coords.shape[1] // BLOCK
    return pl.pallas_call(
        coord_kernel,
        out_shape=[
            jax.ShapeDtypeStruct((blocks + 1, 16, BLOCK), BF),
            jax.ShapeDtypeStruct((send.size // 2, 8, BLOCK), F32),
            jax.ShapeDtypeStruct((8, BLOCK), F32),
        ],
        in_specs=[SMEM, VMEM],
        out_specs=[VMEM] * 3,
        compiler_params=params(16),
        cost_estimate=cost(coords.size * 30, coords.size * 12),
    )(send, coords)


TURNS = 8


def aim_kernel(rank, near_order, far_order, coords_in, plain, near, far, coords, target, sem):
    groups, size = plain.shape[0], coords.shape[1]
    copy = pltpu.make_async_copy(
        coords_in.at[:, pl.ds(pl.multiple_of(rank[0] * size, size), size)], coords, sem
    )
    copy.start()
    across = lax.broadcasted_iota(jnp.int32, (BLOCK, BLOCK), 1)
    same = jnp.where(rows((BLOCK, BLOCK)) == across, 1.0, 0.0).astype(BF)
    copy.wait()

    def turn(parts):
        x = jnp.concatenate(parts, axis=0)
        return lax.dot_general(same, x, NT, preferred_element_type=F32).astype(BF)

    def natural(i, _):
        parts = []
        for k in range(TURNS):
            x = point(coords, TURNS * i + k)
            parts.append(target_rows(jnp.concatenate([x, x], axis=0)))
            target[TURNS * i + k] = parts[-1]
        plain[i] = turn(parts)
        return 0
    lax.fori_loop(0, groups, natural, 0, unroll=2)

    def by_count(i, _):
        near[i] = turn([target[near_order[TURNS * i + k]] for k in range(TURNS)])
        far[i] = turn([target[far_order[TURNS * i + k]] for k in range(TURNS)])
        return 0
    lax.fori_loop(0, groups, by_count, 0, unroll=4)


def aims(rank, near_order, far_order, coords):
    targets = near_order.shape[0]
    return pl.pallas_call(
        aim_kernel,
        out_shape=[jax.ShapeDtypeStruct((targets // TURNS, BLOCK, BLOCK), BF)] * 3,
        in_specs=[SMEM, SMEM, SMEM, HBM],
        out_specs=[VMEM] * 3,
        scratch_shapes=[
            pltpu.VMEM((coords.shape[0], targets * BLOCK), F32),
            pltpu.VMEM((targets, 16, BLOCK), BF),
            pltpu.SemaphoreType.DMA(()),
        ],
        compiler_params=params(16),
        cost_estimate=cost(2 * 10 ** 9, 10 ** 7),
    )(rank, near_order, far_order, held(coords))


def place(index):
    inner = index & 7
    return index - inner + 2 * (inner & 3) + (inner >> 2)


def gather_kernel(rank, core, send, coords, ready, *rest):
    parts, (down, up, far, near, full, sem) = rest[:8], rest[8:]
    npeer, cap = send.shape
    side = core[0]
    lot = cap + cap // 2
    plan = (
        (down, 0, 3), (down, lot, 1 + 4 * side), (up, 0, 2), (up, lot, 4 - 4 * side),
        (far, 0, 5 - side), (near, 0, side),
    )
    copies = []
    for at, (out, base, group) in enumerate(plan):
        copies.append(pltpu.make_async_copy(
            coords.at[pl.ds(group * (cap // 2), cap // 2)],
            out.at[pl.ds(base + cap, cap // 2)],
            sem.at[at],
        ))
        copies[-1].start()
    half = parts[0].shape[1]
    blocks = 8 * half
    me = rank[0]
    for turn, part in enumerate(parts):
        base = (lax.rem(me + turn // 2, 4) * 2 + turn % 2) * half
        for p in range(7):
            def store(i, _):
                at = pl.multiple_of(i * 8, 8)
                full[pl.ds(pl.multiple_of(p * blocks + base + at, 8), 8), :] = part[p, pl.ds(at, 8), :]
                return 0
            lax.fori_loop(0, half // 8, store, 0, unroll=True)

    def ones(i, _):
        full[pl.ds(pl.multiple_of(7 * blocks + i * 8, 8), 8), :] = jnp.ones((8, BLOCK), F32)
        return 0
    lax.fori_loop(0, blocks // 8, ones, 0, unroll=8)
    for out, base, group in plan:
        def pick(i, _):
            out[base + i] = full[pl.ds(place(send[group, i]), 8, stride=blocks), :]
            return 0
        lax.fori_loop(0, cap, pick, 0, unroll=8)
    for copy in copies:
        copy.wait()


def gathered(rank, core, send, coords, ready, parts):
    blocks = 8 * parts[0].shape[1]
    npeer, cap = send.shape
    lot = cap + cap // 2
    return pl.pallas_call(
        gather_kernel,
        out_shape=[jax.ShapeDtypeStruct((n * lot, 8, BLOCK), F32) for n in (2, 2, 1, 1)]
        + [jax.ShapeDtypeStruct((8 * blocks, BLOCK), F32)],
        in_specs=[SMEM, SMEM, SMEM, VMEM, ANY] + [VMEM] * 8,
        out_specs=[VMEM] * 5,
        scratch_shapes=[pltpu.SemaphoreType.DMA((npeer,))],
        compiler_params=params(16),
    )(rank, core, send, coords, ready, *parts)


def table_kernel(rank, *rest):
    parts, table = rest[:-1], rest[-1]
    half = (table.shape[0] - 1) // 8
    top = jnp.ones((1, BLOCK), F32)
    table[8 * half] = jnp.zeros((16, BLOCK), BF)
    for at, part in enumerate(parts):
        base = (lax.rem(rank[0] + (0, 1, 3)[at // 2], 4) * 2 + at % 2) * half

        def build(i, _):
            x = part[pl.ds(place(i), 7, stride=half), :]
            table[base + i] = field_rows(jnp.concatenate([x, top], axis=0))
            return 0
        lax.fori_loop(0, half, build, 0, unroll=8)


def early_table(rank, parts):
    half = parts[0].shape[1]
    return pl.pallas_call(
        table_kernel,
        out_shape=jax.ShapeDtypeStruct((8 * half + 1, 16, BLOCK), BF),
        in_specs=[SMEM] + [VMEM] * len(parts),
        out_specs=VMEM,
        compiler_params=params(16),
        cost_estimate=cost(2 * 10 ** 9, 10 ** 7),
    )(rank, *[part.reshape(-1, BLOCK) for part in parts])


SIZES = (7, 5, 4, 3, 2, 1)


def work_order(slots, wanted, none, every):
    kmax, targets = slots.shape
    index = jnp.arange(targets, dtype=jnp.int32)
    found = wanted.astype(jnp.int32)
    position = jnp.cumsum(found, axis=0) - found
    seat = jnp.arange(kmax, dtype=jnp.int32)[:, None, None]
    taken = (position[None] == seat) & wanted[None]
    counts = jnp.sum(found, axis=0)
    lists = jnp.sum(jnp.where(taken, slots[None], 0), axis=1)
    lists = jnp.where(seat[:, 0] < counts, lists, none)
    key = counts * targets + (targets - 1 - index)
    rank = jnp.sum((key[None, :] > key[:, None]).astype(jnp.int32), axis=1)
    order = jnp.sum(jnp.where(rank[:, None] == index[None, :], index[:, None], 0), axis=0)
    above = jnp.array(SIZES[1:] + (-1 if every else 0,), jnp.int32)
    groups = jnp.sum((counts > above[:, None]).astype(jnp.int32), axis=1)
    return lists, order, (groups + TURNS - 1) // TURNS


def lifted(x, at):
    none = jnp.zeros_like(x)
    return jnp.concatenate([x if turn == at else none for turn in range(TURNS)], axis=0)


def weights(target, coords):
    columns = [lifted(x, at) for at, some in enumerate(coords) for x in some]
    power = jnp.dot(target, jnp.concatenate(columns, axis=1), preferred_element_type=F32)
    weight = jnp.exp2(power)
    high = weight.astype(BF)
    return high, (weight - high.astype(F32)).astype(BF)


def summed(weight, field):
    return lax.dot_general(weight, field, NT, preferred_element_type=F32)


def turned(parts):
    packed = None
    for at, part in enumerate(parts):
        size = part.shape[1]
        wide = jnp.concatenate([part, jnp.zeros((BLOCK, BLOCK - size), F32)], axis=1)
        wide = pltpu.roll(wide, size * at, 1) if at else wide
        packed = wide if packed is None else packed + wide
    return packed.T


def self_kernel(side, rank, source, target, own, out):
    half = out.shape[0]
    first = (rank[0] * 2 + side) * half
    top = jnp.ones((1, BLOCK), F32)

    def group(i):
        coords, fields, parts = [], [], []
        for turn in range(TURNS):
            at = TURNS * i + turn
            coords.append([source[first + at]])
            x = own[pl.ds(place(at), 7, stride=half), :]
            field = lifted(field_rows(jnp.concatenate([x, top], axis=0)), turn)
            fields += [field, field]
        high, low = weights(target[side * (half // TURNS) + i], coords)
        for turn in range(TURNS):
            at = slice(turn * BLOCK, (turn + 1) * BLOCK)
            parts += [high[:, at], low[:, at]]
        return summed(jnp.concatenate(parts, axis=1), jnp.concatenate(fields, axis=1)).T

    lots = 4

    def step(i, _):
        totals = [group(lots * i + lot) for lot in range(lots)]
        for lot, total in enumerate(totals):
            for turn in range(TURNS):
                out[TURNS * (lots * i + lot) + turn] = total[16 * turn:16 * turn + 16]
        return 0
    lax.fori_loop(0, half // TURNS // lots, step, 0)


def self_sums(side, rank, source, target, own):
    half = own.shape[1]
    return pl.pallas_call(
        functools.partial(self_kernel, side),
        out_shape=jax.ShapeDtypeStruct((half, 16, BLOCK), F32),
        in_specs=[SMEM] + [VMEM] * 3,
        out_specs=VMEM,
        compiler_params=params(16),
        cost_estimate=cost(3 * 10 ** 9, 10 ** 7),
    )(rank, source, target, own.reshape(-1, BLOCK))


def each_group(lists, order, bounds, target, source, table, use):
    first = jnp.int32(0)
    for part, count in enumerate(SIZES):
        def group(at):
            chosen = [order[TURNS * at + turn] for turn in range(TURNS)]
            slots = [[lists[k, b] for k in range(count)] for b in chosen]
            high, low = weights(target[at], [[source[s] for s in some] for some in slots])
            parts = []
            for turn, some in enumerate(slots):
                at = slice(turn * count * BLOCK, (turn + 1) * count * BLOCK)
                parts.append(summed(
                    jnp.concatenate([high[:, at], low[:, at]], axis=1),
                    jnp.concatenate([table[s] for s in some] * 2, axis=1),
                ))
            sums = turned(parts)
            return [(b, sums[16 * turn:16 * turn + 16]) for turn, b in enumerate(chosen)]

        shift = 0 if count > 3 else 1

        def step(i, base):
            found = []
            for lot in range(1 << shift):
                found += group(jnp.minimum(base + (i << shift) + lot, target.shape[0] - 1))
            for b, sums in found:
                use(b, sums)
            return base
        steps = jnp.maximum((bounds[part] - first + (1 << shift) - 1) >> shift, 0)
        lax.fori_loop(0, steps, step, first)
        first = first + (steps << shift)


def near_kernel(rank, lists, order, bounds, target, source, early, full, first_half, second_half, out, start, table, sem):
    half = first_half.shape[0]
    blocks = source.shape[0] - 1
    moved = pltpu.make_async_copy(early, table, sem)
    moved.start()

    def copy(i, _):
        for base, part in ((0, first_half), (half, second_half)):
            x = part[i]
            out[base + i] = x
            start[base + i] = x
        return 0
    lax.fori_loop(0, half, copy, 0, unroll=8)
    moved.wait()
    base = lax.rem(rank[0] + 2, 4) * 2 * half

    def build(i, _):
        table[base + i] = field_rows(full[pl.ds(base + place(i), 8, stride=blocks), :])
        return 0
    lax.fori_loop(0, 2 * half, build, 0, unroll=8)

    def use(b, sums):
        out[b] = start[b] + sums
    each_group(lists, order, bounds, target, source, table, use)


def near_sums(rank, lists, order, bounds, target, source, early, full, first_half, second_half):
    return pl.pallas_call(
        near_kernel,
        out_shape=jax.ShapeDtypeStruct((order.shape[0], 16, BLOCK), F32),
        in_specs=[SMEM] * 4 + [VMEM] * 6,
        out_specs=VMEM,
        scratch_shapes=[
            pltpu.VMEM((order.shape[0], 16, BLOCK), F32),
            pltpu.VMEM(early.shape, BF),
            pltpu.SemaphoreType.DMA(()),
        ],
        compiler_params=params(16),
        cost_estimate=cost(8 * 10 ** 9, 10 ** 7),
    )(rank, lists, order, bounds, target, source, early, full, first_half, second_half)


def far_kernel(core, lists, order, bounds, target, start, *rest):
    parts = rest[:-3]
    out, source, table = rest[-3:]
    side = core[0]
    cap = parts[-1].shape[0] * 2 // 3
    groups = (3, 2, 4 + side, 1 - side, 5 - 4 * side, 4 * side)
    for part, group in zip(parts, groups):
        base = group * cap

        def coords(i, _):
            x = part[cap + i]
            turned = pltpu.roll(x, 4, 0)
            row = rows(x.shape)
            source[base + 2 * i] = source_rows(jnp.where(row < 4, x, turned))
            source[base + 2 * i + 1] = source_rows(jnp.where(row < 4, turned, x))
            return 0
        lax.fori_loop(0, cap // 2, coords, 0, unroll=4)

        def fields(i, _):
            table[base + i] = field_rows(part[i])
            return 0
        lax.fori_loop(0, cap, fields, 0, unroll=8)
    none = len(parts) * cap
    source[none] = jnp.zeros((16, BLOCK), BF)
    table[none] = jnp.zeros((16, BLOCK), BF)

    def use(b, sums):
        total = sums + start[b]
        out[:, block(b)] = (total[0:7] + total[8:15]) / total[7:8]
    each_group(lists, order, bounds, target, source, table, use)


def far_sums(core, lists, order, bounds, target, start, parts):
    size = len(parts) * (parts[-1].shape[0] * 2 // 3) + 1
    return pl.pallas_call(
        far_kernel,
        out_shape=jax.ShapeDtypeStruct((7, order.shape[0] * BLOCK), F32),
        in_specs=[SMEM] * 4 + [VMEM] * (2 + len(parts)),
        out_specs=VMEM,
        scratch_shapes=[pltpu.VMEM((size, 16, BLOCK), BF)] * 2,
        compiler_params=params(16),
    )(core, lists, order, bounds, target, start, *parts)


def body(kernels, shots, coords, send_list, block_list, block_count):
    slices = lax.axis_size("cuts")
    ranges = lax.axis_size("event")
    events, nparams, points = kernels.shape
    blocks = points // BLOCK
    npeer, cap = send_list.shape[2:]
    targets = block_list.shape[1]
    rank = jnp.reshape(lax.axis_index("event"), (1,)).astype(jnp.int32)
    core = jnp.reshape(lax.axis_index("cuts") % 2, (1,)).astype(jnp.int32)
    send = send_list.reshape(npeer, cap)
    kernels = kernels.transpose(1, 0, 2).reshape(nparams, events, blocks, BLOCK)
    kernels = kernels.transpose(0, 2, 1, 3).reshape(nparams, blocks * events, BLOCK)
    kernels = held(kernels)

    power, kernels = local_power(kernels, slices)
    coords, power = lax.optimization_barrier((coords, power))
    power = lax.all_to_all(power, "cuts", 0, 0)
    source, near_coord, token = coord_tables(send, coords)
    slots = block_list[0].T[1:]
    live = jnp.arange(1, block_list.shape[2], dtype=jnp.int32)[:, None] < block_count
    near_work = work_order(slots, live & (slots < blocks), blocks, False)
    far_work = work_order(slots - blocks, live & (slots >= blocks), npeer * cap, True)
    npts = float(points * slices)
    across_a, across_b, ahead_b, behind_a = weighted(
        (((2, 0),), ((2, 1),), ((1, 1),), ((3, 0),)), rank, shots, power, kernels, token, npts, ranges
    )
    from_left = shifted(across_a, "event", 1)
    from_right = shifted(across_b, "event", -1)
    left_b = shifted(ahead_b, "event", 1)
    right_a = shifted(behind_a, "event", -1)
    mine_a, mine_b, ahead_a, behind_b = weighted(
        (((0, 0),), ((0, 1),), ((1, 0),), ((3, 1),)), rank, shots, power, kernels, token, npts, ranges
    )
    from_left, from_right, near_work, far_work = lax.optimization_barrier(
        (from_left, from_right, near_work, far_work)
    )
    aimed = aims(rank, near_work[1], far_work[1], coords)
    left_a = shifted(ahead_a + from_left, "event", 1)
    right_b = shifted(behind_b + from_right, "event", -1)
    left_a, right_b, left_b, right_a, aimed = lax.optimization_barrier(
        (left_a, right_b, left_b, right_a, aimed)
    )
    target, near_target, far_target = aimed
    own_a = mine_a + left_a + right_a
    own_b = mine_b + right_b + left_b

    own_a, own_b = lax.optimization_barrier((own_a, own_b))
    left_a = shifted(own_a, "event", 1)
    right_b = shifted(own_b, "event", -1)
    left_b = shifted(own_b, "event", 1)
    right_a = shifted(own_a, "event", -1)
    first_half = self_sums(0, rank, source, target, own_a)
    left_a, right_b, first_half = lax.optimization_barrier((left_a, right_b, first_half))
    far_a = shifted(left_a, "event", 1)
    far_b = shifted(right_b, "event", -1)
    second_half = self_sums(1, rank, source, target, own_b)

    early = early_table(rank, (own_a, own_b, right_a, right_b, left_a, left_b))
    down, up, far, near, full = gathered(
        rank, core, send, near_coord, early,
        (own_a, own_b, right_a, right_b, far_a, far_b, left_a, left_b),
    )
    lot = near.shape[0]
    near = swapped(near, "cuts", 1)
    down = shifted(down, "cuts", -2)
    up = shifted(up, "cuts", 2)
    far = swapped(far, "cuts", -3)
    start = near_sums(rank, *near_work, near_target, source, early, full, first_half, second_half)
    down, up, start = lax.optimization_barrier((down, up, start))
    parts = (
        down, up, far, near, swapped(down[lot:], "cuts", 1), swapped(up[lot:], "cuts", 1)
    )
    return far_sums(core, *far_work, far_target, start, parts)


def solution(mesh):
    placed = (
        P("event", None, "cuts"),
        P(),
        P(None, "cuts"),
        P("cuts", "event", None, None),
        P("cuts", "event", None),
        P("cuts", "event"),
    )
    return jax.shard_map(
        body, mesh=mesh, in_specs=placed, out_specs=P(None, ("cuts", "event")), check_vma=False
    )
```

```python
import functools

import jax
import jax.numpy as jnp
from jax import lax
from jax.experimental import pallas as pl
from jax.experimental.pallas import tpu as pltpu
from jax.sharding import PartitionSpec as P

BLOCK = 128
BF = jnp.bfloat16
F32 = jnp.float32
LOG2E = 1.4426950408889634
NT = (((1,), (1,)), ((), ()))
TN = (((0,), (0,)), ((), ()))
VMEM = pl.BlockSpec(memory_space=pltpu.VMEM)
SMEM = pl.BlockSpec(memory_space=pltpu.SMEM)
ANY = pl.BlockSpec(memory_space=pl.ANY)
HBM = pl.BlockSpec(memory_space=pltpu.HBM)


def params(mib):
    return pltpu.CompilerParams(vmem_limit_bytes=mib << 20)


def cost(flops, moved):
    return pl.CostEstimate(flops=flops, bytes_accessed=moved, transcendentals=0)


def shifted(value, axis, steps):
    count = lax.axis_size(axis)
    pairs = [(source, (source + steps) % count) for source in range(count)]
    return lax.ppermute(value, axis, pairs)


def swapped(value, axis, steps):
    count = lax.axis_size(axis)
    pairs = [(source, (source + (steps if source % 2 == 0 else -steps)) % count) for source in range(count)]
    return lax.ppermute(value, axis, pairs)


def held(x):
    return pltpu.with_memory_space_constraint(x, pltpu.HBM)


def rows(shape):
    return lax.broadcasted_iota(jnp.int32, shape, 0)


def block(index):
    return pl.ds(pl.multiple_of(index * BLOCK, BLOCK), BLOCK)


def power_kernel(kernels, out, local, sems):
    params_here, count = kernels.shape[0], kernels.shape[1] // 8
    copies = [
        pltpu.make_async_copy(kernels.at[p], local.at[p], sems.at[p])
        for p in range(params_here)
    ]
    for copy in copies:
        copy.start()
    lane = lax.broadcasted_iota(jnp.int32, (8, BLOCK), 1)
    tile = jnp.zeros((8, BLOCK), F32)
    for p in range(params_here):
        copies[p].wait()

        def add(i, totals):
            found = []
            for part in range(4):
                x = local[p, pl.ds(pl.multiple_of((i * 4 + part) * 8, 8), 8), :]
                found.append(totals[part] + x * x)
            return tuple(found)
        zero = jnp.zeros((8, BLOCK), F32)
        totals = lax.fori_loop(0, count // 4, add, (zero,) * 4, unroll=4)
        total = (totals[0] + totals[1]) + (totals[2] + totals[3])
        tile = jnp.where(lane == p, jnp.sum(total, axis=1, keepdims=True), tile)
    for peer in range(out.shape[0]):
        out[peer] = tile


def local_power(kernels, peers):
    return pl.pallas_call(
        power_kernel,
        out_shape=jax.ShapeDtypeStruct((peers, 8, BLOCK), F32),
        in_specs=[HBM],
        out_specs=VMEM,
        scratch_shapes=[
            pltpu.VMEM(kernels.shape, F32),
            pltpu.SemaphoreType.DMA((kernels.shape[0],)),
        ],
        compiler_params=params(16),
        cost_estimate=cost(2 * kernels.size, 4 * kernels.size),
    )(kernels)


def scale_kernel(npts, ranges, plan, rank, shots, power, kernels, ready, *rest):
    outs, local, sems = rest[:-2], rest[-2], rest[-1]
    me = rank[0]
    span = local.shape[2]
    pieces = [(out, at, turn, side) for out, parts in zip(outs, plan) for at, (turn, side) in enumerate(parts)]
    copies = []
    for n, (_, _, turn, side) in enumerate(pieces):
        base = pl.multiple_of((lax.rem(me + turn, ranges) * 2 + side) * span, span)
        copies.append(pltpu.make_async_copy(
            kernels.at[:, pl.ds(base, span), :], local.at[n], sems.at[n]
        ))
        copies[-1].start()
    total = jnp.sum(power[...], axis=0)
    total = total + pltpu.roll(total, 2, 0)
    total = total + pltpu.roll(total, 4, 0)
    weight = jnp.int32(0)
    for event in range(shots.shape[0]):
        weight += shots[event]
    weight = jnp.full((8, BLOCK), weight, jnp.int32).astype(F32)
    row = rows((8, BLOCK))
    shot = jnp.where(
        row % 2 == 0,
        jnp.full((8, BLOCK), shots[2 * me], jnp.int32),
        jnp.full((8, BLOCK), shots[2 * me + 1], jnp.int32),
    ).astype(F32)
    scale = shot / (jnp.sqrt(total / npts + 1e-06) * weight)
    nparams = kernels.shape[0]
    factors = [jnp.broadcast_to(scale[:, p:p + 1], (8, BLOCK)) for p in range(nparams)]
    for n, (out, at, _, _) in enumerate(pieces):
        copies[n].wait()
        for p in range(nparams):
            def one(i, _):
                low = pl.multiple_of(i * 16, 16)
                x = local[n, p, pl.ds(low, 8), :] * factors[p]
                y = local[n, p, pl.ds(low + 8, 8), :] * factors[p]
                x = x + pltpu.roll(x, 7, 0)
                y = y + pltpu.roll(y, 1, 0)
                out[at * nparams + p, pl.ds(pl.multiple_of(i * 8, 8), 8), :] = jnp.where(row % 2 == 0, x, y)
                return 0
            lax.fori_loop(0, span // 16, one, 0, unroll=4)


def weighted(plan, rank, shots, power, kernels, ready, npts, ranges):
    nparams = kernels.shape[0]
    span = kernels.shape[1] // (2 * ranges)
    count = sum(len(parts) for parts in plan)
    return pl.pallas_call(
        functools.partial(scale_kernel, npts, ranges, plan),
        out_shape=[
            jax.ShapeDtypeStruct((nparams * len(parts), span // 2, BLOCK), F32) for parts in plan
        ],
        in_specs=[SMEM, SMEM, VMEM, HBM, ANY],
        out_specs=[VMEM] * len(plan),
        scratch_shapes=[
            pltpu.VMEM((count, nparams, span, BLOCK), F32),
            pltpu.SemaphoreType.DMA((count,)),
        ],
        compiler_params=params(16),
        cost_estimate=cost(3 * kernels.size, 6 * kernels.size),
    )(rank, shots, power, kernels, ready)


def source_rows(x):
    row = rows(x.shape)
    high = x.astype(BF).astype(F32)
    rest = x - high
    low = rest.astype(BF).astype(F32)
    first = jnp.where(row == 7, low, high)
    second = jnp.where(row == 3, rest - low, jnp.where(row == 7, 0.0, low))
    return jnp.concatenate([first, second], axis=0).astype(BF)


def target_rows(x):
    row = rows(x.shape)
    high = x.astype(BF).astype(F32)
    low = x - high
    first = jnp.where(row % 4 == 3, 1.0, jnp.where(row < 4, high, low))
    second = jnp.where(row == 7, 0.0, first)
    return jnp.concatenate([first, second], axis=0).astype(BF)


def field_rows(x):
    high = x.astype(BF).astype(F32)
    return jnp.concatenate([high, x - high], axis=0).astype(BF)


def point(coords, index):
    x = (coords[:, block(index)] - 1.5) * (LOG2E ** 0.5)
    half = -0.5 * jnp.sum(x * x, axis=0, keepdims=True)
    return jnp.concatenate([x, half], axis=0)


def coord_kernel(send, coords, source, out, token):
    token[...] = jnp.zeros_like(token)
    npeer, cap = send.shape
    blocks = coords.shape[1] // BLOCK

    def sources(i, _):
        x = point(coords, i)
        source[i] = source_rows(jnp.concatenate([x, x], axis=0))
        return 0
    lax.fori_loop(0, blocks, sources, 0, unroll=4)
    source[blocks] = jnp.zeros((16, BLOCK), BF)

    for group in range(npeer):
        def pick(i, _):
            pair = [point(coords, send[group, 2 * i + k]) for k in range(2)]
            out[group * (cap // 2) + i] = jnp.concatenate(pair, axis=0)
            return 0
        lax.fori_loop(0, cap // 2, pick, 0, unroll=4)


def coord_tables(send, coords):
    blocks = coords.shape[1] // BLOCK
    return pl.pallas_call(
        coord_kernel,
        out_shape=[
            jax.ShapeDtypeStruct((blocks + 1, 16, BLOCK), BF),
            jax.ShapeDtypeStruct((send.size // 2, 8, BLOCK), F32),
            jax.ShapeDtypeStruct((8, BLOCK), F32),
        ],
        in_specs=[SMEM, VMEM],
        out_specs=[VMEM] * 3,
        compiler_params=params(16),
        cost_estimate=cost(coords.size * 30, coords.size * 12),
    )(send, coords)


TURNS = 8


def aim_kernel(rank, near_order, far_order, coords_in, plain, near, far, coords, target, sem):
    groups, size = plain.shape[0], coords.shape[1]
    copy = pltpu.make_async_copy(
        coords_in.at[:, pl.ds(pl.multiple_of(rank[0] * size, size), size)], coords, sem
    )
    copy.start()
    across = lax.broadcasted_iota(jnp.int32, (BLOCK, BLOCK), 1)
    same = jnp.where(rows((BLOCK, BLOCK)) == across, 1.0, 0.0).astype(BF)
    copy.wait()

    def turn(parts):
        x = jnp.concatenate(parts, axis=0)
        return lax.dot_general(same, x, NT, preferred_element_type=F32).astype(BF)

    def natural(i, _):
        parts = []
        for k in range(TURNS):
            x = point(coords, TURNS * i + k)
            parts.append(target_rows(jnp.concatenate([x, x], axis=0)))
            target[TURNS * i + k] = parts[-1]
        plain[i] = turn(parts)
        return 0
    lax.fori_loop(0, groups, natural, 0, unroll=2)

    def by_count(i, _):
        near[i] = turn([target[near_order[TURNS * i + k]] for k in range(TURNS)])
        far[i] = turn([target[far_order[TURNS * i + k]] for k in range(TURNS)])
        return 0
    lax.fori_loop(0, groups, by_count, 0, unroll=4)


def aims(rank, near_order, far_order, coords):
    targets = near_order.shape[0]
    return pl.pallas_call(
        aim_kernel,
        out_shape=[jax.ShapeDtypeStruct((targets // TURNS, BLOCK, BLOCK), BF)] * 3,
        in_specs=[SMEM, SMEM, SMEM, HBM],
        out_specs=[VMEM] * 3,
        scratch_shapes=[
            pltpu.VMEM((coords.shape[0], targets * BLOCK), F32),
            pltpu.VMEM((targets, 16, BLOCK), BF),
            pltpu.SemaphoreType.DMA(()),
        ],
        compiler_params=params(16),
        cost_estimate=cost(2 * 10 ** 9, 10 ** 7),
    )(rank, near_order, far_order, held(coords))


def place(index):
    inner = index & 7
    return index - inner + 2 * (inner & 3) + (inner >> 2)


def gather_kernel(rank, core, send, coords, ready, *rest):
    parts, (down, up, far, near, full, sem) = rest[:8], rest[8:]
    npeer, cap = send.shape
    side = core[0]
    lot = cap + cap // 2
    plan = (
        (down, 0, 3), (down, lot, 1 + 4 * side), (up, 0, 2), (up, lot, 4 - 4 * side),
        (far, 0, 5 - side), (near, 0, side),
    )
    copies = []
    for at, (out, base, group) in enumerate(plan):
        copies.append(pltpu.make_async_copy(
            coords.at[pl.ds(group * (cap // 2), cap // 2)],
            out.at[pl.ds(base + cap, cap // 2)],
            sem.at[at],
        ))
        copies[-1].start()
    half = parts[0].shape[1]
    blocks = 8 * half
    me = rank[0]
    for turn, part in enumerate(parts):
        base = (lax.rem(me + turn // 2, 4) * 2 + turn % 2) * half
        for p in range(7):
            def store(i, _):
                at = pl.multiple_of(i * 8, 8)
                full[pl.ds(pl.multiple_of(p * blocks + base + at, 8), 8), :] = part[p, pl.ds(at, 8), :]
                return 0
            lax.fori_loop(0, half // 8, store, 0, unroll=True)

    def ones(i, _):
        full[pl.ds(pl.multiple_of(7 * blocks + i * 8, 8), 8), :] = jnp.ones((8, BLOCK), F32)
        return 0
    lax.fori_loop(0, blocks // 8, ones, 0, unroll=8)
    for out, base, group in plan:
        def pick(i, _):
            out[base + i] = full[pl.ds(place(send[group, i]), 8, stride=blocks), :]
            return 0
        lax.fori_loop(0, cap, pick, 0, unroll=8)
    for copy in copies:
        copy.wait()


def gathered(rank, core, send, coords, ready, parts):
    blocks = 8 * parts[0].shape[1]
    npeer, cap = send.shape
    lot = cap + cap // 2
    return pl.pallas_call(
        gather_kernel,
        out_shape=[jax.ShapeDtypeStruct((n * lot, 8, BLOCK), F32) for n in (2, 2, 1, 1)]
        + [jax.ShapeDtypeStruct((8 * blocks, BLOCK), F32)],
        in_specs=[SMEM, SMEM, SMEM, VMEM, ANY] + [VMEM] * 8,
        out_specs=[VMEM] * 5,
        scratch_shapes=[pltpu.SemaphoreType.DMA((npeer,))],
        compiler_params=params(16),
    )(rank, core, send, coords, ready, *parts)


def table_kernel(rank, *rest):
    parts, table = rest[:-1], rest[-1]
    half = (table.shape[0] - 1) // 8
    top = jnp.ones((1, BLOCK), F32)
    table[8 * half] = jnp.zeros((16, BLOCK), BF)
    for at, part in enumerate(parts):
        base = (lax.rem(rank[0] + (0, 1, 3)[at // 2], 4) * 2 + at % 2) * half

        def build(i, _):
            x = part[pl.ds(place(i), 7, stride=half), :]
            table[base + i] = field_rows(jnp.concatenate([x, top], axis=0))
            return 0
        lax.fori_loop(0, half, build, 0, unroll=8)


def early_table(rank, parts):
    half = parts[0].shape[1]
    return pl.pallas_call(
        table_kernel,
        out_shape=jax.ShapeDtypeStruct((8 * half + 1, 16, BLOCK), BF),
        in_specs=[SMEM] + [VMEM] * len(parts),
        out_specs=VMEM,
        compiler_params=params(16),
        cost_estimate=cost(2 * 10 ** 9, 10 ** 7),
    )(rank, *[part.reshape(-1, BLOCK) for part in parts])


SIZES = (7, 5, 4, 3, 2, 1)


def work_order(slots, wanted, none, every):
    kmax, targets = slots.shape
    index = jnp.arange(targets, dtype=jnp.int32)
    found = wanted.astype(jnp.int32)
    position = jnp.cumsum(found, axis=0) - found
    seat = jnp.arange(kmax, dtype=jnp.int32)[:, None, None]
    taken = (position[None] == seat) & wanted[None]
    counts = jnp.sum(found, axis=0)
    lists = jnp.sum(jnp.where(taken, slots[None], 0), axis=1)
    lists = jnp.where(seat[:, 0] < counts, lists, none)
    key = counts * targets + (targets - 1 - index)
    rank = jnp.sum((key[None, :] > key[:, None]).astype(jnp.int32), axis=1)
    order = jnp.sum(jnp.where(rank[:, None] == index[None, :], index[:, None], 0), axis=0)
    above = jnp.array(SIZES[1:] + (-1 if every else 0,), jnp.int32)
    groups = jnp.sum((counts > above[:, None]).astype(jnp.int32), axis=1)
    return lists, order, (groups + TURNS - 1) // TURNS


def lifted(x, at):
    none = jnp.zeros_like(x)
    return jnp.concatenate([x if turn == at else none for turn in range(TURNS)], axis=0)


def weights(target, coords):
    columns = [lifted(x, at) for at, some in enumerate(coords) for x in some]
    power = jnp.dot(target, jnp.concatenate(columns, axis=1), preferred_element_type=F32)
    weight = jnp.exp2(power)
    high = weight.astype(BF)
    return high, (weight - high.astype(F32)).astype(BF)


def summed(weight, field):
    return lax.dot_general(weight, field, NT, preferred_element_type=F32)


def turned(parts):
    packed = None
    for at, part in enumerate(parts):
        size = part.shape[1]
        wide = jnp.concatenate([part, jnp.zeros((BLOCK, BLOCK - size), F32)], axis=1)
        wide = pltpu.roll(wide, size * at, 1) if at else wide
        packed = wide if packed is None else packed + wide
    return packed.T


def self_kernel(side, rank, source, target, own, out):
    half = out.shape[0]
    first = (rank[0] * 2 + side) * half
    top = jnp.ones((1, BLOCK), F32)

    def group(i):
        coords, fields, parts = [], [], []
        for turn in range(TURNS):
            at = TURNS * i + turn
            coords.append([source[first + at]])
            x = own[pl.ds(place(at), 7, stride=half), :]
            field = lifted(field_rows(jnp.concatenate([x, top], axis=0)), turn)
            fields += [field, field]
        high, low = weights(target[side * (half // TURNS) + i], coords)
        for turn in range(TURNS):
            at = slice(turn * BLOCK, (turn + 1) * BLOCK)
            parts += [high[:, at], low[:, at]]
        return summed(jnp.concatenate(parts, axis=1), jnp.concatenate(fields, axis=1)).T

    lots = 4

    def step(i, _):
        totals = [group(lots * i + lot) for lot in range(lots)]
        for lot, total in enumerate(totals):
            for turn in range(TURNS):
                out[TURNS * (lots * i + lot) + turn] = total[16 * turn:16 * turn + 16]
        return 0
    lax.fori_loop(0, half // TURNS // lots, step, 0)


def self_sums(side, rank, source, target, own):
    half = own.shape[1]
    return pl.pallas_call(
        functools.partial(self_kernel, side),
        out_shape=jax.ShapeDtypeStruct((half, 16, BLOCK), F32),
        in_specs=[SMEM] + [VMEM] * 3,
        out_specs=VMEM,
        compiler_params=params(16),
        cost_estimate=cost(3 * 10 ** 9, 10 ** 7),
    )(rank, source, target, own.reshape(-1, BLOCK))


def each_group(lists, order, bounds, target, source, table, use):
    first = jnp.int32(0)
    for part, count in enumerate(SIZES):
        def group(at):
            chosen = [order[TURNS * at + turn] for turn in range(TURNS)]
            slots = [[lists[k, b] for k in range(count)] for b in chosen]
            high, low = weights(target[at], [[source[s] for s in some] for some in slots])
            parts = []
            for turn, some in enumerate(slots):
                at = slice(turn * count * BLOCK, (turn + 1) * count * BLOCK)
                parts.append(summed(
                    jnp.concatenate([high[:, at], low[:, at]], axis=1),
                    jnp.concatenate([table[s] for s in some] * 2, axis=1),
                ))
            sums = turned(parts)
            return [(b, sums[16 * turn:16 * turn + 16]) for turn, b in enumerate(chosen)]

        shift = 0 if count > 3 else 1

        def step(i, base):
            found = []
            for lot in range(1 << shift):
                found += group(jnp.minimum(base + (i << shift) + lot, target.shape[0] - 1))
            for b, sums in found:
                use(b, sums)
            return base
        steps = jnp.maximum((bounds[part] - first + (1 << shift) - 1) >> shift, 0)
        lax.fori_loop(0, steps, step, first)
        first = first + (steps << shift)


def near_kernel(rank, lists, order, bounds, target, source, early, full, first_half, second_half, out, start, table, sem):
    half = first_half.shape[0]
    blocks = source.shape[0] - 1
    moved = pltpu.make_async_copy(early, table, sem)
    moved.start()

    def copy(i, _):
        for base, part in ((0, first_half), (half, second_half)):
            x = part[i]
            out[base + i] = x
            start[base + i] = x
        return 0
    lax.fori_loop(0, half, copy, 0, unroll=8)
    moved.wait()
    base = lax.rem(rank[0] + 2, 4) * 2 * half

    def build(i, _):
        table[base + i] = field_rows(full[pl.ds(base + place(i), 8, stride=blocks), :])
        return 0
    lax.fori_loop(0, 2 * half, build, 0, unroll=8)

    def use(b, sums):
        out[b] = start[b] + sums
    each_group(lists, order, bounds, target, source, table, use)


def near_sums(rank, lists, order, bounds, target, source, early, full, first_half, second_half):
    return pl.pallas_call(
        near_kernel,
        out_shape=jax.ShapeDtypeStruct((order.shape[0], 16, BLOCK), F32),
        in_specs=[SMEM] * 4 + [VMEM] * 6,
        out_specs=VMEM,
        scratch_shapes=[
            pltpu.VMEM((order.shape[0], 16, BLOCK), F32),
            pltpu.VMEM(early.shape, BF),
            pltpu.SemaphoreType.DMA(()),
        ],
        compiler_params=params(16),
        cost_estimate=cost(8 * 10 ** 9, 10 ** 7),
    )(rank, lists, order, bounds, target, source, early, full, first_half, second_half)


def far_kernel(core, lists, order, bounds, target, start, *rest):
    parts = rest[:-3]
    out, source, table = rest[-3:]
    side = core[0]
    cap = parts[-1].shape[0] * 2 // 3
    groups = (3, 2, 4 + side, 1 - side, 5 - 4 * side, 4 * side)
    for part, group in zip(parts, groups):
        base = group * cap

        def coords(i, _):
            x = part[cap + i]
            turned = pltpu.roll(x, 4, 0)
            row = rows(x.shape)
            source[base + 2 * i] = source_rows(jnp.where(row < 4, x, turned))
            source[base + 2 * i + 1] = source_rows(jnp.where(row < 4, turned, x))
            return 0
        lax.fori_loop(0, cap // 2, coords, 0, unroll=4)

        def fields(i, _):
            table[base + i] = field_rows(part[i])
            return 0
        lax.fori_loop(0, cap, fields, 0, unroll=8)
    none = len(parts) * cap
    source[none] = jnp.zeros((16, BLOCK), BF)
    table[none] = jnp.zeros((16, BLOCK), BF)

    def use(b, sums):
        total = sums + start[b]
        out[:, block(b)] = (total[0:7] + total[8:15]) / total[7:8]
    each_group(lists, order, bounds, target, source, table, use)


def far_sums(core, lists, order, bounds, target, start, parts):
    size = len(parts) * (parts[-1].shape[0] * 2 // 3) + 1
    return pl.pallas_call(
        far_kernel,
        out_shape=jax.ShapeDtypeStruct((7, order.shape[0] * BLOCK), F32),
        in_specs=[SMEM] * 4 + [VMEM] * (2 + len(parts)),
        out_specs=VMEM,
        scratch_shapes=[pltpu.VMEM((size, 16, BLOCK), BF)] * 2,
        compiler_params=params(16),
    )(core, lists, order, bounds, target, start, *parts)


def body(kernels, shots, coords, send_list, block_list, block_count):
    slices = lax.axis_size("cuts")
    ranges = lax.axis_size("event")
    events, nparams, points = kernels.shape
    blocks = points // BLOCK
    npeer, cap = send_list.shape[2:]
    targets = block_list.shape[1]
    rank = jnp.reshape(lax.axis_index("event"), (1,)).astype(jnp.int32)
    core = jnp.reshape(lax.axis_index("cuts") % 2, (1,)).astype(jnp.int32)
    send = send_list.reshape(npeer, cap)
    kernels = kernels.transpose(1, 0, 2).reshape(nparams, events, blocks, BLOCK)
    kernels = kernels.transpose(0, 2, 1, 3).reshape(nparams, blocks * events, BLOCK)
    kernels = held(kernels)

    power = local_power(kernels, slices)
    coords, power = lax.optimization_barrier((coords, power))
    power = lax.all_to_all(power, "cuts", 0, 0)
    source, near_coord, token = coord_tables(send, coords)
    slots = block_list[0].T[1:]
    live = jnp.arange(1, block_list.shape[2], dtype=jnp.int32)[:, None] < block_count
    near_work = work_order(slots, live & (slots < blocks), blocks, False)
    far_work = work_order(slots - blocks, live & (slots >= blocks), npeer * cap, True)
    npts = float(points * slices)
    across_a, across_b, ahead_b, behind_a = weighted(
        (((2, 0),), ((2, 1),), ((1, 1),), ((3, 0),)), rank, shots, power, kernels, token, npts, ranges
    )
    from_left = shifted(across_a, "event", 1)
    from_right = shifted(across_b, "event", -1)
    left_b = shifted(ahead_b, "event", 1)
    right_a = shifted(behind_a, "event", -1)
    mine_a, mine_b, ahead_a, behind_b = weighted(
        (((0, 0),), ((0, 1),), ((1, 0),), ((3, 1),)), rank, shots, power, kernels, token, npts, ranges
    )
    from_left, from_right, near_work, far_work = lax.optimization_barrier(
        (from_left, from_right, near_work, far_work)
    )
    aimed = aims(rank, near_work[1], far_work[1], coords)
    left_a = shifted(ahead_a + from_left, "event", 1)
    right_b = shifted(behind_b + from_right, "event", -1)
    left_a, right_b, left_b, right_a, aimed = lax.optimization_barrier(
        (left_a, right_b, left_b, right_a, aimed)
    )
    target, near_target, far_target = aimed
    own_a = mine_a + left_a + right_a
    own_b = mine_b + right_b + left_b

    own_a, own_b = lax.optimization_barrier((own_a, own_b))
    left_a = shifted(own_a, "event", 1)
    right_b = shifted(own_b, "event", -1)
    left_b = shifted(own_b, "event", 1)
    right_a = shifted(own_a, "event", -1)
    first_half = self_sums(0, rank, source, target, own_a)
    left_a, right_b, first_half = lax.optimization_barrier((left_a, right_b, first_half))
    far_a = shifted(left_a, "event", 1)
    far_b = shifted(right_b, "event", -1)
    second_half = self_sums(1, rank, source, target, own_b)

    early = early_table(rank, (own_a, own_b, right_a, right_b, left_a, left_b))
    down, up, far, near, full = gathered(
        rank, core, send, near_coord, early,
        (own_a, own_b, right_a, right_b, far_a, far_b, left_a, left_b),
    )
    lot = near.shape[0]
    near = swapped(near, "cuts", 1)
    down = shifted(down, "cuts", -2)
    up = shifted(up, "cuts", 2)
    far = swapped(far, "cuts", -3)
    start = near_sums(rank, *near_work, near_target, source, early, full, first_half, second_half)
    down, up, start = lax.optimization_barrier((down, up, start))
    parts = (
        down, up, far, near, swapped(down[lot:], "cuts", 1), swapped(up[lot:], "cuts", 1)
    )
    return far_sums(core, *far_work, far_target, start, parts)


def solution(mesh):
    placed = (
        P("event", None, "cuts"),
        P(),
        P(None, "cuts"),
        P("cuts", "event", None, None),
        P("cuts", "event", None),
        P("cuts", "event"),
    )
    return jax.shard_map(
        body, mesh=mesh, in_specs=placed, out_specs=P(None, ("cuts", "event")), check_vma=False
    )
```

```python
import functools

import jax
import jax.numpy as jnp
from jax import lax
from jax.experimental import pallas as pl
from jax.experimental.pallas import tpu as pltpu
from jax.sharding import PartitionSpec as P

BLOCK = 128
BF = jnp.bfloat16
F32 = jnp.float32
LOG2E = 1.4426950408889634
NT = (((1,), (1,)), ((), ()))
TN = (((0,), (0,)), ((), ()))
VMEM = pl.BlockSpec(memory_space=pltpu.VMEM)
SMEM = pl.BlockSpec(memory_space=pltpu.SMEM)
ANY = pl.BlockSpec(memory_space=pl.ANY)
HBM = pl.BlockSpec(memory_space=pltpu.HBM)


def params(mib):
    return pltpu.CompilerParams(vmem_limit_bytes=mib << 20)


def cost(flops, moved):
    return pl.CostEstimate(flops=flops, bytes_accessed=moved, transcendentals=0)


def shifted(value, axis, steps):
    count = lax.axis_size(axis)
    pairs = [(source, (source + steps) % count) for source in range(count)]
    return lax.ppermute(value, axis, pairs)


def swapped(value, axis, steps):
    count = lax.axis_size(axis)
    pairs = [(source, (source + (steps if source % 2 == 0 else -steps)) % count) for source in range(count)]
    return lax.ppermute(value, axis, pairs)


def held(x):
    return pltpu.with_memory_space_constraint(x, pltpu.HBM)


def rows(shape):
    return lax.broadcasted_iota(jnp.int32, shape, 0)


def block(index):
    return pl.ds(pl.multiple_of(index * BLOCK, BLOCK), BLOCK)


def power_kernel(kernels, out, local, sems):
    params_here, count = kernels.shape[0], kernels.shape[1] // 8
    copies = [
        pltpu.make_async_copy(kernels.at[p], local.at[p], sems.at[p])
        for p in range(params_here)
    ]
    for copy in copies:
        copy.start()
    lane = lax.broadcasted_iota(jnp.int32, (8, BLOCK), 1)
    tile = jnp.zeros((8, BLOCK), F32)
    for p in range(params_here):
        copies[p].wait()

        def add(i, totals):
            found = []
            for part in range(4):
                x = local[p, pl.ds(pl.multiple_of((i * 4 + part) * 8, 8), 8), :]
                found.append(totals[part] + x * x)
            return tuple(found)
        zero = jnp.zeros((8, BLOCK), F32)
        totals = lax.fori_loop(0, count // 4, add, (zero,) * 4, unroll=4)
        total = (totals[0] + totals[1]) + (totals[2] + totals[3])
        tile = jnp.where(lane == p, jnp.sum(total, axis=1, keepdims=True), tile)
    for peer in range(out.shape[0]):
        out[peer] = tile


def local_power(kernels, peers):
    return pl.pallas_call(
        power_kernel,
        out_shape=jax.ShapeDtypeStruct((peers, 8, BLOCK), F32),
        in_specs=[HBM],
        out_specs=VMEM,
        scratch_shapes=[
            pltpu.VMEM(kernels.shape, F32),
            pltpu.SemaphoreType.DMA((kernels.shape[0],)),
        ],
        compiler_params=params(16),
        cost_estimate=cost(2 * kernels.size, 4 * kernels.size),
    )(kernels)


def scale_kernel(npts, ranges, plan, rank, shots, power, kernels, ready, *rest):
    outs, local, sems = rest[:-2], rest[-2], rest[-1]
    me = rank[0]
    span = local.shape[2]
    pieces = [(out, at, turn, side) for out, parts in zip(outs, plan) for at, (turn, side) in enumerate(parts)]
    copies = []
    for n, (_, _, turn, side) in enumerate(pieces):
        base = pl.multiple_of((lax.rem(me + turn, ranges) * 2 + side) * span, span)
        copies.append(pltpu.make_async_copy(
            kernels.at[:, pl.ds(base, span), :], local.at[n], sems.at[n]
        ))
        copies[-1].start()
    total = jnp.sum(power[...], axis=0)
    total = total + pltpu.roll(total, 2, 0)
    total = total + pltpu.roll(total, 4, 0)
    weight = jnp.int32(0)
    for event in range(shots.shape[0]):
        weight += shots[event]
    weight = jnp.full((8, BLOCK), weight, jnp.int32).astype(F32)
    row = rows((8, BLOCK))
    shot = jnp.where(
        row % 2 == 0,
        jnp.full((8, BLOCK), shots[2 * me], jnp.int32),
        jnp.full((8, BLOCK), shots[2 * me + 1], jnp.int32),
    ).astype(F32)
    scale = shot / (jnp.sqrt(total / npts + 1e-06) * weight)
    nparams = kernels.shape[0]
    factors = [jnp.broadcast_to(scale[:, p:p + 1], (8, BLOCK)) for p in range(nparams)]
    for n, (out, at, _, _) in enumerate(pieces):
        copies[n].wait()
        for p in range(nparams):
            def one(i, _):
                low = pl.multiple_of(i * 16, 16)
                x = local[n, p, pl.ds(low, 8), :] * factors[p]
                y = local[n, p, pl.ds(low + 8, 8), :] * factors[p]
                x = x + pltpu.roll(x, 7, 0)
                y = y + pltpu.roll(y, 1, 0)
                out[at * nparams + p, pl.ds(pl.multiple_of(i * 8, 8), 8), :] = jnp.where(row % 2 == 0, x, y)
                return 0
            lax.fori_loop(0, span // 16, one, 0, unroll=4)


def weighted(plan, rank, shots, power, kernels, ready, npts, ranges):
    nparams = kernels.shape[0]
    span = kernels.shape[1] // (2 * ranges)
    count = sum(len(parts) for parts in plan)
    return pl.pallas_call(
        functools.partial(scale_kernel, npts, ranges, plan),
        out_shape=[
            jax.ShapeDtypeStruct((nparams * len(parts), span // 2, BLOCK), F32) for parts in plan
        ],
        in_specs=[SMEM, SMEM, VMEM, HBM, ANY],
        out_specs=[VMEM] * len(plan),
        scratch_shapes=[
            pltpu.VMEM((count, nparams, span, BLOCK), F32),
            pltpu.SemaphoreType.DMA((count,)),
        ],
        compiler_params=params(16),
        cost_estimate=cost(3 * kernels.size, 6 * kernels.size),
    )(rank, shots, power, kernels, ready)


def source_rows(x):
    row = rows(x.shape)
    high = x.astype(BF).astype(F32)
    rest = x - high
    low = rest.astype(BF).astype(F32)
    first = jnp.where(row == 7, low, high)
    second = jnp.where(row == 3, rest - low, jnp.where(row == 7, 0.0, low))
    return jnp.concatenate([first, second], axis=0).astype(BF)


def target_rows(x):
    row = rows(x.shape)
    high = x.astype(BF).astype(F32)
    low = x - high
    first = jnp.where(row % 4 == 3, 1.0, jnp.where(row < 4, high, low))
    second = jnp.where(row == 7, 0.0, first)
    return jnp.concatenate([first, second], axis=0).astype(BF)


def field_rows(x):
    high = x.astype(BF).astype(F32)
    return jnp.concatenate([high, x - high], axis=0).astype(BF)


def point(coords, index):
    x = (coords[:, block(index)] - 1.5) * (LOG2E ** 0.5)
    half = -0.5 * jnp.sum(x * x, axis=0, keepdims=True)
    return jnp.concatenate([x, half], axis=0)


def coord_kernel(send, coords, source, out, token):
    token[...] = jnp.zeros_like(token)
    npeer, cap = send.shape
    blocks = coords.shape[1] // BLOCK

    def sources(i, _):
        x = point(coords, i)
        source[i] = source_rows(jnp.concatenate([x, x], axis=0))
        return 0
    lax.fori_loop(0, blocks, sources, 0, unroll=4)
    source[blocks] = jnp.zeros((16, BLOCK), BF)

    for group in range(npeer):
        def pick(i, _):
            pair = [point(coords, send[group, 2 * i + k]) for k in range(2)]
            out[group * (cap // 2) + i] = jnp.concatenate(pair, axis=0)
            return 0
        lax.fori_loop(0, cap // 2, pick, 0, unroll=4)


def coord_tables(send, coords):
    blocks = coords.shape[1] // BLOCK
    return pl.pallas_call(
        coord_kernel,
        out_shape=[
            jax.ShapeDtypeStruct((blocks + 1, 16, BLOCK), BF),
            jax.ShapeDtypeStruct((send.size // 2, 8, BLOCK), F32),
            jax.ShapeDtypeStruct((8, BLOCK), F32),
        ],
        in_specs=[SMEM, VMEM],
        out_specs=[VMEM] * 3,
        compiler_params=params(16),
        cost_estimate=cost(coords.size * 30, coords.size * 12),
    )(send, coords)


TURNS = 8


def aim_kernel(rank, near_order, far_order, coords_in, plain, near, far, coords, target, sem):
    groups, size = plain.shape[0], coords.shape[1]
    copy = pltpu.make_async_copy(
        coords_in.at[:, pl.ds(pl.multiple_of(rank[0] * size, size), size)], coords, sem
    )
    copy.start()
    across = lax.broadcasted_iota(jnp.int32, (BLOCK, BLOCK), 1)
    same = jnp.where(rows((BLOCK, BLOCK)) == across, 1.0, 0.0).astype(BF)
    copy.wait()

    def turn(parts):
        x = jnp.concatenate(parts, axis=0)
        return lax.dot_general(same, x, NT, preferred_element_type=F32).astype(BF)

    def natural(i, _):
        parts = []
        for k in range(TURNS):
            x = point(coords, TURNS * i + k)
            parts.append(target_rows(jnp.concatenate([x, x], axis=0)))
            target[TURNS * i + k] = parts[-1]
        plain[i] = turn(parts)
        return 0
    lax.fori_loop(0, groups, natural, 0, unroll=2)

    def by_count(i, _):
        near[i] = turn([target[near_order[TURNS * i + k]] for k in range(TURNS)])
        far[i] = turn([target[far_order[TURNS * i + k]] for k in range(TURNS)])
        return 0
    lax.fori_loop(0, groups, by_count, 0, unroll=4)


def aims(rank, near_order, far_order, coords):
    targets = near_order.shape[0]
    return pl.pallas_call(
        aim_kernel,
        out_shape=[jax.ShapeDtypeStruct((targets // TURNS, BLOCK, BLOCK), BF)] * 3,
        in_specs=[SMEM, SMEM, SMEM, HBM],
        out_specs=[VMEM] * 3,
        scratch_shapes=[
            pltpu.VMEM((coords.shape[0], targets * BLOCK), F32),
            pltpu.VMEM((targets, 16, BLOCK), BF),
            pltpu.SemaphoreType.DMA(()),
        ],
        compiler_params=params(16),
        cost_estimate=cost(2 * 10 ** 9, 10 ** 7),
    )(rank, near_order, far_order, held(coords))


def place(index):
    inner = index & 7
    return index - inner + 2 * (inner & 3) + (inner >> 2)


def gather_kernel(rank, core, send, coords, ready, *rest):
    parts, (down, up, far, near, full, sem) = rest[:8], rest[8:]
    npeer, cap = send.shape
    side = core[0]
    lot = cap + cap // 2
    plan = (
        (down, 0, 3), (down, lot, 1 + 4 * side), (up, 0, 2), (up, lot, 4 - 4 * side),
        (far, 0, 5 - side), (near, 0, side),
    )
    copies = []
    for at, (out, base, group) in enumerate(plan):
        copies.append(pltpu.make_async_copy(
            coords.at[pl.ds(group * (cap // 2), cap // 2)],
            out.at[pl.ds(base + cap, cap // 2)],
            sem.at[at],
        ))
        copies[-1].start()
    half = parts[0].shape[1]
    blocks = 8 * half
    me = rank[0]
    for turn, part in enumerate(parts):
        base = (lax.rem(me + turn // 2, 4) * 2 + turn % 2) * half
        for p in range(7):
            def store(i, _):
                at = pl.multiple_of(i * 8, 8)
                full[pl.ds(pl.multiple_of(p * blocks + base + at, 8), 8), :] = part[p, pl.ds(at, 8), :]
                return 0
            lax.fori_loop(0, half // 8, store, 0, unroll=True)

    def ones(i, _):
        full[pl.ds(pl.multiple_of(7 * blocks + i * 8, 8), 8), :] = jnp.ones((8, BLOCK), F32)
        return 0
    lax.fori_loop(0, blocks // 8, ones, 0, unroll=8)
    for out, base, group in plan:
        def pick(i, _):
            out[base + i] = full[pl.ds(place(send[group, i]), 8, stride=blocks), :]
            return 0
        lax.fori_loop(0, cap, pick, 0, unroll=8)
    for copy in copies:
        copy.wait()


def gathered(rank, core, send, coords, ready, parts):
    blocks = 8 * parts[0].shape[1]
    npeer, cap = send.shape
    lot = cap + cap // 2
    return pl.pallas_call(
        gather_kernel,
        out_shape=[jax.ShapeDtypeStruct((n * lot, 8, BLOCK), F32) for n in (2, 2, 1, 1)]
        + [jax.ShapeDtypeStruct((8 * blocks, BLOCK), F32)],
        in_specs=[SMEM, SMEM, SMEM, VMEM, ANY] + [VMEM] * 8,
        out_specs=[VMEM] * 5,
        scratch_shapes=[pltpu.SemaphoreType.DMA((npeer,))],
        compiler_params=params(16),
    )(rank, core, send, coords, ready, *parts)


def table_kernel(rank, *rest):
    parts, table = rest[:-1], rest[-1]
    half = (table.shape[0] - 1) // 8
    top = jnp.ones((1, BLOCK), F32)
    table[8 * half] = jnp.zeros((16, BLOCK), BF)
    for at, part in enumerate(parts):
        base = (lax.rem(rank[0] + (0, 1, 3)[at // 2], 4) * 2 + at % 2) * half

        def build(i, _):
            x = part[pl.ds(place(i), 7, stride=half), :]
            table[base + i] = field_rows(jnp.concatenate([x, top], axis=0))
            return 0
        lax.fori_loop(0, half, build, 0, unroll=8)


def early_table(rank, parts):
    half = parts[0].shape[1]
    return pl.pallas_call(
        table_kernel,
        out_shape=jax.ShapeDtypeStruct((8 * half + 1, 16, BLOCK), BF),
        in_specs=[SMEM] + [VMEM] * len(parts),
        out_specs=VMEM,
        compiler_params=params(16),
        cost_estimate=cost(2 * 10 ** 9, 10 ** 7),
    )(rank, *[part.reshape(-1, BLOCK) for part in parts])


SIZES = (7, 5, 4, 3, 2, 1)


def work_order(slots, wanted, none, every):
    kmax, targets = slots.shape
    index = jnp.arange(targets, dtype=jnp.int32)
    found = wanted.astype(jnp.int32)
    position = jnp.cumsum(found, axis=0) - found
    seat = jnp.arange(kmax, dtype=jnp.int32)[:, None, None]
    taken = (position[None] == seat) & wanted[None]
    counts = jnp.sum(found, axis=0)
    lists = jnp.sum(jnp.where(taken, slots[None], 0), axis=1)
    lists = jnp.where(seat[:, 0] < counts, lists, none)
    key = counts * targets + (targets - 1 - index)
    rank = jnp.sum((key[None, :] > key[:, None]).astype(jnp.int32), axis=1)
    order = jnp.sum(jnp.where(rank[:, None] == index[None, :], index[:, None], 0), axis=0)
    above = jnp.array(SIZES[1:] + (-1 if every else 0,), jnp.int32)
    groups = jnp.sum((counts > above[:, None]).astype(jnp.int32), axis=1)
    return lists, order, (groups + TURNS - 1) // TURNS


def lifted(x, at):
    none = jnp.zeros_like(x)
    return jnp.concatenate([x if turn == at else none for turn in range(TURNS)], axis=0)


def weights(target, coords):
    columns = [lifted(x, at) for at, some in enumerate(coords) for x in some]
    power = jnp.dot(target, jnp.concatenate(columns, axis=1), preferred_element_type=F32)
    weight = jnp.exp2(power)
    high = weight.astype(BF)
    return high, (weight - high.astype(F32)).astype(BF)


def summed(weight, field):
    return lax.dot_general(weight, field, NT, preferred_element_type=F32)


def turned(parts):
    packed = None
    for at, part in enumerate(parts):
        size = part.shape[1]
        wide = jnp.concatenate([part, jnp.zeros((BLOCK, BLOCK - size), F32)], axis=1)
        wide = pltpu.roll(wide, size * at, 1) if at else wide
        packed = wide if packed is None else packed + wide
    return packed.T


def self_kernel(side, rank, source, target, own, out):
    half = out.shape[0]
    first = (rank[0] * 2 + side) * half
    top = jnp.ones((1, BLOCK), F32)

    def group(i):
        coords, fields, parts = [], [], []
        for turn in range(TURNS):
            at = TURNS * i + turn
            coords.append([source[first + at]])
            x = own[pl.ds(place(at), 7, stride=half), :]
            field = lifted(field_rows(jnp.concatenate([x, top], axis=0)), turn)
            fields += [field, field]
        high, low = weights(target[side * (half // TURNS) + i], coords)
        for turn in range(TURNS):
            at = slice(turn * BLOCK, (turn + 1) * BLOCK)
            parts += [high[:, at], low[:, at]]
        return summed(jnp.concatenate(parts, axis=1), jnp.concatenate(fields, axis=1)).T

    lots = 4

    def step(i, _):
        totals = [group(lots * i + lot) for lot in range(lots)]
        for lot, total in enumerate(totals):
            for turn in range(TURNS):
                out[TURNS * (lots * i + lot) + turn] = total[16 * turn:16 * turn + 16]
        return 0
    lax.fori_loop(0, half // TURNS // lots, step, 0)


def self_sums(side, rank, source, target, own):
    half = own.shape[1]
    return pl.pallas_call(
        functools.partial(self_kernel, side),
        out_shape=jax.ShapeDtypeStruct((half, 16, BLOCK), F32),
        in_specs=[SMEM] + [VMEM] * 3,
        out_specs=VMEM,
        compiler_params=params(16),
        cost_estimate=cost(3 * 10 ** 9, 10 ** 7),
    )(rank, source, target, own.reshape(-1, BLOCK))


def each_group(lists, order, bounds, target, source, table, use):
    first = jnp.int32(0)
    for part, count in enumerate(SIZES):
        def group(at):
            chosen = [order[TURNS * at + turn] for turn in range(TURNS)]
            slots = [[lists[k, b] for k in range(count)] for b in chosen]
            high, low = weights(target[at], [[source[s] for s in some] for some in slots])
            parts = []
            for turn, some in enumerate(slots):
                at = slice(turn * count * BLOCK, (turn + 1) * count * BLOCK)
                parts.append(summed(
                    jnp.concatenate([high[:, at], low[:, at]], axis=1),
                    jnp.concatenate([table[s] for s in some] * 2, axis=1),
                ))
            sums = turned(parts)
            return [(b, sums[16 * turn:16 * turn + 16]) for turn, b in enumerate(chosen)]

        shift = 0 if count > 3 else 1

        def step(i, base):
            found = []
            for lot in range(1 << shift):
                found += group(jnp.minimum(base + (i << shift) + lot, target.shape[0] - 1))
            for b, sums in found:
                use(b, sums)
            return base
        steps = jnp.maximum((bounds[part] - first + (1 << shift) - 1) >> shift, 0)
        lax.fori_loop(0, steps, step, first)
        first = first + (steps << shift)


def near_kernel(rank, lists, order, bounds, target, source, early, full, first_half, second_half, out, start, table, sem):
    half = first_half.shape[0]
    blocks = source.shape[0] - 1
    moved = pltpu.make_async_copy(early, table, sem)
    moved.start()

    def copy(i, _):
        for base, part in ((0, first_half), (half, second_half)):
            x = part[i]
            out[base + i] = x
            start[base + i] = x
        return 0
    lax.fori_loop(0, half, copy, 0, unroll=8)
    moved.wait()
    base = lax.rem(rank[0] + 2, 4) * 2 * half

    def build(i, _):
        table[base + i] = field_rows(full[pl.ds(base + place(i), 8, stride=blocks), :])
        return 0
    lax.fori_loop(0, 2 * half, build, 0, unroll=8)

    def use(b, sums):
        out[b] = start[b] + sums
    each_group(lists, order, bounds, target, source, table, use)


def near_sums(rank, lists, order, bounds, target, source, early, full, first_half, second_half):
    return pl.pallas_call(
        near_kernel,
        out_shape=jax.ShapeDtypeStruct((order.shape[0], 16, BLOCK), F32),
        in_specs=[SMEM] * 4 + [VMEM] * 6,
        out_specs=VMEM,
        scratch_shapes=[
            pltpu.VMEM((order.shape[0], 16, BLOCK), F32),
            pltpu.VMEM(early.shape, BF),
            pltpu.SemaphoreType.DMA(()),
        ],
        compiler_params=params(16),
        cost_estimate=cost(8 * 10 ** 9, 10 ** 7),
    )(rank, lists, order, bounds, target, source, early, full, first_half, second_half)


def far_kernel(core, lists, order, bounds, target, start, *rest):
    parts = rest[:-3]
    out, source, table = rest[-3:]
    side = core[0]
    cap = parts[-1].shape[0] * 2 // 3
    groups = (3, 2, 4 + side, 1 - side, 5 - 4 * side, 4 * side)
    for part, group in zip(parts, groups):
        base = group * cap

        def coords(i, _):
            x = part[cap + i]
            turned = pltpu.roll(x, 4, 0)
            row = rows(x.shape)
            source[base + 2 * i] = source_rows(jnp.where(row < 4, x, turned))
            source[base + 2 * i + 1] = source_rows(jnp.where(row < 4, turned, x))
            return 0
        lax.fori_loop(0, cap // 2, coords, 0, unroll=4)

        def fields(i, _):
            table[base + i] = field_rows(part[i])
            return 0
        lax.fori_loop(0, cap, fields, 0, unroll=8)
    none = len(parts) * cap
    source[none] = jnp.zeros((16, BLOCK), BF)
    table[none] = jnp.zeros((16, BLOCK), BF)

    def use(b, sums):
        total = sums + start[b]
        out[:, block(b)] = (total[0:7] + total[8:15]) / total[7:8]
    each_group(lists, order, bounds, target, source, table, use)


def far_sums(core, lists, order, bounds, target, start, parts):
    size = len(parts) * (parts[-1].shape[0] * 2 // 3) + 1
    return pl.pallas_call(
        far_kernel,
        out_shape=jax.ShapeDtypeStruct((7, order.shape[0] * BLOCK), F32),
        in_specs=[SMEM] * 4 + [VMEM] * (2 + len(parts)),
        out_specs=VMEM,
        scratch_shapes=[pltpu.VMEM((size, 16, BLOCK), BF)] * 2,
        compiler_params=params(16),
    )(core, lists, order, bounds, target, start, *parts)


def body(kernels, shots, coords, send_list, block_list, block_count):
    slices = lax.axis_size("cuts")
    ranges = lax.axis_size("event")
    events, nparams, points = kernels.shape
    blocks = points // BLOCK
    npeer, cap = send_list.shape[2:]
    targets = block_list.shape[1]
    rank = jnp.reshape(lax.axis_index("event"), (1,)).astype(jnp.int32)
    core = jnp.reshape(lax.axis_index("cuts") % 2, (1,)).astype(jnp.int32)
    send = send_list.reshape(npeer, cap)
    kernels = kernels.transpose(1, 0, 2).reshape(nparams, events, blocks, BLOCK)
    kernels = kernels.transpose(0, 2, 1, 3).reshape(nparams, blocks * events, BLOCK)
    kernels = held(kernels)

    power = local_power(kernels, slices)
    coords, power = lax.optimization_barrier((coords, power))
    power = lax.all_to_all(power, "cuts", 0, 0)
    source, near_coord, token = coord_tables(send, coords)
    slots = block_list[0].T[1:]
    live = jnp.arange(1, block_list.shape[2], dtype=jnp.int32)[:, None] < block_count
    near_work = work_order(slots, live & (slots < blocks), blocks, False)
    far_work = work_order(slots - blocks, live & (slots >= blocks), npeer * cap, True)
    npts = float(points * slices)
    across_a, across_b, ahead_b, behind_a = weighted(
        (((2, 0),), ((2, 1),), ((1, 1),), ((3, 0),)), rank, shots, power, kernels, token, npts, ranges
    )
    from_left = shifted(across_a, "event", 1)
    from_right = shifted(across_b, "event", -1)
    left_b = shifted(ahead_b, "event", 1)
    right_a = shifted(behind_a, "event", -1)
    mine_a, mine_b, ahead_a, behind_b = weighted(
        (((0, 0),), ((0, 1),), ((1, 0),), ((3, 1),)), rank, shots, power, kernels, token, npts, ranges
    )
    from_left, from_right, near_work, far_work = lax.optimization_barrier(
        (from_left, from_right, near_work, far_work)
    )
    aimed = aims(rank, near_work[1], far_work[1], coords)
    left_a = shifted(ahead_a + from_left, "event", 1)
    right_b = shifted(behind_b + from_right, "event", -1)
    left_a, right_b, left_b, right_a, aimed = lax.optimization_barrier(
        (left_a, right_b, left_b, right_a, aimed)
    )
    target, near_target, far_target = aimed
    own_a = mine_a + left_a + right_a
    own_b = mine_b + right_b + left_b

    own_a, own_b = lax.optimization_barrier((own_a, own_b))
    left_a = shifted(own_a, "event", 1)
    right_b = shifted(own_b, "event", -1)
    left_b = shifted(own_b, "event", 1)
    right_a = shifted(own_a, "event", -1)
    first_half = self_sums(0, rank, source, target, own_a)
    left_a, right_b, first_half = lax.optimization_barrier((left_a, right_b, first_half))
    far_a = shifted(left_a, "event", 1)
    far_b = shifted(right_b, "event", -1)
    second_half = self_sums(1, rank, source, target, own_b)

    early = early_table(rank, (own_a, own_b, right_a, right_b, left_a, left_b))
    down, up, far, near, full = gathered(
        rank, core, send, near_coord, early,
        (own_a, own_b, right_a, right_b, far_a, far_b, left_a, left_b),
    )
    lot = near.shape[0]
    down = shifted(down, "cuts", -2)
    up = shifted(up, "cuts", 2)
    far = swapped(far, "cuts", -3)
    start = near_sums(rank, *near_work, near_target, source, early, full, first_half, second_half)
    down, up, near, start = lax.optimization_barrier((down, up, near, start))
    near = swapped(near, "cuts", 1)
    parts = (
        down, up, far, near, swapped(down[lot:], "cuts", 1), swapped(up[lot:], "cuts", 1)
    )
    return far_sums(core, *far_work, far_target, start, parts)


def solution(mesh):
    placed = (
        P("event", None, "cuts"),
        P(),
        P(None, "cuts"),
        P("cuts", "event", None, None),
        P("cuts", "event", None),
        P("cuts", "event"),
    )
    return jax.shard_map(
        body, mesh=mesh, in_specs=placed, out_specs=P(None, ("cuts", "event")), check_vma=False
    )
```

```python
import functools

import jax
import jax.numpy as jnp
from jax import lax
from jax.experimental import pallas as pl
from jax.experimental.pallas import tpu as pltpu
from jax.sharding import PartitionSpec as P

BLOCK = 128
BF = jnp.bfloat16
F32 = jnp.float32
LOG2E = 1.4426950408889634
NT = (((1,), (1,)), ((), ()))
TN = (((0,), (0,)), ((), ()))
VMEM = pl.BlockSpec(memory_space=pltpu.VMEM)
SMEM = pl.BlockSpec(memory_space=pltpu.SMEM)
ANY = pl.BlockSpec(memory_space=pl.ANY)
HBM = pl.BlockSpec(memory_space=pltpu.HBM)


def params(mib):
    return pltpu.CompilerParams(vmem_limit_bytes=mib << 20)


def cost(flops, moved):
    return pl.CostEstimate(flops=flops, bytes_accessed=moved, transcendentals=0)


def shifted(value, axis, steps):
    count = lax.axis_size(axis)
    pairs = [(source, (source + steps) % count) for source in range(count)]
    return lax.ppermute(value, axis, pairs)


def swapped(value, axis, steps):
    count = lax.axis_size(axis)
    pairs = [(source, (source + (steps if source % 2 == 0 else -steps)) % count) for source in range(count)]
    return lax.ppermute(value, axis, pairs)


def held(x):
    return pltpu.with_memory_space_constraint(x, pltpu.HBM)


def rows(shape):
    return lax.broadcasted_iota(jnp.int32, shape, 0)


def block(index):
    return pl.ds(pl.multiple_of(index * BLOCK, BLOCK), BLOCK)


def power_kernel(kernels, out, local, sems):
    params_here, count = kernels.shape[0], kernels.shape[1] // 8
    copies = [
        pltpu.make_async_copy(kernels.at[p], local.at[p], sems.at[p])
        for p in range(params_here)
    ]
    for copy in copies:
        copy.start()
    lane = lax.broadcasted_iota(jnp.int32, (8, BLOCK), 1)
    tile = jnp.zeros((8, BLOCK), F32)
    for p in range(params_here):
        copies[p].wait()

        def add(i, totals):
            found = []
            for part in range(4):
                x = local[p, pl.ds(pl.multiple_of((i * 4 + part) * 8, 8), 8), :]
                found.append(totals[part] + x * x)
            return tuple(found)
        zero = jnp.zeros((8, BLOCK), F32)
        totals = lax.fori_loop(0, count // 4, add, (zero,) * 4, unroll=4)
        total = (totals[0] + totals[1]) + (totals[2] + totals[3])
        tile = jnp.where(lane == p, jnp.sum(total, axis=1, keepdims=True), tile)
    for peer in range(out.shape[0]):
        out[peer] = tile


def local_power(kernels, peers):
    return pl.pallas_call(
        power_kernel,
        out_shape=jax.ShapeDtypeStruct((peers, 8, BLOCK), F32),
        in_specs=[HBM],
        out_specs=VMEM,
        scratch_shapes=[
            pltpu.VMEM(kernels.shape, F32),
            pltpu.SemaphoreType.DMA((kernels.shape[0],)),
        ],
        compiler_params=params(16),
        cost_estimate=cost(2 * kernels.size, 4 * kernels.size),
    )(kernels)


def scale_kernel(npts, ranges, plan, rank, shots, power, kernels, ready, *rest):
    outs, local, sems = rest[:-2], rest[-2], rest[-1]
    me = rank[0]
    span = local.shape[2]
    pieces = [(out, at, turn, side) for out, parts in zip(outs, plan) for at, (turn, side) in enumerate(parts)]
    copies = []
    for n, (_, _, turn, side) in enumerate(pieces):
        base = pl.multiple_of((lax.rem(me + turn, ranges) * 2 + side) * span, span)
        copies.append(pltpu.make_async_copy(
            kernels.at[:, pl.ds(base, span), :], local.at[n], sems.at[n]
        ))
        copies[-1].start()
    total = jnp.sum(power[...], axis=0)
    total = total + pltpu.roll(total, 2, 0)
    total = total + pltpu.roll(total, 4, 0)
    weight = jnp.int32(0)
    for event in range(shots.shape[0]):
        weight += shots[event]
    weight = jnp.full((8, BLOCK), weight, jnp.int32).astype(F32)
    row = rows((8, BLOCK))
    shot = jnp.where(
        row % 2 == 0,
        jnp.full((8, BLOCK), shots[2 * me], jnp.int32),
        jnp.full((8, BLOCK), shots[2 * me + 1], jnp.int32),
    ).astype(F32)
    scale = shot / (jnp.sqrt(total / npts + 1e-06) * weight)
    nparams = kernels.shape[0]
    factors = [jnp.broadcast_to(scale[:, p:p + 1], (8, BLOCK)) for p in range(nparams)]
    for n, (out, at, _, _) in enumerate(pieces):
        copies[n].wait()
        for p in range(nparams):
            def one(i, _):
                low = pl.multiple_of(i * 16, 16)
                x = local[n, p, pl.ds(low, 8), :] * factors[p]
                y = local[n, p, pl.ds(low + 8, 8), :] * factors[p]
                x = x + pltpu.roll(x, 7, 0)
                y = y + pltpu.roll(y, 1, 0)
                out[at * nparams + p, pl.ds(pl.multiple_of(i * 8, 8), 8), :] = jnp.where(row % 2 == 0, x, y)
                return 0
            lax.fori_loop(0, span // 16, one, 0, unroll=4)


def weighted(plan, rank, shots, power, kernels, ready, npts, ranges):
    nparams = kernels.shape[0]
    span = kernels.shape[1] // (2 * ranges)
    count = sum(len(parts) for parts in plan)
    return pl.pallas_call(
        functools.partial(scale_kernel, npts, ranges, plan),
        out_shape=[
            jax.ShapeDtypeStruct((nparams * len(parts), span // 2, BLOCK), F32) for parts in plan
        ],
        in_specs=[SMEM, SMEM, VMEM, HBM, ANY],
        out_specs=[VMEM] * len(plan),
        scratch_shapes=[
            pltpu.VMEM((count, nparams, span, BLOCK), F32),
            pltpu.SemaphoreType.DMA((count,)),
        ],
        compiler_params=params(16),
        cost_estimate=cost(3 * kernels.size, 6 * kernels.size),
    )(rank, shots, power, kernels, ready)


def source_rows(x):
    row = rows(x.shape)
    high = x.astype(BF).astype(F32)
    rest = x - high
    low = rest.astype(BF).astype(F32)
    first = jnp.where(row == 7, low, high)
    second = jnp.where(row == 3, rest - low, jnp.where(row == 7, 0.0, low))
    return jnp.concatenate([first, second], axis=0).astype(BF)


def target_rows(x):
    row = rows(x.shape)
    high = x.astype(BF).astype(F32)
    low = x - high
    first = jnp.where(row % 4 == 3, 1.0, jnp.where(row < 4, high, low))
    second = jnp.where(row == 7, 0.0, first)
    return jnp.concatenate([first, second], axis=0).astype(BF)


def field_rows(x):
    high = x.astype(BF).astype(F32)
    return jnp.concatenate([high, x - high], axis=0).astype(BF)


def point(coords, index):
    x = (coords[:, block(index)] - 1.5) * (LOG2E ** 0.5)
    half = -0.5 * jnp.sum(x * x, axis=0, keepdims=True)
    return jnp.concatenate([x, half], axis=0)


def coord_kernel(send, coords, source, out, token):
    token[...] = jnp.zeros_like(token)
    npeer, cap = send.shape
    blocks = coords.shape[1] // BLOCK

    def sources(i, _):
        x = point(coords, i)
        source[i] = source_rows(jnp.concatenate([x, x], axis=0))
        return 0
    lax.fori_loop(0, blocks, sources, 0, unroll=4)
    source[blocks] = jnp.zeros((16, BLOCK), BF)

    for group in range(npeer):
        def pick(i, _):
            pair = [point(coords, send[group, 2 * i + k]) for k in range(2)]
            out[group * (cap // 2) + i] = jnp.concatenate(pair, axis=0)
            return 0
        lax.fori_loop(0, cap // 2, pick, 0, unroll=4)


def coord_tables(send, coords):
    blocks = coords.shape[1] // BLOCK
    return pl.pallas_call(
        coord_kernel,
        out_shape=[
            jax.ShapeDtypeStruct((blocks + 1, 16, BLOCK), BF),
            jax.ShapeDtypeStruct((send.size // 2, 8, BLOCK), F32),
            jax.ShapeDtypeStruct((8, BLOCK), F32),
        ],
        in_specs=[SMEM, VMEM],
        out_specs=[VMEM] * 3,
        compiler_params=params(16),
        cost_estimate=cost(coords.size * 30, coords.size * 12),
    )(send, coords)


TURNS = 8


def aim_kernel(rank, near_order, far_order, coords_in, plain, near, far, coords, target, sem):
    groups, size = plain.shape[0], coords.shape[1]
    copy = pltpu.make_async_copy(
        coords_in.at[:, pl.ds(pl.multiple_of(rank[0] * size, size), size)], coords, sem
    )
    copy.start()
    across = lax.broadcasted_iota(jnp.int32, (BLOCK, BLOCK), 1)
    same = jnp.where(rows((BLOCK, BLOCK)) == across, 1.0, 0.0).astype(BF)
    copy.wait()

    def turn(parts):
        x = jnp.concatenate(parts, axis=0)
        return lax.dot_general(same, x, NT, preferred_element_type=F32).astype(BF)

    def natural(i, _):
        parts = []
        for k in range(TURNS):
            x = point(coords, TURNS * i + k)
            parts.append(target_rows(jnp.concatenate([x, x], axis=0)))
            target[TURNS * i + k] = parts[-1]
        plain[i] = turn(parts)
        return 0
    lax.fori_loop(0, groups, natural, 0, unroll=2)

    def by_count(i, _):
        near[i] = turn([target[near_order[TURNS * i + k]] for k in range(TURNS)])
        far[i] = turn([target[far_order[TURNS * i + k]] for k in range(TURNS)])
        return 0
    lax.fori_loop(0, groups, by_count, 0, unroll=4)


def aims(rank, near_order, far_order, coords):
    targets = near_order.shape[0]
    return pl.pallas_call(
        aim_kernel,
        out_shape=[jax.ShapeDtypeStruct((targets // TURNS, BLOCK, BLOCK), BF)] * 3,
        in_specs=[SMEM, SMEM, SMEM, HBM],
        out_specs=[VMEM] * 3,
        scratch_shapes=[
            pltpu.VMEM((coords.shape[0], targets * BLOCK), F32),
            pltpu.VMEM((targets, 16, BLOCK), BF),
            pltpu.SemaphoreType.DMA(()),
        ],
        compiler_params=params(16),
        cost_estimate=cost(2 * 10 ** 9, 10 ** 7),
    )(rank, near_order, far_order, held(coords))


def place(index):
    inner = index & 7
    return index - inner + 2 * (inner & 3) + (inner >> 2)


def gather_kernel(rank, core, send, coords, ready, *rest):
    parts, (down, up, far, near, full, sem) = rest[:8], rest[8:]
    npeer, cap = send.shape
    side = core[0]
    lot = cap + cap // 2
    plan = (
        (down, 0, 3), (down, lot, 1 + 4 * side), (up, 0, 2), (up, lot, 4 - 4 * side),
        (far, 0, 5 - side), (near, 0, side),
    )
    copies = []
    for at, (out, base, group) in enumerate(plan):
        copies.append(pltpu.make_async_copy(
            coords.at[pl.ds(group * (cap // 2), cap // 2)],
            out.at[pl.ds(base + cap, cap // 2)],
            sem.at[at],
        ))
        copies[-1].start()
    half = parts[0].shape[1]
    blocks = 8 * half
    me = rank[0]
    for turn, part in enumerate(parts):
        base = (lax.rem(me + turn // 2, 4) * 2 + turn % 2) * half
        for p in range(7):
            def store(i, _):
                at = pl.multiple_of(i * 8, 8)
                full[pl.ds(pl.multiple_of(p * blocks + base + at, 8), 8), :] = part[p, pl.ds(at, 8), :]
                return 0
            lax.fori_loop(0, half // 8, store, 0, unroll=True)

    def ones(i, _):
        full[pl.ds(pl.multiple_of(7 * blocks + i * 8, 8), 8), :] = jnp.ones((8, BLOCK), F32)
        return 0
    lax.fori_loop(0, blocks // 8, ones, 0, unroll=8)
    for out, base, group in plan:
        def pick(i, _):
            out[base + i] = full[pl.ds(place(send[group, i]), 8, stride=blocks), :]
            return 0
        lax.fori_loop(0, cap, pick, 0, unroll=8)
    for copy in copies:
        copy.wait()


def gathered(rank, core, send, coords, ready, parts):
    blocks = 8 * parts[0].shape[1]
    npeer, cap = send.shape
    lot = cap + cap // 2
    return pl.pallas_call(
        gather_kernel,
        out_shape=[jax.ShapeDtypeStruct((n * lot, 8, BLOCK), F32) for n in (2, 2, 1, 1)]
        + [jax.ShapeDtypeStruct((8 * blocks, BLOCK), F32)],
        in_specs=[SMEM, SMEM, SMEM, VMEM, ANY] + [VMEM] * 8,
        out_specs=[VMEM] * 5,
        scratch_shapes=[pltpu.SemaphoreType.DMA((npeer,))],
        compiler_params=params(16),
    )(rank, core, send, coords, ready, *parts)


def table_kernel(rank, *rest):
    parts, table = rest[:-1], rest[-1]
    half = (table.shape[0] - 1) // 8
    top = jnp.ones((1, BLOCK), F32)
    table[8 * half] = jnp.zeros((16, BLOCK), BF)
    for at, part in enumerate(parts):
        base = (lax.rem(rank[0] + (0, 1, 3)[at // 2], 4) * 2 + at % 2) * half

        def build(i, _):
            x = part[pl.ds(place(i), 7, stride=half), :]
            table[base + i] = field_rows(jnp.concatenate([x, top], axis=0))
            return 0
        lax.fori_loop(0, half, build, 0, unroll=8)


def early_table(rank, parts):
    half = parts[0].shape[1]
    return pl.pallas_call(
        table_kernel,
        out_shape=jax.ShapeDtypeStruct((8 * half + 1, 16, BLOCK), BF),
        in_specs=[SMEM] + [VMEM] * len(parts),
        out_specs=VMEM,
        compiler_params=params(16),
        cost_estimate=cost(2 * 10 ** 9, 10 ** 7),
    )(rank, *[part.reshape(-1, BLOCK) for part in parts])


SIZES = (7, 5, 4, 3, 2, 1)


def work_order(slots, wanted, none, every):
    kmax, targets = slots.shape
    index = jnp.arange(targets, dtype=jnp.int32)
    found = wanted.astype(jnp.int32)
    position = jnp.cumsum(found, axis=0) - found
    seat = jnp.arange(kmax, dtype=jnp.int32)[:, None, None]
    taken = (position[None] == seat) & wanted[None]
    counts = jnp.sum(found, axis=0)
    lists = jnp.sum(jnp.where(taken, slots[None], 0), axis=1)
    lists = jnp.where(seat[:, 0] < counts, lists, none)
    key = counts * targets + (targets - 1 - index)
    rank = jnp.sum((key[None, :] > key[:, None]).astype(jnp.int32), axis=1)
    order = jnp.sum(jnp.where(rank[:, None] == index[None, :], index[:, None], 0), axis=0)
    above = jnp.array(SIZES[1:] + (-1 if every else 0,), jnp.int32)
    groups = jnp.sum((counts > above[:, None]).astype(jnp.int32), axis=1)
    return lists, order, (groups + TURNS - 1) // TURNS


def lifted(x, at):
    none = jnp.zeros_like(x)
    return jnp.concatenate([x if turn == at else none for turn in range(TURNS)], axis=0)


def weights(target, coords):
    columns = [lifted(x, at) for at, some in enumerate(coords) for x in some]
    power = jnp.dot(target, jnp.concatenate(columns, axis=1), preferred_element_type=F32)
    weight = jnp.exp2(power)
    high = weight.astype(BF)
    return high, (weight - high.astype(F32)).astype(BF)


def summed(weight, field):
    return lax.dot_general(weight, field, NT, preferred_element_type=F32)


def turned(parts):
    packed = None
    for at, part in enumerate(parts):
        size = part.shape[1]
        wide = jnp.concatenate([part, jnp.zeros((BLOCK, BLOCK - size), F32)], axis=1)
        wide = pltpu.roll(wide, size * at, 1) if at else wide
        packed = wide if packed is None else packed + wide
    return packed.T


def self_kernel(side, rank, source, target, own, out):
    half = out.shape[0]
    first = (rank[0] * 2 + side) * half
    top = jnp.ones((1, BLOCK), F32)

    def group(i):
        coords, fields, parts = [], [], []
        for turn in range(TURNS):
            at = TURNS * i + turn
            coords.append([source[first + at]])
            x = own[pl.ds(place(at), 7, stride=half), :]
            field = lifted(field_rows(jnp.concatenate([x, top], axis=0)), turn)
            fields += [field, field]
        high, low = weights(target[side * (half // TURNS) + i], coords)
        for turn in range(TURNS):
            at = slice(turn * BLOCK, (turn + 1) * BLOCK)
            parts += [high[:, at], low[:, at]]
        return summed(jnp.concatenate(parts, axis=1), jnp.concatenate(fields, axis=1)).T

    lots = 4

    def step(i, _):
        totals = [group(lots * i + lot) for lot in range(lots)]
        for lot, total in enumerate(totals):
            for turn in range(TURNS):
                out[TURNS * (lots * i + lot) + turn] = total[16 * turn:16 * turn + 16]
        return 0
    lax.fori_loop(0, half // TURNS // lots, step, 0)


def self_sums(side, rank, source, target, own):
    half = own.shape[1]
    return pl.pallas_call(
        functools.partial(self_kernel, side),
        out_shape=jax.ShapeDtypeStruct((half, 16, BLOCK), F32),
        in_specs=[SMEM] + [VMEM] * 3,
        out_specs=VMEM,
        compiler_params=params(16),
        cost_estimate=cost(3 * 10 ** 9, 10 ** 7),
    )(rank, source, target, own.reshape(-1, BLOCK))


def each_group(lists, order, bounds, target, source, table, use):
    first = jnp.int32(0)
    for part, count in enumerate(SIZES):
        def group(at):
            chosen = [order[TURNS * at + turn] for turn in range(TURNS)]
            slots = [[lists[k, b] for k in range(count)] for b in chosen]
            high, low = weights(target[at], [[source[s] for s in some] for some in slots])
            parts = []
            for turn, some in enumerate(slots):
                at = slice(turn * count * BLOCK, (turn + 1) * count * BLOCK)
                parts.append(summed(
                    jnp.concatenate([high[:, at], low[:, at]], axis=1),
                    jnp.concatenate([table[s] for s in some] * 2, axis=1),
                ))
            sums = turned(parts)
            return [(b, sums[16 * turn:16 * turn + 16]) for turn, b in enumerate(chosen)]

        shift = 0 if count > 4 else 1

        def step(i, base):
            found = []
            for lot in range(1 << shift):
                found += group(jnp.minimum(base + (i << shift) + lot, target.shape[0] - 1))
            for b, sums in found:
                use(b, sums)
            return base
        steps = jnp.maximum((bounds[part] - first + (1 << shift) - 1) >> shift, 0)
        lax.fori_loop(0, steps, step, first)
        first = first + (steps << shift)


def near_kernel(rank, lists, order, bounds, target, source, early, full, first_half, second_half, out, start, table, sem):
    half = first_half.shape[0]
    blocks = source.shape[0] - 1
    moved = pltpu.make_async_copy(early, table, sem)
    moved.start()

    def copy(i, _):
        for base, part in ((0, first_half), (half, second_half)):
            x = part[i]
            out[base + i] = x
            start[base + i] = x
        return 0
    lax.fori_loop(0, half, copy, 0, unroll=8)
    moved.wait()
    base = lax.rem(rank[0] + 2, 4) * 2 * half

    def build(i, _):
        table[base + i] = field_rows(full[pl.ds(base + place(i), 8, stride=blocks), :])
        return 0
    lax.fori_loop(0, 2 * half, build, 0, unroll=8)

    def use(b, sums):
        out[b] = start[b] + sums
    each_group(lists, order, bounds, target, source, table, use)


def near_sums(rank, lists, order, bounds, target, source, early, full, first_half, second_half):
    return pl.pallas_call(
        near_kernel,
        out_shape=jax.ShapeDtypeStruct((order.shape[0], 16, BLOCK), F32),
        in_specs=[SMEM] * 4 + [VMEM] * 6,
        out_specs=VMEM,
        scratch_shapes=[
            pltpu.VMEM((order.shape[0], 16, BLOCK), F32),
            pltpu.VMEM(early.shape, BF),
            pltpu.SemaphoreType.DMA(()),
        ],
        compiler_params=params(16),
        cost_estimate=cost(8 * 10 ** 9, 10 ** 7),
    )(rank, lists, order, bounds, target, source, early, full, first_half, second_half)


def far_kernel(core, lists, order, bounds, target, start, *rest):
    parts = rest[:-3]
    out, source, table = rest[-3:]
    side = core[0]
    cap = parts[-1].shape[0] * 2 // 3
    groups = (3, 2, 4 + side, 1 - side, 5 - 4 * side, 4 * side)
    for part, group in zip(parts, groups):
        base = group * cap

        def coords(i, _):
            x = part[cap + i]
            turned = pltpu.roll(x, 4, 0)
            row = rows(x.shape)
            source[base + 2 * i] = source_rows(jnp.where(row < 4, x, turned))
            source[base + 2 * i + 1] = source_rows(jnp.where(row < 4, turned, x))
            return 0
        lax.fori_loop(0, cap // 2, coords, 0, unroll=4)

        def fields(i, _):
            table[base + i] = field_rows(part[i])
            return 0
        lax.fori_loop(0, cap, fields, 0, unroll=8)
    none = len(parts) * cap
    source[none] = jnp.zeros((16, BLOCK), BF)
    table[none] = jnp.zeros((16, BLOCK), BF)

    def use(b, sums):
        total = sums + start[b]
        out[:, block(b)] = (total[0:7] + total[8:15]) / total[7:8]
    each_group(lists, order, bounds, target, source, table, use)


def far_sums(core, lists, order, bounds, target, start, parts):
    size = len(parts) * (parts[-1].shape[0] * 2 // 3) + 1
    return pl.pallas_call(
        far_kernel,
        out_shape=jax.ShapeDtypeStruct((7, order.shape[0] * BLOCK), F32),
        in_specs=[SMEM] * 4 + [VMEM] * (2 + len(parts)),
        out_specs=VMEM,
        scratch_shapes=[pltpu.VMEM((size, 16, BLOCK), BF)] * 2,
        compiler_params=params(16),
    )(core, lists, order, bounds, target, start, *parts)


def body(kernels, shots, coords, send_list, block_list, block_count):
    slices = lax.axis_size("cuts")
    ranges = lax.axis_size("event")
    events, nparams, points = kernels.shape
    blocks = points // BLOCK
    npeer, cap = send_list.shape[2:]
    targets = block_list.shape[1]
    rank = jnp.reshape(lax.axis_index("event"), (1,)).astype(jnp.int32)
    core = jnp.reshape(lax.axis_index("cuts") % 2, (1,)).astype(jnp.int32)
    send = send_list.reshape(npeer, cap)
    kernels = kernels.transpose(1, 0, 2).reshape(nparams, events, blocks, BLOCK)
    kernels = kernels.transpose(0, 2, 1, 3).reshape(nparams, blocks * events, BLOCK)
    kernels = held(kernels)

    power = local_power(kernels, slices)
    coords, power = lax.optimization_barrier((coords, power))
    power = lax.all_to_all(power, "cuts", 0, 0)
    source, near_coord, token = coord_tables(send, coords)
    slots = block_list[0].T[1:]
    live = jnp.arange(1, block_list.shape[2], dtype=jnp.int32)[:, None] < block_count
    near_work = work_order(slots, live & (slots < blocks), blocks, False)
    far_work = work_order(slots - blocks, live & (slots >= blocks), npeer * cap, True)
    npts = float(points * slices)
    across_a, across_b, ahead_b, behind_a = weighted(
        (((2, 0),), ((2, 1),), ((1, 1),), ((3, 0),)), rank, shots, power, kernels, token, npts, ranges
    )
    from_left = shifted(across_a, "event", 1)
    from_right = shifted(across_b, "event", -1)
    left_b = shifted(ahead_b, "event", 1)
    right_a = shifted(behind_a, "event", -1)
    mine_a, mine_b, ahead_a, behind_b = weighted(
        (((0, 0),), ((0, 1),), ((1, 0),), ((3, 1),)), rank, shots, power, kernels, token, npts, ranges
    )
    from_left, from_right, near_work, far_work = lax.optimization_barrier(
        (from_left, from_right, near_work, far_work)
    )
    aimed = aims(rank, near_work[1], far_work[1], coords)
    left_a = shifted(ahead_a + from_left, "event", 1)
    right_b = shifted(behind_b + from_right, "event", -1)
    left_a, right_b, left_b, right_a, aimed = lax.optimization_barrier(
        (left_a, right_b, left_b, right_a, aimed)
    )
    target, near_target, far_target = aimed
    own_a = mine_a + left_a + right_a
    own_b = mine_b + right_b + left_b

    own_a, own_b = lax.optimization_barrier((own_a, own_b))
    left_a = shifted(own_a, "event", 1)
    right_b = shifted(own_b, "event", -1)
    left_b = shifted(own_b, "event", 1)
    right_a = shifted(own_a, "event", -1)
    first_half = self_sums(0, rank, source, target, own_a)
    left_a, right_b, first_half = lax.optimization_barrier((left_a, right_b, first_half))
    far_a = shifted(left_a, "event", 1)
    far_b = shifted(right_b, "event", -1)
    second_half = self_sums(1, rank, source, target, own_b)

    early = early_table(rank, (own_a, own_b, right_a, right_b, left_a, left_b))
    down, up, far, near, full = gathered(
        rank, core, send, near_coord, early,
        (own_a, own_b, right_a, right_b, far_a, far_b, left_a, left_b),
    )
    lot = near.shape[0]
    down = shifted(down, "cuts", -2)
    up = shifted(up, "cuts", 2)
    far = swapped(far, "cuts", -3)
    start = near_sums(rank, *near_work, near_target, source, early, full, first_half, second_half)
    down, up, near, start = lax.optimization_barrier((down, up, near, start))
    near = swapped(near, "cuts", 1)
    parts = (
        down, up, far, near, swapped(down[lot:], "cuts", 1), swapped(up[lot:], "cuts", 1)
    )
    return far_sums(core, *far_work, far_target, start, parts)


def solution(mesh):
    placed = (
        P("event", None, "cuts"),
        P(),
        P(None, "cuts"),
        P("cuts", "event", None, None),
        P("cuts", "event", None),
        P("cuts", "event"),
    )
    return jax.shard_map(
        body, mesh=mesh, in_specs=placed, out_specs=P(None, ("cuts", "event")), check_vma=False
    )
```
